256 devices in a mesh: beam: 16 (over x, y), tensor: 16 (over z, core).
Axes of the slice: x: 4, y: 4, z: 8, core: 2. Of those that a mesh axis runs over, the one named last changes fastest.
Arguments:
- ssm_state: float32 [16, 8, 16, 16384], P('beam', None, None, 'tensor'), may hold values from -6 to 6
- conv_state: bfloat16 [16, 8, 3, 16384], P('beam', None, None, 'tensor'), may hold values from -6 to 6
- suffix_kv: bfloat16 [16, 8, 16, 4096], P('beam', None, None, 'tensor'), may hold values from -4 to 4
- mamba_x: bfloat16 [2, 16, 8, 16384], P(None, 'beam', None, 'tensor'), may hold values from -6 to 6
- mamba_gate: bfloat16 [2, 16, 8, 16384], P(None, 'beam', None, 'tensor'), may hold values from -6 to 6
- conv_weight: bfloat16 [4, 16384], P(None, 'tensor'), may hold values from -3 to 3
- conv_bias: bfloat16 [16384], P('tensor'), may hold values from -3 to 3
- xproj_weight: bfloat16 [16384, 288], P('tensor'), may hold values from -0.046875 to 0.046875
- dt_gain: float32 [256], replicated, may hold values from 0.25 to 1.75
- dtproj_weight: bfloat16 [256, 16384], P(None, 'tensor'), may hold values from -0.375 to 0.375
- dt_bias: float32 [16384], P('tensor'), may hold values from -3 to 1
- state_rates: float32 [16, 16384], P(None, 'tensor'), may hold values from 0.05 to 4
- skip_gain: float32 [16384], P('tensor'), may hold values from 0.5 to 1.5
- queries: bfloat16 [2, 16, 8, 8192], P(None, 'beam', None, 'tensor'), may hold values from -32 to 32
- new_kv: bfloat16 [2, 16, 8, 4096], P(None, 'beam', None, 'tensor'), may hold values from -4 to 4
- kv_pool: bfloat16 [4096, 16, 4096], P('beam', None, 'tensor'), may hold values from -4 to 4
- page_order: int32 [4096], replicated, may hold values from 0 to 4095, each once
- ctx_len: int32 [8], replicated, may hold values from 1 to 8192, 32768 in all
- parents: int32 [2, 16, 8, 1], replicated, may hold values from 0 to 15; in each aligned block of 8 rows (0 to 7, 8 to 15, ..., all dimensions but the last counted through in order) at most 2 rows name the same one
Outputs:
- mamba_out: bfloat16 [2, 16, 8, 16384], P(None, 'beam', None, 'tensor')
- attn_out: bfloat16 [2, 16, 8, 8192], P(None, 'beam', None, 'tensor')
The draws below stay inside these ranges and needn't reach their ends.
Inputs may be any that keep to these rules, and one draw needn't show every extreme that they name: parents[s, b, r, 0] is the beam whose state and own tokens beam b of request r continues at step s; for one step and one child beam b, no beam is the parent of more than 2 of the 8 requests, and some beam is the parent of exactly 2. `ctx_len`: the longest prefix has exactly 8192 tokens, and all sum to 32768. `page_order`: each pool page appears once.
All inputs are finite; a program needn't handle non-finite values.
Results may differ from the reference program's by a relative error of at most 0.019.
Values may be sent and summed in bfloat16 or wider, within the bound.
A program may use at most 128 MiB of HBM per device.

```python
import math
import jax
import jax.numpy as jnp
import numpy as np
from jax import lax

DI = 16384
DS = 16
DT_RANK = 256
DCONV = 4
HQ = 64
HD = 128
REQ = 8
STEPS = 2
PAGE = 16
MAXP = 512
SUF = 16
BEAMS = 16
CTX = 8192
POOL = 4096
CACHE_HEADS = 16
CAP = 2


def clipped(key, full_shape):
    return jnp.clip(jax.random.normal(key, full_shape, jnp.float32), -4.0, 4.0)


def cache_rows(key, leading):
    full_shape = tuple(leading) + (CACHE_HEADS, 2, HD)
    normal_noise = clipped(jax.random.fold_in(key, 1), full_shape)
    key_half = normal_noise[..., 0:1, :]
    cache_entries = jnp.concatenate([key_half, normal_noise[..., 1:2, :]], axis=-2)
    return cache_entries.reshape(tuple(leading) + (CACHE_HEADS * 2 * HD,)).astype(jnp.bfloat16)


def draw_kv_pool(key, part):
    key = jax.random.fold_in(key, 11)
    return cache_rows(key, (POOL, PAGE))


def draw_suffix_kv(key, part):
    key = jax.random.fold_in(key, 12)
    return cache_rows(key, (BEAMS, REQ, SUF))


def draw_new_kv(key, part):
    key = jax.random.fold_in(key, 13)
    return cache_rows(key, (STEPS, BEAMS, REQ))


def draw_queries(key, part):
    key = jax.random.fold_in(key, 14)
    normal_noise = clipped(jax.random.fold_in(key, 1), (STEPS, BEAMS, REQ, HQ, HD)) * 2.0
    return normal_noise.reshape(STEPS, BEAMS, REQ, HQ * HD).astype(jnp.bfloat16)


def shard_levels(stream_key, extent, shards, least, top_value):
    factor_of = 1.0
    for dim, shards_of in shards:
        heights = jax.random.uniform(jax.random.fold_in(jax.random.fold_in(stream_key, 6), dim), (shards_of,), jnp.float32, least / len(shards), top_value / len(shards))
        factor_of = factor_of * jnp.repeat(jnp.exp(heights), extent[dim] // shards_of).reshape((-1,) + (1,) * (len(extent) - 1 - dim))
    return factor_of


def split_up(number_of, total, most, skew):
    loads = [(1 << 20) // math.isqrt(standing ** skew) + 1 for standing in range(2, number_of + 1)]
    rest, holding = total - most - (number_of - 1), [1] * (number_of - 1)
    while rest > 0:
        movable = [i for i in range(number_of - 1) if holding[i] < most]
        pool, left = sum([loads[i] for i in movable]), rest
        for i in movable:
            addition = min(most - holding[i], max(1, left * loads[i] // pool), rest)
            holding[i] = holding[i] + addition
            rest = rest - addition
    return np.array([most] + holding)


def ragged_sizes(own_key, number_of, total, limit, slope):
    if number_of == 2:
        one = jax.random.randint(own_key, (), max(1, total - limit), min(limit, total - 1) + 1)
        return jnp.stack([one, total - one])
    tallies = jnp.asarray(split_up(number_of, total, limit, slope), jnp.int32)
    twos = (number_of - 1) // 2
    source_of, taker = tallies[1:1 + 2 * twos:2], tallies[2:2 + 2 * twos:2]
    margin = jnp.minimum(source_of - 1, limit - taker)
    shifted = jax.random.randint(jax.random.fold_in(own_key, 1), (twos,), 0, 1 << 20) % (margin + 1)
    tallies = tallies.at[1:1 + 2 * twos:2].set(source_of - shifted).at[2:2 + 2 * twos:2].set(taker + shifted)
    return tallies[jax.random.permutation(jax.random.fold_in(own_key, 2), number_of)]


def assign_block(stream_key, own, number, rows, count, top, most, lean):
    ranking = jax.random.permutation(stream_key, count)
    packed, ordinary = portions_of(count, rows * top, most, lean, True), portions_of(count, rows * top, most, lean, False)
    places = jnp.arange(count)

    def named(lengths, offset_by):
        used = int((lengths > 0).sum())
        fixed = max(1, used // 4)
        shifted = fixed + (places - fixed + offset_by * (used - fixed)) % max(1, count - fixed)
        return jnp.zeros((count,), jnp.int32).at[ranking[jnp.where(places < fixed, places, shifted)]].set(jnp.asarray(lengths, jnp.int32))

    lengths = jnp.where(number % 4 == 0, named(packed, number // 4), named(ordinary, number - number // 4 - 1))
    mixed = jax.random.permutation(jax.random.fold_in(own, 3), count)
    giver, receiver = mixed[0:count // 2 * 2:2], mixed[1:count // 2 * 2:2]
    margin = jnp.minimum(lengths[giver] - 1, most - lengths[receiver]) // 2
    margin = jnp.where((giver == ranking[0]) | (receiver == ranking[0]) | (lengths[receiver] == 0), 0, jnp.maximum(margin, 0))
    shifted = jax.random.randint(jax.random.fold_in(own, 4), (count // 2,), 0, 1 << 20) % (margin + 1)
    lengths = lengths.at[giver].add(-shifted).at[receiver].add(shifted)
    members = jnp.searchsorted(jnp.cumsum(lengths), jnp.arange(rows * top), side="right").astype(jnp.int32)
    table = members.reshape(top, rows).T
    table = table[jax.random.permutation(jax.random.fold_in(own, 1), rows)]
    offset_by = jax.random.randint(jax.random.fold_in(own, 2), (rows, 1), 0, top)
    return jnp.take_along_axis(table, (jnp.arange(top)[None, :] + offset_by) % top, axis=1)


def portions_of(count, total, limit, slope, full):
    portions = [(1 << 20) // math.isqrt(standing ** slope) + 1 for standing in range(1, count + 1)]
    largest = limit if full else min(limit, max(-(-total // count), total * portions[0] // sum(portions)))
    least = 1 if total - largest >= count - 1 else 0
    holding, spare = [largest] + [least] * (count - 1), total - largest - least * (count - 1)
    while spare > 0:
        movable = [i for i in range(1, count) if holding[i] < largest] or [i for i in range(1, count) if holding[i] < limit]
        mass, budget = sum([portions[i] for i in movable]), spare
        for i in movable:
            extra = min(limit - holding[i], max(1, budget * portions[i] // mass), spare)
            holding[i] = holding[i] + extra
            spare = spare - extra
    return np.array(holding)


def gaussian(key, dims, width, limit, cuts=(), kind=jnp.bfloat16):
    values = width * jax.random.normal(key, dims, jnp.float32)
    if cuts:
        values = values * shard_levels(key, dims, cuts, -0.22, 0.18)
    return jnp.clip(values, -limit, limit).astype(kind)


def setup_inputs(seed: int = 0) -> dict:
    key_of = jax.random.split(jax.random.key(seed), 20)
    ssm_state = gaussian(key_of[0], (BEAMS, REQ, DS, DI), 1.0, 6.0, ((0, 16), (3, 16)), jnp.float32)
    conv_state = gaussian(key_of[1], (BEAMS, REQ, DCONV - 1, DI), 1.0, 6.0, ((0, 16), (3, 16)))
    suffix_kv = draw_suffix_kv(jax.random.fold_in(key_of[19], 71), 0)
    mamba_x = gaussian(key_of[3], (STEPS, BEAMS, REQ, DI), 1.0, 6.0, ((1, 16), (3, 16)))
    mamba_gate = gaussian(key_of[4], (STEPS, BEAMS, REQ, DI), 1.0, 6.0, ((1, 16), (3, 16)))
    conv_weight = gaussian(key_of[5], (DCONV, DI), DCONV ** -0.5, 3.0, ((1, 16),))
    conv_bias = gaussian(key_of[6], (DI,), 0.5, 3.0, ((0, 16),))
    xproj_weight = gaussian(key_of[7], (DI, DT_RANK + 2 * DS), DI ** -0.5, 0.046875, ((0, 16),))
    dt_gain = jnp.clip(1.0 + 0.15 * jax.random.normal(key_of[8], (DT_RANK,), jnp.float32), 0.25, 1.75)
    dtproj_weight = gaussian(key_of[9], (DT_RANK, DI), DT_RANK ** -0.5, 0.375, ((1, 16),))
    dt_bias = jnp.clip(-3.0 + 4.0 * jax.random.uniform(key_of[10], (DI,), jnp.float32) ** shard_levels(key_of[10], (DI,), ((0, 16),), -0.2, 0.2), -3.0, 1.0)
    state_rates = jnp.clip(jnp.exp(math.log(4.0) - 4.3820266 * jax.random.uniform(key_of[11], (DS, DI), jnp.float32) ** shard_levels(key_of[11], (DS, DI), ((1, 16),), -0.2, 0.2)), 0.05, 4.0)
    skip_gain = jnp.clip(0.5 + 1.0 * jax.random.uniform(key_of[12], (DI,), jnp.float32) ** shard_levels(key_of[12], (DI,), ((0, 16),), -0.2, 0.2), 0.5, 1.5)
    queries = draw_queries(jax.random.fold_in(key_of[19], 71), 0)
    new_kv = draw_new_kv(jax.random.fold_in(key_of[19], 71), 0)
    kv_pool = draw_kv_pool(jax.random.fold_in(key_of[19], 71), 0)
    page_order = jax.random.permutation(key_of[16], POOL).astype(jnp.int32)
    ctx_len = ragged_sizes(key_of[17], REQ, REQ * CTX // 2, CTX, 2).astype(jnp.int32)
    parents_keys = jax.random.split(jax.random.fold_in(key_of[18], 1), STEPS * BEAMS * REQ // REQ)
    parents_turns = jax.random.permutation(jax.random.fold_in(key_of[18], 3), STEPS * BEAMS * REQ // REQ)
    parents = jax.vmap(lambda own, number: assign_block(jax.random.fold_in(key_of[18], 2), own, number, REQ, BEAMS, 1, CAP, 2))(parents_keys, parents_turns).reshape((STEPS, BEAMS, REQ, 1))
    return dict(ssm_state=ssm_state, conv_state=conv_state, suffix_kv=suffix_kv, mamba_x=mamba_x, mamba_gate=mamba_gate, conv_weight=conv_weight, conv_bias=conv_bias, xproj_weight=xproj_weight, dt_gain=dt_gain, dtproj_weight=dtproj_weight, dt_bias=dt_bias, state_rates=state_rates, skip_gain=skip_gain, queries=queries, new_kv=new_kv, kv_pool=kv_pool, page_order=page_order, ctx_len=ctx_len, parents=parents)


def attend(queries_now, suffix, kv_pool, page_table, ctx_len):
    score_scale = HD ** (-0.5)
    group = HQ // CACHE_HEADS

    def one_request(operands):
        query_req, suffix_req, pages_req, length_req = operands
        prefix_rows = kv_pool[pages_req].reshape(CTX, CACHE_HEADS, 2, HD).astype(jnp.float32)
        suffix_rows = suffix_req.reshape(BEAMS, -1, CACHE_HEADS, 2, HD).astype(jnp.float32)
        query_heads = query_req.reshape(BEAMS, CACHE_HEADS, group, HD).astype(jnp.float32)
        prefix_scores = jnp.einsum('bcgd,tcd->bcgt', query_heads, prefix_rows[:, :, 0]) * score_scale
        visible = jnp.arange(CTX, dtype=jnp.int32) < length_req
        prefix_scores = jnp.where(visible[None, None, None, :], prefix_scores, -jnp.inf)
        suffix_scores = jnp.einsum('bcgd,btcd->bcgt', query_heads, suffix_rows[:, :, :, 0]) * score_scale
        highest = jnp.maximum(lax.optimization_barrier(jnp.max(prefix_scores, axis=-1)), lax.optimization_barrier(jnp.max(suffix_scores, axis=-1)))
        prefix_exp = jnp.exp(prefix_scores - highest[..., None])
        suffix_exp = jnp.exp(suffix_scores - highest[..., None])
        normaliser = lax.optimization_barrier(jnp.sum(prefix_exp, axis=-1)) + lax.optimization_barrier(jnp.sum(suffix_exp, axis=-1))
        prefix_low = lax.optimization_barrier((prefix_exp / normaliser[..., None]).astype(jnp.bfloat16))
        suffix_low = lax.optimization_barrier((suffix_exp / normaliser[..., None]).astype(jnp.bfloat16))
        prefix_weights = prefix_low.astype(jnp.float32)
        suffix_weights = suffix_low.astype(jnp.float32)
        result = jnp.einsum('bcgt,tcd->bcgd', prefix_weights, prefix_rows[:, :, 1])
        result = result + jnp.einsum('bcgt,btcd->bcgd', suffix_weights, suffix_rows[:, :, :, 1])
        return result.reshape(BEAMS, HQ * HD).astype(jnp.bfloat16)
    per_request = lax.map(one_request, (jnp.swapaxes(queries_now, 0, 1), jnp.swapaxes(suffix, 0, 1), page_table, ctx_len))
    return jnp.swapaxes(per_request, 0, 1)

def reference(ssm_state, conv_state, suffix_kv, mamba_x, mamba_gate, conv_weight, conv_bias, xproj_weight, dt_gain, dtproj_weight, dt_bias, state_rates, skip_gain, queries, new_kv, kv_pool, page_order, ctx_len, parents):
    columns = jnp.arange(REQ, dtype=jnp.int32)[None, :]
    page_table = page_order.reshape(REQ, MAXP)
    ssm_now = ssm_state
    window = conv_state
    suffix = suffix_kv
    conv_kernel = conv_weight.astype(jnp.float32)
    conv_shift = conv_bias.astype(jnp.float32)
    mamba_steps = []
    attn_steps = []
    for decode_step in range(STEPS):
        parent_now = parents[decode_step, :, :, 0]
        carried = ssm_now[parent_now, columns]
        window_old = window[parent_now, columns]
        suffix_old = suffix[parent_now, columns]
        window_full = jnp.concatenate([window_old, mamba_x[decode_step][:, :, None, :]], axis=2)
        window = window_full[:, :, 1:]
        conv_out = jax.nn.silu(lax.optimization_barrier(jnp.sum(window_full.astype(jnp.float32) * conv_kernel[None, None], axis=2)) + conv_shift)
        conv_low = conv_out.astype(jnp.bfloat16).reshape(BEAMS * REQ, DI)
        projected = jnp.dot(conv_low, xproj_weight, preferred_element_type=jnp.float32).reshape(BEAMS, REQ, -1)
        rank_part = projected[..., :DT_RANK]
        input_map = projected[..., DT_RANK:DT_RANK + DS]
        output_map = projected[..., DT_RANK + DS:]
        rank_norm = rank_part * lax.rsqrt(lax.optimization_barrier(jnp.mean(rank_part * rank_part, axis=-1, keepdims=True)) + 1e-06) * dt_gain
        rank_norm = rank_norm.astype(jnp.bfloat16).reshape(BEAMS * REQ, DT_RANK)
        step_size = jax.nn.softplus(jnp.dot(rank_norm, dtproj_weight, preferred_element_type=jnp.float32).reshape(BEAMS, REQ, DI) + dt_bias)
        ssm_now = jnp.exp(-step_size[:, :, None, :] * state_rates[None, None]) * carried + (step_size * conv_out)[:, :, None, :] * input_map[..., None]
        mixture = lax.optimization_barrier(jnp.sum(output_map[..., None] * ssm_now, axis=2)) + skip_gain * conv_out
        mamba_steps.append((mixture * jax.nn.silu(mamba_gate[decode_step].astype(jnp.float32))).astype(jnp.bfloat16))
        suffix = jnp.concatenate([suffix_old, new_kv[decode_step][:, :, None, :]], axis=2)
        attn_steps.append(attend(queries[decode_step], suffix, kv_pool, page_table, ctx_len))
    return (jnp.stack(mamba_steps), jnp.stack(attn_steps))
```

```python
import jax
import jax.numpy as jnp
from jax import lax
from jax.experimental import pallas as pl
from jax.experimental.pallas import tpu as pltpu
from jax.sharding import PartitionSpec as P

NB = 16
REQ = 8
DS = 16
DT_RANK = 256
HD = 128
PAGE = 16
MAXP = 512
CH = 1024
LT = CH // 128
GROUP = 4
PAGES = 256
BLK = 16
NBLK = PAGES // BLK + REQ
UNROLL = 4
POOL = 4096
PROJ = DT_RANK + 2 * DS
PROJ_PAD = 384
LOG2E = 1.4426950408889634
NEG = -1e30

f32 = jnp.float32
bf16 = jnp.bfloat16
i32 = jnp.int32
MESH = pl.DeviceIdType.MESH


def iota(shape, dim):
    return lax.broadcasted_iota(i32, shape, dim)


def dot(a, b):
    return lax.dot_general(a, b, (((1,), (0,)), ((), ())), preferred_element_type=f32)


def dot_nt(a, b):
    return lax.dot_general(a, b, (((1,), (1,)), ((), ())), preferred_element_type=f32)


def one(mask):
    return jnp.where(mask, 1.0, 0.0).astype(bf16)


def onef(mask):
    return jnp.where(mask, 1.0, 0.0).astype(f32)


def to_rows(x):
    return jnp.concatenate([x[:, i * 128 : (i + 1) * 128] for i in range(LT)], axis=0)


def from_rows(x):
    return jnp.concatenate([x[i * REQ : (i + 1) * REQ] for i in range(LT)], axis=1)


def silu(v):
    return v / (1.0 + jnp.exp(-v))


def softplus(v):
    return jnp.maximum(v, 0.0) + jnp.log(1.0 + jnp.exp(-jnp.abs(v)))


def slot_key(par, me):
    chosen = par == me
    upper = one(iota((REQ, REQ), 0) < iota((REQ, REQ), 1))
    rank = dot(one(chosen), upper)
    return jnp.where(chosen, rank, -1.0)


def pack_matrix(key):
    rows, cols = NB * LT * 2, LT * REQ
    rb = one((iota((rows, NB), 0) >> 4) == iota((rows, NB), 1))
    cr = one((iota((REQ, cols), 1) & 7) == iota((REQ, cols), 0))
    spread = dot(dot(rb, key.astype(bf16)).astype(bf16), cr)
    row, col = iota((rows, cols), 0), iota((rows, cols), 1)
    return one((spread == (row & 1).astype(f32)) & (((row >> 1) & 7) == (col >> 3)))


def own_column(par, me):
    row = jnp.sum(jnp.where(iota((NB, REQ), 0) == me, par.astype(f32), 0.0), axis=0, keepdims=True)
    eye = iota((REQ, REQ), 0) == iota((REQ, REQ), 1)
    col = jnp.sum(jnp.where(eye, row, 0.0), axis=1, keepdims=True)
    return row, col


def unpack_matrix(par, me):
    row, col = own_column(par, me)
    alike = (row == col) & (iota((REQ, REQ), 1) < iota((REQ, REQ), 0))
    order = jnp.sum(onef(alike), axis=1, keepdims=True)
    code = jnp.concatenate([col * 2.0 + order] * LT, axis=0)
    rows, cols = LT * REQ, NB * LT * 2
    r, c = iota((rows, cols), 0), iota((rows, cols), 1)
    code_of = ((c >> 4) * 2 + (c & 1)).astype(f32)
    return one((code == code_of) & ((r >> 3) == ((c >> 1) & 7)))


def column128(m):
    spread = dot(one((iota((128, NB), 0) >> 3) == iota((128, NB), 1)), m.astype(bf16))
    pick = iota((128, REQ), 1) == (iota((128, REQ), 0) & 7)
    return jnp.sum(jnp.where(pick, spread, 0.0), axis=1, keepdims=True)


def kernel(
    par_h, po_h, ctx_h, cs_h, cw_h, cb_h, x_h, gate_h, q_h, nkv_h, suf_h, gain_h, dtb_h, rates_h, skip_h,
    s_h, xw_h, dtw_h, kv_h,
    mo_h, ao_h,
    par_ref, po_ref, ctx_ref, cs_ref, cw_ref, cb_ref, x_ref, gate_ref, q_ref, nkv_ref, suf_ref, gain_ref, dtb_ref,
    rates_ref, skip_ref, s_v, xw_v, dtw_v, kv_v,
    mo_ref, ao_ref,
    h1s, h1r, h2s, h2r, qa, zb, prb, zzs, zzr, os_, or_, lse,
    tab, tabs, bias, qr, orun, mrun, osf, s0, s1, rt, d1, d0g, c1, okm,
    lsem, tsem, ssem, rsem,
):
    me = lax.axis_index("beam")
    mt = lax.axis_index("tensor")
    nt = zb.shape[0]
    H1, H2, QA, ZB, PR, OO, LS, ZZ = range(8)

    def push(src, dst, to, k, axis):
        pltpu.make_async_remote_copy(
            src_ref=src, dst_ref=dst, send_sem=ssem.at[k], recv_sem=rsem.at[k], device_id={axis: to},
            device_id_type=MESH,
        ).start()

    def exchange(src, dst, k):
        for d in range(1, NB):
            peer = lax.rem(me + d, NB)
            push(src.at[peer], dst.at[me], peer, k, "beam")

    def gather(buf, k, n, my, axis):
        for d in range(1, n):
            push(buf.at[my], buf.at[my], lax.rem(my + d, n), k, axis)

    def all_of(buf, k, n, axis):
        part = buf.at[pl.ds(0, n - 1)]
        return pltpu.make_async_remote_copy(
            src_ref=part, dst_ref=part, send_sem=ssem.at[k], recv_sem=rsem.at[k], device_id={axis: 0},
            device_id_type=MESH,
        )

    def landed(buf, k, n=NB, axis="beam"):
        all_of(buf, k, n, axis).wait_recv()

    def sent(buf, k, n=NB, axis="beam"):
        all_of(buf, k, n, axis).wait_send()

    pairs = [
        (par_h, par_ref), (cs_h, cs_ref), (cw_h, cw_ref), (q_h, q_ref), (s_h, s_v), (rates_h, rates_ref),
        (x_h, x_ref), (cb_h, cb_ref), (po_h, po_ref), (ctx_h, ctx_ref), (xw_h, xw_v), (kv_h, kv_v),
        (suf_h, suf_ref), (nkv_h, nkv_ref), (dtw_h, dtw_v), (dtb_h, dtb_ref), (gain_h, gain_ref),
        (skip_h, skip_ref), (gate_h, gate_ref),
    ]
    copies = [pltpu.make_async_copy(a, b, lsem.at[i]) for i, (a, b) in enumerate(pairs)]
    (c_par, c_cs, c_cw, c_q, c_s, c_rates, c_x, c_cb, c_po, c_ctx, c_xw, c_kv, c_suf, c_nkv, c_dtw, c_dtb, c_gain,
     c_skip, c_gate) = copies
    for c in copies:
        c.start()
    barrier = pltpu.get_barrier_semaphore()
    for d in range(1, NB):
        pl.semaphore_signal(barrier, inc=1, device_id={"beam": lax.rem(me + d, NB)}, device_id_type=MESH)
    for d in range(1, nt):
        pl.semaphore_signal(barrier, inc=1, device_id={"tensor": lax.rem(mt + d, nt)}, device_id_type=MESH)

    c_par.wait()
    par_t = par_ref[...].astype(f32).astype(bf16)
    eye16 = one(iota((NB, NB), 0) == iota((NB, NB), 1))
    p0 = dot_nt(eye16, par_t[0:REQ]).astype(i32)
    p1 = dot_nt(eye16, par_t[REQ : 2 * REQ]).astype(i32)
    key0 = slot_key(p0, me)
    c_cs.wait()
    c_cw.wait()
    cw = cw_ref[...].astype(f32)
    cw_row = [cw[k : k + 1] for k in range(4)]
    win = [cs_ref[k].astype(f32) for k in range(3)]
    a0 = win[0] * cw_row[0] + win[1] * cw_row[1] + win[2] * cw_row[2]
    a1 = win[1] * cw_row[0] + win[2] * cw_row[1]
    both = jnp.concatenate([to_rows(a0), to_rows(a1)], axis=1).astype(bf16)
    packed = dot(pack_matrix(key0), both).astype(bf16)
    h1s[...] = packed.reshape(NB, 16, 256)
    h1r[pl.ds(me, 1)] = h1s[pl.ds(me, 1)]

    c_q.wait()
    qrows = jnp.concatenate(
        [q_ref[s][:, h * 128 : (h + 1) * 128].astype(f32) for s in range(2) for h in range(GROUP)], axis=0
    ).astype(bf16)
    ri, ci = iota((64, 64), 0), iota((64, 64), 1)
    swap = one(((ri >> 3) == (ci & 7)) & ((ri & 7) == (ci >> 3)))
    qa[pl.ds(me, 1)] = dot(swap, qrows).astype(bf16)[None]

    pl.semaphore_wait(barrier, NB - 1 + nt - 1)

    exchange(h1s, h1r, H1)

    key1 = slot_key(p1, me)
    pb1 = pack_matrix(key1)
    ub0 = unpack_matrix(p0, me)
    ub1 = unpack_matrix(p1, me)
    g = jnp.zeros((NB, REQ), i32)
    for p in range(NB):
        g = g + jnp.where(p1 == p, p0[p : p + 1, :], 0)
    wide = one((iota((REQ, REQ * 128), 1) >> 7) == iota((REQ, REQ * 128), 0))
    x_s0 = dot(one(p0 == me), wide)
    x_sg = dot(one(g == me), wide)
    x_s1 = dot(one(p1 == me), wide)
    tok = iota((NB, REQ * 128), 1) & 127
    mine = onef(iota((NB, REQ * 128), 0) == me)
    ok0 = jnp.where(tok < 16, x_s0, jnp.where(tok == 16, mine, 0.0))
    ok1 = jnp.where(tok < 16, x_sg, jnp.where(tok == 16, x_s1, jnp.where(tok == 17, mine, 0.0)))
    qi, qj = iota((128, 2 * NB), 0), iota((128, 2 * NB), 1)
    pick = one((((qi >> 2) & 1) == (qj >> 4)) & ((qi >> 3) == (qj & 15)))
    okm[...] = dot(pick, jnp.concatenate([ok0, ok1], axis=0).astype(bf16))

    c_rates.wait()
    for n in range(DS):
        rt[n] = jnp.broadcast_to(rates_ref[n : n + 1, :] * (-LOG2E), (REQ, CH))
    c_s.wait()
    row, col = iota((DS * NB * 2, 128), 0), iota((DS * NB * 2, 128), 1)
    rs_ = one(((iota((DS * NB * 2, NB), 0) >> 1) & 15) == iota((DS * NB * 2, NB), 1))
    crn = one((iota((REQ, 128), 1) >> 4) == iota((REQ, 128), 0))
    keys = dot(rs_, dot(key0.astype(bf16), crn).astype(bf16))
    sel0 = one((keys == (row & 1).astype(f32)) & ((row >> 5) == (col & 15)))
    pi, pj = iota((128, 128), 0), iota((128, 128), 1)
    perm1 = one(((pi & 7) == (pj >> 4)) & ((pi >> 3) == (pj & 15)))
    for j in range(4):
        sl = slice(j * 256, (j + 1) * 256)
        sj = s_v[:, sl].astype(bf16)
        s0[:, :, sl] = dot(sel0, sj).reshape(DS, NB * 2, 256)
        s1[:, :, sl] = dot(perm1, sj).reshape(DS, REQ, 256)

    c_x.wait()
    c_cb.wait()
    x0 = x_ref[0].astype(f32)
    x1 = x_ref[1].astype(f32)
    cb8 = cb_ref[...].astype(f32)
    cb = jnp.concatenate([cb8[i : i + 1] for i in range(LT)], axis=1)

    landed(h1r, H1)
    got = dot(ub0, h1r[...].reshape(NB * 16, 256))
    c0 = from_rows(got[:, 0:128]) + cw_row[3] * x0 + cb
    w1 = from_rows(got[:, 128:256]) + cw_row[2] * x0
    both = jnp.concatenate([to_rows(c0), to_rows(w1)], axis=1).astype(bf16)
    h2s[...] = dot(pb1, both).astype(bf16).reshape(NB, 16, 256)
    h2r[pl.ds(me, 1)] = h2s[pl.ds(me, 1)]
    exchange(h2s, h2r, H2)
    gather(qa, QA, NB, me, "beam")

    c_po.wait()
    c_ctx.wait()
    ctx_col = jnp.zeros((REQ, MAXP), i32)
    for r in range(REQ):
        ctx_col = jnp.where(iota((REQ, MAXP), 0) == r, ctx_ref[r], ctx_col)
    nvis = jnp.clip(ctx_col - iota((REQ, MAXP), 1) * PAGE, 0, PAGE)
    po = jnp.concatenate([po_ref[pl.ds(j, REQ, stride=4), :] for j in range(4)], axis=1)
    loc = po - me * PAGES
    flag = (loc >= 0) & (loc < PAGES) & (nvis > 0)
    tri = one(iota((MAXP, MAXP), 0) < iota((MAXP, MAXP), 1))
    rank = dot(one(flag), tri).astype(i32)
    count = jnp.sum(onef(flag), axis=1, keepdims=True).astype(i32)
    nblk = ((count + (BLK - 1)) >> 4).astype(f32)
    eye8 = iota((REQ, REQ), 0) == iota((REQ, REQ), 1)
    nblk_row = jnp.sum(jnp.where(eye8, nblk, 0.0), axis=0, keepdims=True)
    sblk = jnp.sum(
        jnp.where(iota((REQ, REQ), 1) < iota((REQ, REQ), 0), nblk_row, 0.0), axis=1, keepdims=True
    )
    dest = jnp.where(flag, sblk.astype(i32) * BLK + rank, -1)
    hi = dest >> 4
    lo = jnp.where(flag, dest & 15, -1)
    table = jnp.zeros((NBLK, 32), f32)
    for r in range(REQ):
        hot = one(hi[r : r + 1] == iota((NBLK, MAXP), 0))
        low = lo[r : r + 1] == iota((16, MAXP), 0)
        vals = jnp.concatenate(
            [
                jnp.where(low, loc[r : r + 1].astype(f32), 0.0),
                jnp.where(low, nvis[r : r + 1].astype(f32), 0.0),
            ],
            axis=0,
        ).astype(bf16)
        table = table + dot_nt(hot, vals)
    tab[...] = jnp.zeros_like(tab)
    tab[0:NBLK, 0:32] = table.astype(i32)
    lane = iota((REQ, 128), 1)
    subl = iota((REQ, 128), 0)
    sb_i, nb_i = sblk.astype(i32), nblk.astype(i32)
    inside = (sb_i <= lane) & (lane < sb_i + nb_i)
    tab[NBLK : NBLK + 1, :] = jnp.sum(jnp.where(inside, subl, 0).astype(f32), axis=0, keepdims=True).astype(i32)
    tab[NBLK + 1 : NBLK + 2, :] = jnp.sum(
        onef((lane == sb_i) & (nb_i > 0)), axis=0, keepdims=True
    ).astype(i32)
    tab[NBLK + 2 : NBLK + 3, :] = jnp.sum(
        jnp.where((lane == subl) & (nb_i > 0), sb_i + nb_i, 0).astype(f32), axis=0, keepdims=True
    ).astype(i32)
    cp_tab = pltpu.make_async_copy(tab, tabs, tsem)
    cp_tab.start()
    spread = one((iota((16, BLK * PAGE), 1) >> 4) == iota((16, BLK * PAGE), 0))
    seen = dot(table[:, 16:32].astype(bf16), spread)
    bias[...] = jnp.where((iota((NBLK, BLK * PAGE), 1) & 15).astype(f32) < seen, 0.0, NEG)
    orun[0] = jnp.zeros((128, 2 * HD), f32)
    mrun[0] = jnp.full((128, HD), NEG, f32)
    cp_tab.wait()

    c_xw.wait()
    landed(h2r, H2)
    got = dot(ub1, h2r[...].reshape(NB * 16, 256))
    conv0p = silu(from_rows(got[:, 0:128]))
    conv0 = silu(c0)
    conv1 = silu(from_rows(got[:, 128:256]) + cw_row[3] * x1 + cb)
    part = dot_nt(jnp.concatenate([conv0, conv1], axis=0).astype(bf16), xw_v[...])
    zb[pl.ds(mt, 1)] = jnp.zeros((1, 16, PROJ_PAD), bf16)
    zb[pl.ds(mt, 1), :, 0:PROJ] = part.astype(bf16)[None]
    gather(zb, ZB, nt, mt, "tensor")

    landed(qa, QA)
    qf = qa[...].astype(f32)
    for r in range(REQ):
        qr[r] = jnp.concatenate([qf[b, r * 8 : (r + 1) * 8] for b in range(NB)], axis=0).astype(bf16)
    c_kv.wait()
    scale = HD**-0.5 * LOG2E
    ones_blk = jnp.ones((BLK * PAGE, HD), bf16)

    def blocks(step, c):
        first = step * UNROLL
        m_old, o_old = mrun[first], orun[first]
        for u in range(UNROLL):
            i = first + u
            kv = jnp.concatenate([kv_v[tabs[i, k] & (PAGES - 1)] for k in range(BLK)], axis=0)
            s = dot_nt(qr[tabs[NBLK, i] & (REQ - 1)], kv[:, 0:HD]) * scale + bias[pl.ds(i, 1), :]
            m_old = jnp.where(tabs[NBLK + 1, i] > 0, NEG, m_old)
            m_new = jnp.maximum(m_old, jnp.max(s, axis=1, keepdims=True))
            e = jnp.exp2(s - jnp.concatenate([m_new, m_new], axis=1)).astype(bf16)
            v = jnp.concatenate([kv[:, HD : 2 * HD], ones_blk], axis=1)
            fade = jnp.exp2(m_old - m_new)
            o_old = o_old * jnp.concatenate([fade, fade], axis=1) + dot(e, v)
            m_old = m_new
            orun[i + 1] = o_old
            mrun[i + 1] = m_old
        return c

    steps = NBLK // UNROLL
    lax.fori_loop(0, steps // 2, blocks, 0)

    landed(zb, ZB, nt, "tensor")
    proj = jnp.zeros((16, PROJ_PAD), f32)
    for t in range(nt):
        proj = proj + zb[t].astype(f32)
    prb[pl.ds(me, 1)] = proj.astype(bf16)[None]
    gather(prb, PR, NB, me, "beam")

    lax.fori_loop(steps // 2, steps, blocks, 0)
    c_suf.wait()
    c_nkv.wait()
    nk0 = nkv_ref[0].astype(f32)
    nk1 = nkv_ref[1].astype(f32)
    diag = iota((128, 128), 0) == iota((128, 128), 1)
    ti = iota((16, 256), 0)
    for r in range(REQ):
        tail = jnp.where(ti == 0, nk0[r : r + 1], jnp.where(ti == 1, nk1[r : r + 1], 0.0)).astype(bf16)
        kv = jnp.concatenate([suf_ref[r], tail], axis=0)
        s = jnp.where(
            okm[:, r * 128 : r * 128 + 32] > 0.5, dot_nt(qr[r], kv[:, 0:HD]) * scale, NEG
        )
        last = jnp.clip(tabs[NBLK + 2, r], 0, NBLK)
        m_old = mrun[last]
        m_new = jnp.maximum(m_old, jnp.max(s, axis=1, keepdims=True))
        e = jnp.exp2(s - m_new[:, 0:32]).astype(bf16)
        v = jnp.concatenate([kv[:, HD : 2 * HD], jnp.ones((32, HD), bf16)], axis=1)
        fade = jnp.exp2(m_old - m_new)
        o = orun[last] * jnp.concatenate([fade, fade], axis=1) + dot(e, v)
        total = o[:, HD : 2 * HD]
        val = o[:, 0:HD] / total
        for b in range(NB):
            osf[b, r * 8 : (r + 1) * 8, :] = val[b * 8 : (b + 1) * 8]
        lg = m_new + jnp.log2(total)
        lse[pl.ds(me, 1), r : r + 1, :] = jnp.sum(jnp.where(diag, lg, 0.0), axis=0, keepdims=True)[None]
    os_[...] = osf[...].astype(bf16)
    or_[pl.ds(me, 1)] = os_[pl.ds(me, 1)]
    exchange(os_, or_, OO)
    gather(lse, LS, NB, me, "beam")

    for c in (c_dtw, c_dtb, c_gain, c_skip, c_gate):
        c.wait()
    gain = gain_ref[...]

    def normed(rank_rows):
        mean = jnp.sum(rank_rows * rank_rows, axis=1, keepdims=True) * (1.0 / DT_RANK)
        return (rank_rows * lax.rsqrt(mean + 1e-6) * gain).astype(bf16)

    dtb = dtb_ref[...]
    own = proj.astype(bf16).astype(f32)
    d_own = softplus(dot(normed(own[:, 0:DT_RANK]), dtw_v[...]) + dtb)
    d_own0, d_own1 = d_own[0:REQ], d_own[REQ : 2 * REQ]
    own_in = own[:, DT_RANK : DT_RANK + DS]
    own_out = own[:, DT_RANK + DS : DT_RANK + 2 * DS]
    cb_own = jnp.sum(own_in * own_out, axis=1, keepdims=True)
    skip = skip_ref[...]
    base0 = d_own0 * conv0 * cb_own[0:REQ] + skip * conv0
    base1 = d_own1 * conv1 * cb_own[REQ : 2 * REQ] + skip * conv1
    gate0 = silu(gate_ref[0].astype(f32))
    gate1 = silu(gate_ref[1].astype(f32))

    landed(prb, PR)
    prf = prb[...].astype(f32)
    pr0 = prf[:, 0:REQ, :].reshape(128, PROJ_PAD)
    pr1 = prf[:, REQ : 2 * REQ, :].reshape(128, PROJ_PAD)
    rn0 = normed(pr0[:, 0:DT_RANK])
    rn1 = normed(pr1[:, 0:DT_RANK])
    bc0 = pr0[:, DT_RANK:PROJ].astype(bf16)
    c1[...] = (pr1[:, DT_RANK:PROJ_PAD] * column128(onef(g == me))).reshape(NB, REQ, 128)
    g1 = one((column128(p1) == (pj >> 3).astype(f32)) & ((pi & 7) == (pj & 7)))
    rn0g = dot(g1, rn0).astype(bf16)

    r32 = one((iota((32, NB), 0) >> 1) == iota((32, NB), 1))
    c32 = one((iota((REQ, 128), 1) & 7) == iota((REQ, 128), 0))
    key32 = dot(dot(r32, key0.astype(bf16)).astype(bf16), c32)
    si, sj_ = iota((32, 128), 0), iota((32, 128), 1)
    psl = one((key32 == (si & 1).astype(f32)) & ((si >> 1) == (sj_ >> 3)))
    rn0s = dot(psl, rn0).astype(bf16)
    c0s = dot(psl, bc0)
    c0b = [jnp.broadcast_to(c0s[:, DS + n : DS + n + 1], (NB * 2, 128)) for n in range(DS)]
    z0 = []
    for j in range(4):
        sl = slice(j * 256, (j + 1) * 256)
        w = dtw_v[:, sl]
        part1 = softplus(dot(rn1, w) + dtb[:, sl])
        part0 = softplus(dot(rn0g, w) + dtb[:, sl])
        d0g[:, :, sl] = part0.reshape(NB, REQ, 256)
        d1[:, :, sl] = (part0 + part1).reshape(NB, REQ, 256)
        dj = softplus(dot(rn0s, w) + dtb[:, sl])
        acc = jnp.zeros((32, 256), f32)
        for n in range(DS):
            cn = jnp.concatenate([c0b[n], c0b[n]], axis=1)
            acc = acc + cn * (jnp.exp2(dj * (rates_ref[n : n + 1, sl] * (-LOG2E))) * s0[n, :, sl])
        z0 += [acc[:, 0:128], acc[:, 128:256]]
    z0 = jnp.concatenate(z0, axis=0).astype(bf16)
    ui, uj = iota((256, 256), 0), iota((256, 256), 1)
    relay = one(((ui >> 4) == ((uj >> 1) & 15)) & (((ui >> 1) & 7) == (uj >> 5)) & ((ui & 1) == (uj & 1)))
    zzs[:, 64:80, :] = dot(relay, z0).astype(bf16).reshape(NB, 16, 128)

    def children(i, c):
        two = [lax.rem(me + 1 + 2 * i, NB), lax.rem(me + 2 + 2 * i, NB)]
        outs = [c1[b] for b in two]
        deltas = [d1[b] for b in two]
        accs = [jnp.zeros((REQ, CH), f32) for _ in two]
        for n in range(DS):
            rn, sn = rt[n], s1[n]
            for k in range(2):
                accs[k] = accs[k] + outs[k][:, DS + n : DS + n + 1] * (jnp.exp2(deltas[k] * rn) * sn)
        for k in range(2):
            zzs[two[k], 0:64, :] = to_rows(accs[k]).astype(bf16)
        push(zzs.at[two[0]], zzr.at[me], two[0], ZZ, "beam")

        @pl.when(i < NB // 2 - 1)
        def _():
            push(zzs.at[two[1]], zzr.at[me], two[1], ZZ, "beam")

        return c

    lax.fori_loop(0, NB // 2, children, 0)
    zzr[pl.ds(me, 1)] = zzs[pl.ds(me, 1)]

    _, own1 = own_column(p1, me)
    gi, gj = iota((REQ, 128), 0), iota((REQ, 128), 1)
    og = one((own1 == (gj >> 3).astype(f32)) & (gi == (gj & 7)))
    in0p = dot(og, bc0)[:, 0:DS]
    cross = in0p * own_out[REQ : 2 * REQ]
    mixed = jnp.zeros((REQ, CH), f32)
    for n in range(DS):
        mixed = mixed + cross[:, n : n + 1] * jnp.exp2(d_own1 * rt[n])
    base1 = base1 + mixed * (d0g[pl.ds(me, 1)][0] * conv0p)

    landed(or_, OO)
    landed(lse, LS)
    lanes = iota((8, 128), 1)
    want = lanes == me * 8 + iota((8, 128), 0)
    parts = []
    for p in range(NB):
        lp = lse[p]
        parts.append(
            jnp.concatenate(
                [
                    jnp.sum(jnp.where(want, lp[r : r + 1], 0.0), axis=1, keepdims=True)
                    for r in range(REQ)
                ],
                axis=0,
            )
        )
    top = parts[0]
    for p in range(1, NB):
        top = jnp.maximum(top, parts[p])
    den = jnp.zeros((64, 1), f32)
    num = jnp.zeros((64, HD), f32)
    for p in range(NB):
        w = jnp.exp2(parts[p] - top)
        den = den + w
        num = num + w * or_[p].astype(f32)
    att = dot(swap, (num / den).astype(bf16))
    for s in range(2):
        ao_ref[s, 0] = jnp.concatenate(
            [att[(s * GROUP + h) * 8 : (s * GROUP + h + 1) * 8] for h in range(GROUP)], axis=1
        ).astype(bf16)
    out_a = pltpu.make_async_copy(ao_ref, ao_h, tsem)
    out_a.start()

    landed(zzr, ZZ)
    z1 = jnp.zeros((64, 128), f32)
    for p in range(NB):
        z1 = z1 + zzr[p, 0:64, :].astype(f32)
    z0 = dot(ub0, zzr[:, 64:80, :].reshape(256, 128))
    mo_ref[0, 0] = ((from_rows(z0) + base0) * gate0).astype(bf16)
    mo_ref[1, 0] = ((from_rows(z1) + base1) * gate1).astype(bf16)
    out_m = pltpu.make_async_copy(mo_ref, mo_h, lsem.at[0])
    out_m.start()

    sent(h1s, H1)
    sent(h2s, H2)
    sent(qa, QA)
    sent(zb, ZB, nt, "tensor")
    sent(prb, PR)
    sent(os_, OO)
    sent(lse, LS)
    sent(zzs, ZZ)
    out_a.wait()
    out_m.wait()


def local(
    ssm_state,
    conv_state,
    suffix_kv,
    mamba_x,
    mamba_gate,
    conv_weight,
    conv_bias,
    xproj_weight,
    dt_gain,
    dtproj_weight,
    dt_bias,
    state_rates,
    skip_gain,
    queries,
    new_kv,
    kv_pool,
    page_order,
    ctx_len,
    parents,
):
    nt = lax.axis_size("tensor")
    hb = pl.BlockSpec(memory_space=pltpu.HBM)
    dma = pltpu.SemaphoreType.DMA
    V = pltpu.VMEM
    operands = [
        parents.transpose(0, 2, 1, 3).reshape(2 * REQ, NB),
        page_order.reshape(POOL // 128, 128),
        ctx_len,
        conv_state.transpose(0, 2, 1, 3)[0],
        conv_weight,
        conv_bias.reshape(LT, 128),
        mamba_x[:, 0],
        mamba_gate[:, 0],
        queries[:, 0],
        new_kv[:, 0],
        suffix_kv[0],
        dt_gain.reshape(1, DT_RANK),
        dt_bias.reshape(1, CH),
        state_rates,
        skip_gain.reshape(1, CH),
        ssm_state.reshape(REQ * DS, CH),
        xproj_weight.T,
        dtproj_weight,
        kv_pool,
    ]
    held = [V(a.shape, a.dtype) for a in operands]
    held[2] = pltpu.SMEM((REQ,), i32)
    outs = (
        jax.ShapeDtypeStruct((2, 1, REQ, CH), bf16),
        jax.ShapeDtypeStruct((2, 1, REQ, GROUP * HD), bf16),
    )
    return pl.pallas_call(
        kernel,
        out_shape=outs,
        in_specs=[hb] * len(operands),
        out_specs=(hb, hb),
        scratch_shapes=held
        + [
            V(outs[0].shape, bf16),
            V(outs[1].shape, bf16),
            V((NB, 16, 256), bf16),
            V((NB, 16, 256), bf16),
            V((NB, 16, 256), bf16),
            V((NB, 16, 256), bf16),
            V((NB, 64, HD), bf16),
            V((nt, 16, PROJ_PAD), bf16),
            V((NB, 16, PROJ_PAD), bf16),
            V((NB, 80, 128), bf16),
            V((NB, 80, 128), bf16),
            V((NB, 64, HD), bf16),
            V((NB, 64, HD), bf16),
            V((NB, REQ, 128), f32),
            V((32, 128), i32),
            pltpu.SMEM((32, 128), i32),
            V((NBLK, BLK * PAGE), f32),
            V((REQ, 128, HD), bf16),
            V((NBLK + 1, 128, 2 * HD), f32),
            V((NBLK + 1, 128, HD), f32),
            V((NB, 64, HD), f32),
            V((DS, NB * 2, CH), f32),
            V((DS, REQ, CH), f32),
            V((DS, REQ, CH), f32),
            V((NB, REQ, CH), f32),
            V((NB, REQ, CH), f32),
            V((NB, REQ, 128), f32),
            V((128, REQ * 128), f32),
            dma((len(operands),)),
            dma,
            dma((8,)),
            dma((8,)),
        ],
        compiler_params=pltpu.CompilerParams(
            collective_id=0, has_side_effects=True, vmem_limit_bytes=63 * 2**20
        ),
        name="decode",
    )(*operands)


def solution(mesh):
    in_specs = (
        P("beam", None, None, "tensor"),
        P("beam", None, None, "tensor"),
        P("beam", None, None, "tensor"),
        P(None, "beam", None, "tensor"),
        P(None, "beam", None, "tensor"),
        P(None, "tensor"),
        P("tensor"),
        P("tensor", None),
        P(),
        P(None, "tensor"),
        P("tensor"),
        P(None, "tensor"),
        P("tensor"),
        P(None, "beam", None, "tensor"),
        P(None, "beam", None, "tensor"),
        P("beam", None, "tensor"),
        P(),
        P(),
        P(),
    )
    out_specs = (P(None, "beam", None, "tensor"), P(None, "beam", None, "tensor"))
    return jax.shard_map(local, mesh=mesh, in_specs=in_specs, out_specs=out_specs, check_vma=False)
```

```python
import jax
import jax.numpy as jnp
from jax import lax
from jax.experimental import pallas as pl
from jax.experimental.pallas import tpu as pltpu
from jax.sharding import PartitionSpec as P

NB = 16
REQ = 8
DS = 16
DT_RANK = 256
HD = 128
PAGE = 16
MAXP = 512
CH = 1024
LT = CH // 128
GROUP = 4
PAGES = 256
BLK = 16
NBLK = PAGES // BLK + REQ
UNROLL = 8
POOL = 4096
PROJ = DT_RANK + 2 * DS
PROJ_PAD = 384
LOG2E = 1.4426950408889634
NEG = -1e30

f32 = jnp.float32
bf16 = jnp.bfloat16
i32 = jnp.int32
MESH = pl.DeviceIdType.MESH


def iota(shape, dim):
    return lax.broadcasted_iota(i32, shape, dim)


def dot(a, b):
    return lax.dot_general(a, b, (((1,), (0,)), ((), ())), preferred_element_type=f32)


def dot_nt(a, b):
    return lax.dot_general(a, b, (((1,), (1,)), ((), ())), preferred_element_type=f32)


def one(mask):
    return jnp.where(mask, 1.0, 0.0).astype(bf16)


def onef(mask):
    return jnp.where(mask, 1.0, 0.0).astype(f32)


def to_rows(x):
    return jnp.concatenate([x[:, i * 128 : (i + 1) * 128] for i in range(LT)], axis=0)


def from_rows(x):
    return jnp.concatenate([x[i * REQ : (i + 1) * REQ] for i in range(LT)], axis=1)


def silu(v):
    return v / (1.0 + jnp.exp(-v))


def softplus(v):
    return jnp.maximum(v, 0.0) + jnp.log(1.0 + jnp.exp(-jnp.abs(v)))


def slot_key(par, me):
    chosen = par == me
    upper = one(iota((REQ, REQ), 0) < iota((REQ, REQ), 1))
    rank = dot(one(chosen), upper)
    return jnp.where(chosen, rank, -1.0)


def pack_matrix(key):
    rows, cols = NB * LT * 2, LT * REQ
    rb = one((iota((rows, NB), 0) >> 4) == iota((rows, NB), 1))
    cr = one((iota((REQ, cols), 1) & 7) == iota((REQ, cols), 0))
    spread = dot(dot(rb, key.astype(bf16)).astype(bf16), cr)
    row, col = iota((rows, cols), 0), iota((rows, cols), 1)
    return one((spread == (row & 1).astype(f32)) & (((row >> 1) & 7) == (col >> 3)))


def own_column(par, me):
    row = jnp.sum(jnp.where(iota((NB, REQ), 0) == me, par.astype(f32), 0.0), axis=0, keepdims=True)
    eye = iota((REQ, REQ), 0) == iota((REQ, REQ), 1)
    col = jnp.sum(jnp.where(eye, row, 0.0), axis=1, keepdims=True)
    return row, col


def unpack_matrix(par, me):
    row, col = own_column(par, me)
    alike = (row == col) & (iota((REQ, REQ), 1) < iota((REQ, REQ), 0))
    order = jnp.sum(onef(alike), axis=1, keepdims=True)
    code = jnp.concatenate([col * 2.0 + order] * LT, axis=0)
    rows, cols = LT * REQ, NB * LT * 2
    r, c = iota((rows, cols), 0), iota((rows, cols), 1)
    code_of = ((c >> 4) * 2 + (c & 1)).astype(f32)
    return one((code == code_of) & ((r >> 3) == ((c >> 1) & 7)))


def column128(m):
    spread = dot(one((iota((128, NB), 0) >> 3) == iota((128, NB), 1)), m.astype(bf16))
    pick = iota((128, REQ), 1) == (iota((128, REQ), 0) & 7)
    return jnp.sum(jnp.where(pick, spread, 0.0), axis=1, keepdims=True)


def kernel(
    par_h, po_h, ctx_h, cs_h, cw_h, cb_h, x_h, gate_h, q_h, nkv_h, suf_h, gain_h, dtb_h, rates_h, skip_h,
    s_h, xw_h, dtw_h, kv_h,
    mo_h, ao_h,
    par_ref, po_ref, ctx_ref, cs_ref, cw_ref, cb_ref, x_ref, gate_ref, q_ref, nkv_ref, suf_ref, gain_ref, dtb_ref,
    rates_ref, skip_ref, s_v, xw_v, dtw_v, kv_v,
    mo_ref, ao_ref,
    h1s, h1r, h2s, h2r, qa, zb, prb, zzs, zzr, os_, or_, lse,
    tab, tabs, bias, qr, orun, mrun, osf, s0, s1, rt, d1, d0g, c1, okm,
    lsem, tsem, ssem, rsem,
):
    me = lax.axis_index("beam")
    mt = lax.axis_index("tensor")
    nt = zb.shape[0]
    H1, H2, QA, ZB, PR, OO, LS, ZZ = range(8)

    def push(src, dst, to, k, axis):
        pltpu.make_async_remote_copy(
            src_ref=src, dst_ref=dst, send_sem=ssem.at[k], recv_sem=rsem.at[k], device_id={axis: to},
            device_id_type=MESH,
        ).start()

    def exchange(src, dst, k):
        for d in range(1, NB):
            peer = lax.rem(me + d, NB)
            push(src.at[peer], dst.at[me], peer, k, "beam")

    def gather(buf, k, n, my, axis):
        for d in range(1, n):
            push(buf.at[my], buf.at[my], lax.rem(my + d, n), k, axis)

    def all_of(buf, k, n, axis):
        part = buf.at[pl.ds(0, n - 1)]
        return pltpu.make_async_remote_copy(
            src_ref=part, dst_ref=part, send_sem=ssem.at[k], recv_sem=rsem.at[k], device_id={axis: 0},
            device_id_type=MESH,
        )

    def landed(buf, k, n=NB, axis="beam"):
        all_of(buf, k, n, axis).wait_recv()

    def sent(buf, k, n=NB, axis="beam"):
        all_of(buf, k, n, axis).wait_send()

    pairs = [
        (par_h, par_ref), (cs_h, cs_ref), (cw_h, cw_ref), (q_h, q_ref), (s_h, s_v), (rates_h, rates_ref),
        (x_h, x_ref), (cb_h, cb_ref), (po_h, po_ref), (ctx_h, ctx_ref), (xw_h, xw_v), (kv_h, kv_v),
        (suf_h, suf_ref), (nkv_h, nkv_ref), (dtw_h, dtw_v), (dtb_h, dtb_ref), (gain_h, gain_ref),
        (skip_h, skip_ref), (gate_h, gate_ref),
    ]
    copies = [pltpu.make_async_copy(a, b, lsem.at[i]) for i, (a, b) in enumerate(pairs)]
    (c_par, c_cs, c_cw, c_q, c_s, c_rates, c_x, c_cb, c_po, c_ctx, c_xw, c_kv, c_suf, c_nkv, c_dtw, c_dtb, c_gain,
     c_skip, c_gate) = copies
    for c in copies:
        c.start()
    barrier = pltpu.get_barrier_semaphore()
    for d in range(1, NB):
        pl.semaphore_signal(barrier, inc=1, device_id={"beam": lax.rem(me + d, NB)}, device_id_type=MESH)
    for d in range(1, nt):
        pl.semaphore_signal(barrier, inc=1, device_id={"tensor": lax.rem(mt + d, nt)}, device_id_type=MESH)

    c_par.wait()
    par_t = par_ref[...].astype(f32).astype(bf16)
    eye16 = one(iota((NB, NB), 0) == iota((NB, NB), 1))
    p0 = dot_nt(eye16, par_t[0:REQ]).astype(i32)
    p1 = dot_nt(eye16, par_t[REQ : 2 * REQ]).astype(i32)
    key0 = slot_key(p0, me)
    c_cs.wait()
    c_cw.wait()
    cw = cw_ref[...].astype(f32)
    cw_row = [cw[k : k + 1] for k in range(4)]
    win = [cs_ref[k].astype(f32) for k in range(3)]
    a0 = win[0] * cw_row[0] + win[1] * cw_row[1] + win[2] * cw_row[2]
    a1 = win[1] * cw_row[0] + win[2] * cw_row[1]
    both = jnp.concatenate([to_rows(a0), to_rows(a1)], axis=1).astype(bf16)
    packed = dot(pack_matrix(key0), both).astype(bf16)
    h1s[...] = packed.reshape(NB, 16, 256)
    h1r[pl.ds(me, 1)] = h1s[pl.ds(me, 1)]

    c_q.wait()
    qrows = jnp.concatenate(
        [q_ref[s][:, h * 128 : (h + 1) * 128].astype(f32) for s in range(2) for h in range(GROUP)], axis=0
    ).astype(bf16)
    ri, ci = iota((64, 64), 0), iota((64, 64), 1)
    swap = one(((ri >> 3) == (ci & 7)) & ((ri & 7) == (ci >> 3)))
    qa[pl.ds(me, 1)] = dot(swap, qrows).astype(bf16)[None]

    pl.semaphore_wait(barrier, NB - 1 + nt - 1)

    exchange(h1s, h1r, H1)
    gather(qa, QA, NB, me, "beam")

    key1 = slot_key(p1, me)
    pb1 = pack_matrix(key1)
    ub0 = unpack_matrix(p0, me)
    ub1 = unpack_matrix(p1, me)
    g = jnp.zeros((NB, REQ), i32)
    for p in range(NB):
        g = g + jnp.where(p1 == p, p0[p : p + 1, :], 0)
    c_po.wait()
    c_ctx.wait()
    ctx_col = jnp.zeros((REQ, MAXP), i32)
    for r in range(REQ):
        ctx_col = jnp.where(iota((REQ, MAXP), 0) == r, ctx_ref[r], ctx_col)
    nvis = jnp.clip(ctx_col - iota((REQ, MAXP), 1) * PAGE, 0, PAGE)
    po = jnp.concatenate([po_ref[pl.ds(j, REQ, stride=4), :] for j in range(4)], axis=1)
    loc = po - me * PAGES
    flag = (loc >= 0) & (loc < PAGES) & (nvis > 0)
    tri = one(iota((MAXP, MAXP), 0) < iota((MAXP, MAXP), 1))
    rank = dot(one(flag), tri).astype(i32)
    count = jnp.sum(onef(flag), axis=1, keepdims=True).astype(i32)
    nblk = ((count + (BLK - 1)) >> 4).astype(f32)
    eye8 = iota((REQ, REQ), 0) == iota((REQ, REQ), 1)
    nblk_row = jnp.sum(jnp.where(eye8, nblk, 0.0), axis=0, keepdims=True)
    sblk = jnp.sum(
        jnp.where(iota((REQ, REQ), 1) < iota((REQ, REQ), 0), nblk_row, 0.0), axis=1, keepdims=True
    )
    dest = jnp.where(flag, sblk.astype(i32) * BLK + rank, -1)
    hi = dest >> 4
    lo = jnp.where(flag, dest & 15, -1)
    table = jnp.zeros((NBLK, 32), f32)
    for r in range(REQ):
        hot = one(hi[r : r + 1] == iota((NBLK, MAXP), 0))
        low = lo[r : r + 1] == iota((16, MAXP), 0)
        vals = jnp.concatenate(
            [
                jnp.where(low, loc[r : r + 1].astype(f32), 0.0),
                jnp.where(low, nvis[r : r + 1].astype(f32), 0.0),
            ],
            axis=0,
        ).astype(bf16)
        table = table + dot_nt(hot, vals)
    tab[...] = jnp.zeros_like(tab)
    tab[0:NBLK, 0:32] = table.astype(i32)
    lane = iota((REQ, 128), 1)
    subl = iota((REQ, 128), 0)
    sb_i, nb_i = sblk.astype(i32), nblk.astype(i32)
    inside = (sb_i <= lane) & (lane < sb_i + nb_i)
    tab[NBLK : NBLK + 1, :] = jnp.sum(jnp.where(inside, subl, 0).astype(f32), axis=0, keepdims=True).astype(i32)
    tab[NBLK + 1 : NBLK + 2, :] = jnp.sum(
        onef((lane == sb_i) & (nb_i > 0)), axis=0, keepdims=True
    ).astype(i32)
    tab[NBLK + 2 : NBLK + 3, :] = jnp.sum(
        jnp.where((lane == subl) & (nb_i > 0), sb_i + nb_i, 0).astype(f32), axis=0, keepdims=True
    ).astype(i32)
    cp_tab = pltpu.make_async_copy(tab, tabs, tsem)
    cp_tab.start()
    spread = one((iota((16, BLK * PAGE), 1) >> 4) == iota((16, BLK * PAGE), 0))
    seen = dot(table[:, 16:32].astype(bf16), spread)
    bias[...] = jnp.where((iota((NBLK, BLK * PAGE), 1) & 15).astype(f32) < seen, 0.0, NEG)
    orun[0] = jnp.zeros((128, 2 * HD), f32)
    mrun[0] = jnp.full((128, HD), NEG, f32)
    cp_tab.wait()

    c_x.wait()
    c_cb.wait()
    x0 = x_ref[0].astype(f32)
    x1 = x_ref[1].astype(f32)
    cb8 = cb_ref[...].astype(f32)
    cb = jnp.concatenate([cb8[i : i + 1] for i in range(LT)], axis=1)

    landed(h1r, H1)
    got = dot(ub0, h1r[...].reshape(NB * 16, 256))
    c0 = from_rows(got[:, 0:128]) + cw_row[3] * x0 + cb
    w1 = from_rows(got[:, 128:256]) + cw_row[2] * x0
    both = jnp.concatenate([to_rows(c0), to_rows(w1)], axis=1).astype(bf16)
    h2s[...] = dot(pb1, both).astype(bf16).reshape(NB, 16, 256)
    h2r[pl.ds(me, 1)] = h2s[pl.ds(me, 1)]
    exchange(h2s, h2r, H2)

    landed(qa, QA)
    qf = qa[...].astype(f32)
    for r in range(REQ):
        qr[r] = jnp.concatenate([qf[b, r * 8 : (r + 1) * 8] for b in range(NB)], axis=0).astype(bf16)
    c_kv.wait()
    scale = HD**-0.5 * LOG2E
    ones_blk = jnp.ones((BLK * PAGE, HD), bf16)

    def blocks(step, c):
        first = step * UNROLL
        m_old, o_old = mrun[first], orun[first]
        for u in range(UNROLL):
            i = first + u
            kv = jnp.concatenate([kv_v[tabs[i, k] & (PAGES - 1)] for k in range(BLK)], axis=0)
            s = dot_nt(qr[tabs[NBLK, i] & (REQ - 1)], kv[:, 0:HD]) * scale + bias[pl.ds(i, 1), :]
            m_old = jnp.where(tabs[NBLK + 1, i] > 0, NEG, m_old)
            m_new = jnp.maximum(m_old, jnp.max(s, axis=1, keepdims=True))
            e = jnp.exp2(s - jnp.concatenate([m_new, m_new], axis=1)).astype(bf16)
            v = jnp.concatenate([kv[:, HD : 2 * HD], ones_blk], axis=1)
            fade = jnp.exp2(m_old - m_new)
            o_old = o_old * jnp.concatenate([fade, fade], axis=1) + dot(e, v)
            m_old = m_new
            orun[i + 1] = o_old
            mrun[i + 1] = m_old
        return c

    steps = NBLK // UNROLL
    lax.fori_loop(0, 1, blocks, 0)

    c_xw.wait()
    landed(h2r, H2)
    got = dot(ub1, h2r[...].reshape(NB * 16, 256))
    conv0p = silu(from_rows(got[:, 0:128]))
    conv0 = silu(c0)
    conv1 = silu(from_rows(got[:, 128:256]) + cw_row[3] * x1 + cb)
    part = dot_nt(jnp.concatenate([conv0, conv1], axis=0).astype(bf16), xw_v[...])
    zb[pl.ds(mt, 1)] = jnp.zeros((1, 16, PROJ_PAD), bf16)
    zb[pl.ds(mt, 1), :, 0:PROJ] = part.astype(bf16)[None]
    gather(zb, ZB, nt, mt, "tensor")


    wide = one((iota((REQ, REQ * 128), 1) >> 7) == iota((REQ, REQ * 128), 0))
    x_s0 = dot(one(p0 == me), wide)
    x_sg = dot(one(g == me), wide)
    x_s1 = dot(one(p1 == me), wide)
    tok = iota((NB, REQ * 128), 1) & 127
    mine = onef(iota((NB, REQ * 128), 0) == me)
    ok0 = jnp.where(tok < 16, x_s0, jnp.where(tok == 16, mine, 0.0))
    ok1 = jnp.where(tok < 16, x_sg, jnp.where(tok == 16, x_s1, jnp.where(tok == 17, mine, 0.0)))
    qi, qj = iota((128, 2 * NB), 0), iota((128, 2 * NB), 1)
    pick = one((((qi >> 2) & 1) == (qj >> 4)) & ((qi >> 3) == (qj & 15)))
    okm[...] = dot(pick, jnp.concatenate([ok0, ok1], axis=0).astype(bf16))

    c_rates.wait()
    for n in range(DS):
        rt[n] = jnp.broadcast_to(rates_ref[n : n + 1, :] * (-LOG2E), (REQ, CH))
    c_s.wait()
    row, col = iota((DS * NB * 2, 128), 0), iota((DS * NB * 2, 128), 1)
    rs_ = one(((iota((DS * NB * 2, NB), 0) >> 1) & 15) == iota((DS * NB * 2, NB), 1))
    crn = one((iota((REQ, 128), 1) >> 4) == iota((REQ, 128), 0))
    keys = dot(rs_, dot(key0.astype(bf16), crn).astype(bf16))
    sel0 = one((keys == (row & 1).astype(f32)) & ((row >> 5) == (col & 15)))
    pi, pj = iota((128, 128), 0), iota((128, 128), 1)
    perm1 = one(((pi & 7) == (pj >> 4)) & ((pi >> 3) == (pj & 15)))
    for j in range(4):
        sl = slice(j * 256, (j + 1) * 256)
        sj = s_v[:, sl].astype(bf16)
        s0[:, :, sl] = dot(sel0, sj).reshape(DS, NB * 2, 256)
        s1[:, :, sl] = dot(perm1, sj).reshape(DS, REQ, 256)

    lax.fori_loop(1, 2, blocks, 0)

    landed(zb, ZB, nt, "tensor")
    proj = jnp.zeros((16, PROJ_PAD), f32)
    for t in range(nt):
        proj = proj + zb[t].astype(f32)
    prb[pl.ds(me, 1)] = proj.astype(bf16)[None]
    gather(prb, PR, NB, me, "beam")

    lax.fori_loop(2, steps, blocks, 0)
    c_suf.wait()
    c_nkv.wait()
    nk0 = nkv_ref[0].astype(f32)
    nk1 = nkv_ref[1].astype(f32)
    diag = iota((128, 128), 0) == iota((128, 128), 1)
    ti = iota((16, 256), 0)
    for r in range(REQ):
        tail = jnp.where(ti == 0, nk0[r : r + 1], jnp.where(ti == 1, nk1[r : r + 1], 0.0)).astype(bf16)
        kv = jnp.concatenate([suf_ref[r], tail], axis=0)
        s = jnp.where(
            okm[:, r * 128 : r * 128 + 32] > 0.5, dot_nt(qr[r], kv[:, 0:HD]) * scale, NEG
        )
        last = jnp.clip(tabs[NBLK + 2, r], 0, NBLK)
        m_old = mrun[last]
        m_new = jnp.maximum(m_old, jnp.max(s, axis=1, keepdims=True))
        e = jnp.exp2(s - m_new[:, 0:32]).astype(bf16)
        v = jnp.concatenate([kv[:, HD : 2 * HD], jnp.ones((32, HD), bf16)], axis=1)
        fade = jnp.exp2(m_old - m_new)
        o = orun[last] * jnp.concatenate([fade, fade], axis=1) + dot(e, v)
        total = o[:, HD : 2 * HD]
        val = o[:, 0:HD] / total
        for b in range(NB):
            osf[b, r * 8 : (r + 1) * 8, :] = val[b * 8 : (b + 1) * 8]
        lg = m_new + jnp.log2(total)
        lse[pl.ds(me, 1), r : r + 1, :] = jnp.sum(jnp.where(diag, lg, 0.0), axis=0, keepdims=True)[None]
    os_[...] = osf[...].astype(bf16)
    or_[pl.ds(me, 1)] = os_[pl.ds(me, 1)]
    exchange(os_, or_, OO)
    gather(lse, LS, NB, me, "beam")

    for c in (c_dtw, c_dtb, c_gain, c_skip, c_gate):
        c.wait()
    gain = gain_ref[...]

    def normed(rank_rows):
        mean = jnp.sum(rank_rows * rank_rows, axis=1, keepdims=True) * (1.0 / DT_RANK)
        return (rank_rows * lax.rsqrt(mean + 1e-6) * gain).astype(bf16)

    dtb = dtb_ref[...]
    own = proj.astype(bf16).astype(f32)
    d_own = softplus(dot(normed(own[:, 0:DT_RANK]), dtw_v[...]) + dtb)
    d_own0, d_own1 = d_own[0:REQ], d_own[REQ : 2 * REQ]
    own_in = own[:, DT_RANK : DT_RANK + DS]
    own_out = own[:, DT_RANK + DS : DT_RANK + 2 * DS]
    cb_own = jnp.sum(own_in * own_out, axis=1, keepdims=True)
    skip = skip_ref[...]
    base0 = d_own0 * conv0 * cb_own[0:REQ] + skip * conv0
    base1 = d_own1 * conv1 * cb_own[REQ : 2 * REQ] + skip * conv1
    gate0 = silu(gate_ref[0].astype(f32))
    gate1 = silu(gate_ref[1].astype(f32))

    held_here = column128(onef(g == me))
    g1 = one((column128(p1) == (pj >> 3).astype(f32)) & ((pi & 7) == (pj & 7)))
    r32 = one((iota((32, NB), 0) >> 1) == iota((32, NB), 1))
    c32 = one((iota((REQ, 128), 1) & 7) == iota((REQ, 128), 0))
    key32 = dot(dot(r32, key0.astype(bf16)).astype(bf16), c32)
    si, sj_ = iota((32, 128), 0), iota((32, 128), 1)
    psl = one((key32 == (si & 1).astype(f32)) & ((si >> 1) == (sj_ >> 3)))
    ui, uj = iota((256, 256), 0), iota((256, 256), 1)
    relay = one(((ui >> 4) == ((uj >> 1) & 15)) & (((ui >> 1) & 7) == (uj >> 5)) & ((ui & 1) == (uj & 1)))
    _, own1 = own_column(p1, me)
    gi, gj = iota((REQ, 128), 0), iota((REQ, 128), 1)
    og = one((own1 == (gj >> 3).astype(f32)) & (gi == (gj & 7)))

    landed(prb, PR)
    prf = prb[...].astype(f32)
    pr0 = prf[:, 0:REQ, :].reshape(128, PROJ_PAD)
    pr1 = prf[:, REQ : 2 * REQ, :].reshape(128, PROJ_PAD)
    rn0 = normed(pr0[:, 0:DT_RANK])
    rn1 = normed(pr1[:, 0:DT_RANK])
    bc0 = pr0[:, DT_RANK:PROJ].astype(bf16)
    c1[...] = (pr1[:, DT_RANK:PROJ_PAD] * held_here).reshape(NB, REQ, 128)
    rn0g = dot(g1, rn0).astype(bf16)

    rn0s = dot(psl, rn0).astype(bf16)
    c0s = dot(psl, bc0)
    c0b = [jnp.broadcast_to(c0s[:, DS + n : DS + n + 1], (NB * 2, 128)) for n in range(DS)]
    z0 = []
    for j in range(4):
        sl = slice(j * 256, (j + 1) * 256)
        w = dtw_v[:, sl]
        part1 = softplus(dot(rn1, w) + dtb[:, sl])
        part0 = softplus(dot(rn0g, w) + dtb[:, sl])
        d0g[:, :, sl] = part0.reshape(NB, REQ, 256)
        d1[:, :, sl] = (part0 + part1).reshape(NB, REQ, 256)
        dj = softplus(dot(rn0s, w) + dtb[:, sl])
        acc = jnp.zeros((32, 256), f32)
        for n in range(DS):
            cn = jnp.concatenate([c0b[n], c0b[n]], axis=1)
            acc = acc + cn * (jnp.exp2(dj * (rates_ref[n : n + 1, sl] * (-LOG2E))) * s0[n, :, sl])
        z0 += [acc[:, 0:128], acc[:, 128:256]]
    z0 = jnp.concatenate(z0, axis=0).astype(bf16)
    zzs[:, 64:80, :] = dot(relay, z0).astype(bf16).reshape(NB, 16, 128)

    def children(i, c):
        two = [lax.rem(me + 1 + 2 * i, NB), lax.rem(me + 2 + 2 * i, NB)]
        outs = [c1[b] for b in two]
        deltas = [d1[b] for b in two]
        accs = [jnp.zeros((REQ, CH), f32) for _ in two]
        for n in range(DS):
            rn, sn = rt[n], s1[n]
            for k in range(2):
                accs[k] = accs[k] + outs[k][:, DS + n : DS + n + 1] * (jnp.exp2(deltas[k] * rn) * sn)
        for k in range(2):
            zzs[two[k], 0:64, :] = to_rows(accs[k]).astype(bf16)
        push(zzs.at[two[0]], zzr.at[me], two[0], ZZ, "beam")

        @pl.when(i < NB // 2 - 1)
        def _():
            push(zzs.at[two[1]], zzr.at[me], two[1], ZZ, "beam")

        return c

    lax.fori_loop(0, NB // 2, children, 0)
    zzr[pl.ds(me, 1)] = zzs[pl.ds(me, 1)]

    in0p = dot(og, bc0)[:, 0:DS]
    cross = in0p * own_out[REQ : 2 * REQ]
    mixed = jnp.zeros((REQ, CH), f32)
    for n in range(DS):
        mixed = mixed + cross[:, n : n + 1] * jnp.exp2(d_own1 * rt[n])
    base1 = base1 + mixed * (d0g[pl.ds(me, 1)][0] * conv0p)

    landed(or_, OO)
    landed(lse, LS)
    lanes = iota((8, 128), 1)
    want = lanes == me * 8 + iota((8, 128), 0)
    parts = []
    for p in range(NB):
        lp = lse[p]
        parts.append(
            jnp.concatenate(
                [
                    jnp.sum(jnp.where(want, lp[r : r + 1], 0.0), axis=1, keepdims=True)
                    for r in range(REQ)
                ],
                axis=0,
            )
        )
    top = parts[0]
    for p in range(1, NB):
        top = jnp.maximum(top, parts[p])
    den = jnp.zeros((64, 1), f32)
    num = jnp.zeros((64, HD), f32)
    for p in range(NB):
        w = jnp.exp2(parts[p] - top)
        den = den + w
        num = num + w * or_[p].astype(f32)
    att = dot(swap, (num / den).astype(bf16))
    for s in range(2):
        ao_ref[s, 0] = jnp.concatenate(
            [att[(s * GROUP + h) * 8 : (s * GROUP + h + 1) * 8] for h in range(GROUP)], axis=1
        ).astype(bf16)
    out_a = pltpu.make_async_copy(ao_ref, ao_h, tsem)
    out_a.start()

    landed(zzr, ZZ)
    z1 = jnp.zeros((64, 128), f32)
    for p in range(NB):
        z1 = z1 + zzr[p, 0:64, :].astype(f32)
    z0 = dot(ub0, zzr[:, 64:80, :].reshape(256, 128))
    mo_ref[0, 0] = ((from_rows(z0) + base0) * gate0).astype(bf16)
    mo_ref[1, 0] = ((from_rows(z1) + base1) * gate1).astype(bf16)
    out_m = pltpu.make_async_copy(mo_ref, mo_h, lsem.at[0])
    out_m.start()

    sent(h1s, H1)
    sent(h2s, H2)
    sent(qa, QA)
    sent(zb, ZB, nt, "tensor")
    sent(prb, PR)
    sent(os_, OO)
    sent(lse, LS)
    sent(zzs, ZZ)
    out_a.wait()
    out_m.wait()


def publish(m_ref, a_ref, mo_ref, ao_ref, sem):
    first = pltpu.make_async_copy(m_ref, mo_ref, sem.at[0])
    second = pltpu.make_async_copy(a_ref, ao_ref, sem.at[1])
    first.start()
    second.start()
    first.wait()
    second.wait()


def local(
    ssm_state,
    conv_state,
    suffix_kv,
    mamba_x,
    mamba_gate,
    conv_weight,
    conv_bias,
    xproj_weight,
    dt_gain,
    dtproj_weight,
    dt_bias,
    state_rates,
    skip_gain,
    queries,
    new_kv,
    kv_pool,
    page_order,
    ctx_len,
    parents,
):
    nt = lax.axis_size("tensor")
    hb = pl.BlockSpec(memory_space=pltpu.HBM)
    dma = pltpu.SemaphoreType.DMA
    V = pltpu.VMEM
    operands = [
        parents.transpose(0, 2, 1, 3).reshape(2 * REQ, NB),
        page_order.reshape(POOL // 128, 128),
        ctx_len,
        conv_state.transpose(0, 2, 1, 3)[0],
        conv_weight,
        conv_bias.reshape(LT, 128),
        mamba_x[:, 0],
        mamba_gate[:, 0],
        queries[:, 0],
        new_kv[:, 0],
        suffix_kv[0],
        dt_gain.reshape(1, DT_RANK),
        dt_bias.reshape(1, CH),
        state_rates,
        skip_gain.reshape(1, CH),
        ssm_state.reshape(REQ * DS, CH),
        xproj_weight.T,
        dtproj_weight,
        kv_pool,
    ]
    held = [V(a.shape, a.dtype) for a in operands]
    held[2] = pltpu.SMEM((REQ,), i32)
    outs = (
        jax.ShapeDtypeStruct((2, 1, REQ, CH), bf16),
        jax.ShapeDtypeStruct((2, 1, REQ, GROUP * HD), bf16),
    )
    results = pl.pallas_call(
        kernel,
        out_shape=outs,
        in_specs=[hb] * len(operands),
        out_specs=(hb, hb),
        scratch_shapes=held
        + [
            V(outs[0].shape, bf16),
            V(outs[1].shape, bf16),
            V((NB, 16, 256), bf16),
            V((NB, 16, 256), bf16),
            V((NB, 16, 256), bf16),
            V((NB, 16, 256), bf16),
            V((NB, 64, HD), bf16),
            V((nt, 16, PROJ_PAD), bf16),
            V((NB, 16, PROJ_PAD), bf16),
            V((NB, 80, 128), bf16),
            V((NB, 80, 128), bf16),
            V((NB, 64, HD), bf16),
            V((NB, 64, HD), bf16),
            V((NB, REQ, 128), f32),
            V((32, 128), i32),
            pltpu.SMEM((32, 128), i32),
            V((NBLK, BLK * PAGE), f32),
            V((REQ, 128, HD), bf16),
            V((NBLK + 1, 128, 2 * HD), f32),
            V((NBLK + 1, 128, HD), f32),
            V((NB, 64, HD), f32),
            V((DS, NB * 2, CH), f32),
            V((DS, REQ, CH), f32),
            V((DS, REQ, CH), f32),
            V((NB, REQ, CH), f32),
            V((NB, REQ, CH), f32),
            V((NB, REQ, 128), f32),
            V((128, REQ * 128), f32),
            dma((len(operands),)),
            dma,
            dma((8,)),
            dma((8,)),
        ],
        compiler_params=pltpu.CompilerParams(
            collective_id=0, has_side_effects=True, vmem_limit_bytes=63 * 2**20
        ),
        name="decode",
    )(*operands)
    return pl.pallas_call(
        publish,
        out_shape=outs,
        in_specs=[hb, hb],
        out_specs=(hb, hb),
        scratch_shapes=[dma((2,))],
        compiler_params=pltpu.CompilerParams(vmem_limit_bytes=63 * 2**20),
        name="publish",
    )(*results)


def solution(mesh):
    in_specs = (
        P("beam", None, None, "tensor"),
        P("beam", None, None, "tensor"),
        P("beam", None, None, "tensor"),
        P(None, "beam", None, "tensor"),
        P(None, "beam", None, "tensor"),
        P(None, "tensor"),
        P("tensor"),
        P("tensor", None),
        P(),
        P(None, "tensor"),
        P("tensor"),
        P(None, "tensor"),
        P("tensor"),
        P(None, "beam", None, "tensor"),
        P(None, "beam", None, "tensor"),
        P("beam", None, "tensor"),
        P(),
        P(),
        P(),
    )
    out_specs = (P(None, "beam", None, "tensor"), P(None, "beam", None, "tensor"))
    return jax.shard_map(local, mesh=mesh, in_specs=in_specs, out_specs=out_specs, check_vma=False)
```

```python
import jax
import jax.numpy as jnp
from jax import lax
from jax.experimental import pallas as pl
from jax.experimental.pallas import tpu as pltpu
from jax.sharding import PartitionSpec as P

NB = 16
REQ = 8
DS = 16
DT_RANK = 256
HD = 128
PAGE = 16
MAXP = 512
CH = 1024
LT = CH // 128
GROUP = 4
PAGES = 256
BLK = 16
NBLK = PAGES // BLK + REQ
UNROLL = 8
POOL = 4096
PROJ = DT_RANK + 2 * DS
PROJ_PAD = 384
LOG2E = 1.4426950408889634
NEG = -1e30

f32 = jnp.float32
bf16 = jnp.bfloat16
i32 = jnp.int32
MESH = pl.DeviceIdType.MESH


def iota(shape, dim):
    return lax.broadcasted_iota(i32, shape, dim)


def dot(a, b):
    return lax.dot_general(a, b, (((1,), (0,)), ((), ())), preferred_element_type=f32)


def dot_nt(a, b):
    return lax.dot_general(a, b, (((1,), (1,)), ((), ())), preferred_element_type=f32)


def one(mask):
    return jnp.where(mask, 1.0, 0.0).astype(bf16)


def onef(mask):
    return jnp.where(mask, 1.0, 0.0).astype(f32)


def to_rows(x):
    return jnp.concatenate([x[:, i * 128 : (i + 1) * 128] for i in range(LT)], axis=0)


def from_rows(x):
    return jnp.concatenate([x[i * REQ : (i + 1) * REQ] for i in range(LT)], axis=1)


def silu(v):
    return v / (1.0 + jnp.exp(-v))


def softplus(v):
    return jnp.maximum(v, 0.0) + jnp.log(1.0 + jnp.exp(-jnp.abs(v)))


def slot_key(par, me):
    chosen = par == me
    upper = one(iota((REQ, REQ), 0) < iota((REQ, REQ), 1))
    rank = dot(one(chosen), upper)
    return jnp.where(chosen, rank, -1.0)


def pack_matrix(key):
    rows, cols = NB * LT * 2, LT * REQ
    rb = one((iota((rows, NB), 0) >> 4) == iota((rows, NB), 1))
    cr = one((iota((REQ, cols), 1) & 7) == iota((REQ, cols), 0))
    spread = dot(dot(rb, key.astype(bf16)).astype(bf16), cr)
    row, col = iota((rows, cols), 0), iota((rows, cols), 1)
    return one((spread == (row & 1).astype(f32)) & (((row >> 1) & 7) == (col >> 3)))


def own_column(par, me):
    row = jnp.sum(jnp.where(iota((NB, REQ), 0) == me, par.astype(f32), 0.0), axis=0, keepdims=True)
    eye = iota((REQ, REQ), 0) == iota((REQ, REQ), 1)
    col = jnp.sum(jnp.where(eye, row, 0.0), axis=1, keepdims=True)
    return row, col


def unpack_matrix(par, me):
    row, col = own_column(par, me)
    alike = (row == col) & (iota((REQ, REQ), 1) < iota((REQ, REQ), 0))
    order = jnp.sum(onef(alike), axis=1, keepdims=True)
    code = jnp.concatenate([col * 2.0 + order] * LT, axis=0)
    rows, cols = LT * REQ, NB * LT * 2
    r, c = iota((rows, cols), 0), iota((rows, cols), 1)
    code_of = ((c >> 4) * 2 + (c & 1)).astype(f32)
    return one((code == code_of) & ((r >> 3) == ((c >> 1) & 7)))


def column128(m):
    spread = dot(one((iota((128, NB), 0) >> 3) == iota((128, NB), 1)), m.astype(bf16))
    pick = iota((128, REQ), 1) == (iota((128, REQ), 0) & 7)
    return jnp.sum(jnp.where(pick, spread, 0.0), axis=1, keepdims=True)


def kernel(
    par_h, po_h, ctx_h, cs_h, cw_h, cb_h, x_h, gate_h, q_h, nkv_h, suf_h, gain_h, dtb_h, rates_h, skip_h,
    s_h, xw_h, dtw_h, kv_h,
    mo_h, ao_h,
    par_ref, po_ref, ctx_ref, cs_ref, cw_ref, cb_ref, x_ref, gate_ref, q_ref, nkv_ref, suf_ref, gain_ref, dtb_ref,
    rates_ref, skip_ref, s_v, xw_v, dtw_v, kv_v,
    mo_ref, ao_ref,
    h1s, h1r, has, har, h2s, h2r, hcs, hcr, qa, zb, prb, zzs, zzr, os_, or_, lse,
    tab, tabs, bias, qr, orun, mrun, osf, s0, s1, rt, d1, d0g, c1, okm,
    lsem, tsem, ssem, rsem,
):
    me = lax.axis_index("beam")
    mt = lax.axis_index("tensor")
    nt = zb.shape[0]
    H1, H2, QA, ZB, PR, OO, LS, ZZ, HA, HC = range(10)

    def push(src, dst, to, k, axis):
        pltpu.make_async_remote_copy(
            src_ref=src, dst_ref=dst, send_sem=ssem.at[k], recv_sem=rsem.at[k], device_id={axis: to},
            device_id_type=MESH,
        ).start()

    def exchange(src, dst, k):
        for d in range(1, NB):
            peer = lax.rem(me + d, NB)
            push(src.at[peer], dst.at[me], peer, k, "beam")

    def gather(buf, k, n, my, axis):
        for d in range(1, n):
            push(buf.at[my], buf.at[my], lax.rem(my + d, n), k, axis)

    def all_of(buf, k, n, axis):
        part = buf.at[pl.ds(0, n - 1)]
        return pltpu.make_async_remote_copy(
            src_ref=part, dst_ref=part, send_sem=ssem.at[k], recv_sem=rsem.at[k], device_id={axis: 0},
            device_id_type=MESH,
        )

    def landed(buf, k, n=NB, axis="beam"):
        all_of(buf, k, n, axis).wait_recv()

    def sent(buf, k, n=NB, axis="beam"):
        all_of(buf, k, n, axis).wait_send()

    pairs = [
        (par_h, par_ref), (cs_h, cs_ref), (cw_h, cw_ref), (q_h, q_ref), (s_h, s_v), (rates_h, rates_ref),
        (x_h, x_ref), (cb_h, cb_ref), (po_h, po_ref), (ctx_h, ctx_ref), (xw_h, xw_v), (kv_h, kv_v),
        (suf_h, suf_ref), (nkv_h, nkv_ref), (dtw_h, dtw_v), (dtb_h, dtb_ref), (gain_h, gain_ref),
        (skip_h, skip_ref), (gate_h, gate_ref),
    ]
    copies = [pltpu.make_async_copy(a, b, lsem.at[i]) for i, (a, b) in enumerate(pairs)]
    (c_par, c_cs, c_cw, c_q, c_s, c_rates, c_x, c_cb, c_po, c_ctx, c_xw, c_kv, c_suf, c_nkv, c_dtw, c_dtb, c_gain,
     c_skip, c_gate) = copies
    for c in copies:
        c.start()
    barrier = pltpu.get_barrier_semaphore()
    for d in range(1, NB):
        pl.semaphore_signal(barrier, inc=1, device_id={"beam": lax.rem(me + d, NB)}, device_id_type=MESH)
    for d in range(1, nt):
        pl.semaphore_signal(barrier, inc=1, device_id={"tensor": lax.rem(mt + d, nt)}, device_id_type=MESH)

    c_par.wait()
    par_t = par_ref[...].astype(f32).astype(bf16)
    eye16 = one(iota((NB, NB), 0) == iota((NB, NB), 1))
    p0 = dot_nt(eye16, par_t[0:REQ]).astype(i32)
    p1 = dot_nt(eye16, par_t[REQ : 2 * REQ]).astype(i32)
    key0 = slot_key(p0, me)
    c_cs.wait()
    c_cw.wait()
    cw = cw_ref[...].astype(f32)
    cw_row = [cw[k : k + 1] for k in range(4)]
    win = [cs_ref[k].astype(f32) for k in range(3)]
    a0 = win[0] * cw_row[0] + win[1] * cw_row[1] + win[2] * cw_row[2]
    a1 = win[1] * cw_row[0] + win[2] * cw_row[1]
    both = jnp.concatenate([to_rows(a0), to_rows(a1)], axis=1).astype(bf16)
    packed = dot(pack_matrix(key0), both).astype(bf16)
    h1s[...] = packed[:, 128:256].reshape(NB, 16, 128)
    has[...] = packed[:, 0:128].reshape(NB, 16, 128)
    h1r[pl.ds(me, 1)] = h1s[pl.ds(me, 1)]
    har[pl.ds(me, 1)] = has[pl.ds(me, 1)]

    c_q.wait()
    qrows = jnp.concatenate(
        [q_ref[s][:, h * 128 : (h + 1) * 128].astype(f32) for s in range(2) for h in range(GROUP)], axis=0
    ).astype(bf16)
    ri, ci = iota((64, 64), 0), iota((64, 64), 1)
    swap = one(((ri >> 3) == (ci & 7)) & ((ri & 7) == (ci >> 3)))
    qa[pl.ds(me, 1)] = dot(swap, qrows).astype(bf16)[None]

    pl.semaphore_wait(barrier, NB - 1 + nt - 1)

    exchange(h1s, h1r, H1)
    exchange(has, har, HA)

    key1 = slot_key(p1, me)
    pb1 = pack_matrix(key1)
    ub0 = unpack_matrix(p0, me)
    ub1 = unpack_matrix(p1, me)
    g = jnp.zeros((NB, REQ), i32)
    for p in range(NB):
        g = g + jnp.where(p1 == p, p0[p : p + 1, :], 0)
    c_x.wait()
    c_cb.wait()
    x0 = x_ref[0].astype(f32)
    x1 = x_ref[1].astype(f32)
    cb8 = cb_ref[...].astype(f32)
    cb = jnp.concatenate([cb8[i : i + 1] for i in range(LT)], axis=1)

    landed(h1r, H1)
    w1 = from_rows(dot(ub0, h1r[...].reshape(NB * 16, 128))) + cw_row[2] * x0
    h2s[...] = dot(pb1, to_rows(w1).astype(bf16)).astype(bf16).reshape(NB, 16, 128)
    h2r[pl.ds(me, 1)] = h2s[pl.ds(me, 1)]
    exchange(h2s, h2r, H2)
    gather(qa, QA, NB, me, "beam")

    landed(har, HA)
    c0 = from_rows(dot(ub0, har[...].reshape(NB * 16, 128))) + cw_row[3] * x0 + cb
    conv0 = silu(c0)
    hcs[...] = dot(pb1, to_rows(conv0).astype(bf16)).astype(bf16).reshape(NB, 16, 128)
    hcr[pl.ds(me, 1)] = hcs[pl.ds(me, 1)]

    c_po.wait()
    c_ctx.wait()
    ctx_col = jnp.zeros((REQ, MAXP), i32)
    for r in range(REQ):
        ctx_col = jnp.where(iota((REQ, MAXP), 0) == r, ctx_ref[r], ctx_col)
    nvis = jnp.clip(ctx_col - iota((REQ, MAXP), 1) * PAGE, 0, PAGE)
    po = jnp.concatenate([po_ref[pl.ds(j, REQ, stride=4), :] for j in range(4)], axis=1)
    loc = po - me * PAGES
    flag = (loc >= 0) & (loc < PAGES) & (nvis > 0)
    tri = one(iota((MAXP, MAXP), 0) < iota((MAXP, MAXP), 1))
    rank = dot(one(flag), tri).astype(i32)
    count = jnp.sum(onef(flag), axis=1, keepdims=True).astype(i32)
    nblk = ((count + (BLK - 1)) >> 4).astype(f32)
    eye8 = iota((REQ, REQ), 0) == iota((REQ, REQ), 1)
    nblk_row = jnp.sum(jnp.where(eye8, nblk, 0.0), axis=0, keepdims=True)
    sblk = jnp.sum(
        jnp.where(iota((REQ, REQ), 1) < iota((REQ, REQ), 0), nblk_row, 0.0), axis=1, keepdims=True
    )
    dest = jnp.where(flag, sblk.astype(i32) * BLK + rank, -1)
    hi = dest >> 4
    lo = jnp.where(flag, dest & 15, -1)
    table = jnp.zeros((NBLK, 32), f32)
    for r in range(REQ):
        hot = one(hi[r : r + 1] == iota((NBLK, MAXP), 0))
        low = lo[r : r + 1] == iota((16, MAXP), 0)
        vals = jnp.concatenate(
            [
                jnp.where(low, loc[r : r + 1].astype(f32), 0.0),
                jnp.where(low, nvis[r : r + 1].astype(f32), 0.0),
            ],
            axis=0,
        ).astype(bf16)
        table = table + dot_nt(hot, vals)
    tab[...] = jnp.zeros_like(tab)
    tab[0:NBLK, 0:32] = table.astype(i32)
    lane = iota((REQ, 128), 1)
    subl = iota((REQ, 128), 0)
    sb_i, nb_i = sblk.astype(i32), nblk.astype(i32)
    inside = (sb_i <= lane) & (lane < sb_i + nb_i)
    tab[NBLK : NBLK + 1, :] = jnp.sum(jnp.where(inside, subl, 0).astype(f32), axis=0, keepdims=True).astype(i32)
    tab[NBLK + 1 : NBLK + 2, :] = jnp.sum(
        onef((lane == sb_i) & (nb_i > 0)), axis=0, keepdims=True
    ).astype(i32)
    tab[NBLK + 2 : NBLK + 3, :] = jnp.sum(
        jnp.where((lane == subl) & (nb_i > 0), sb_i + nb_i, 0).astype(f32), axis=0, keepdims=True
    ).astype(i32)
    cp_tab = pltpu.make_async_copy(tab, tabs, tsem)
    cp_tab.start()
    spread = one((iota((16, BLK * PAGE), 1) >> 4) == iota((16, BLK * PAGE), 0))
    seen = dot(table[:, 16:32].astype(bf16), spread)
    bias[...] = jnp.where((iota((NBLK, BLK * PAGE), 1) & 15).astype(f32) < seen, 0.0, NEG)
    orun[0] = jnp.zeros((128, 2 * HD), f32)
    mrun[0] = jnp.full((128, HD), NEG, f32)
    cp_tab.wait()

    c_xw.wait()
    landed(h2r, H2)
    conv1 = silu(from_rows(dot(ub1, h2r[...].reshape(NB * 16, 128))) + cw_row[3] * x1 + cb)
    part = dot_nt(jnp.concatenate([conv0, conv1], axis=0).astype(bf16), xw_v[...])
    zb[pl.ds(mt, 1)] = jnp.zeros((1, 16, PROJ_PAD), bf16)
    zb[pl.ds(mt, 1), :, 0:PROJ] = part.astype(bf16)[None]
    gather(zb, ZB, nt, mt, "tensor")
    exchange(hcs, hcr, HC)


    wide = one((iota((REQ, REQ * 128), 1) >> 7) == iota((REQ, REQ * 128), 0))
    x_s0 = dot(one(p0 == me), wide)
    x_sg = dot(one(g == me), wide)
    x_s1 = dot(one(p1 == me), wide)
    tok = iota((NB, REQ * 128), 1) & 127
    mine = onef(iota((NB, REQ * 128), 0) == me)
    ok0 = jnp.where(tok < 16, x_s0, jnp.where(tok == 16, mine, 0.0))
    ok1 = jnp.where(tok < 16, x_sg, jnp.where(tok == 16, x_s1, jnp.where(tok == 17, mine, 0.0)))
    qi, qj = iota((128, 2 * NB), 0), iota((128, 2 * NB), 1)
    pick = one((((qi >> 2) & 1) == (qj >> 4)) & ((qi >> 3) == (qj & 15)))
    okm[...] = dot(pick, jnp.concatenate([ok0, ok1], axis=0).astype(bf16))

    c_rates.wait()
    for n in range(DS):
        rt[n] = jnp.broadcast_to(rates_ref[n : n + 1, :] * (-LOG2E), (REQ, CH))
    c_s.wait()
    row, col = iota((DS * NB * 2, 128), 0), iota((DS * NB * 2, 128), 1)
    rs_ = one(((iota((DS * NB * 2, NB), 0) >> 1) & 15) == iota((DS * NB * 2, NB), 1))
    crn = one((iota((REQ, 128), 1) >> 4) == iota((REQ, 128), 0))
    keys = dot(rs_, dot(key0.astype(bf16), crn).astype(bf16))
    sel0 = one((keys == (row & 1).astype(f32)) & ((row >> 5) == (col & 15)))
    pi, pj = iota((128, 128), 0), iota((128, 128), 1)
    perm1 = one(((pi & 7) == (pj >> 4)) & ((pi >> 3) == (pj & 15)))
    for j in range(4):
        sl = slice(j * 256, (j + 1) * 256)
        sj = s_v[:, sl].astype(bf16)
        s0[:, :, sl] = dot(sel0, sj).reshape(DS, NB * 2, 256)
        s1[:, :, sl] = dot(perm1, sj).reshape(DS, REQ, 256)


    landed(qa, QA)
    qf = qa[...].astype(f32)
    for r in range(REQ):
        qr[r] = jnp.concatenate([qf[b, r * 8 : (r + 1) * 8] for b in range(NB)], axis=0).astype(bf16)
    c_kv.wait()
    scale = HD**-0.5 * LOG2E
    ones_blk = jnp.ones((BLK * PAGE, HD), bf16)

    def blocks(step, c):
        first = step * UNROLL
        m_old, o_old = mrun[first], orun[first]
        for u in range(UNROLL):
            i = first + u
            kv = jnp.concatenate([kv_v[tabs[i, k] & (PAGES - 1)] for k in range(BLK)], axis=0)
            s = dot_nt(qr[tabs[NBLK, i] & (REQ - 1)], kv[:, 0:HD]) * scale + bias[pl.ds(i, 1), :]
            m_old = jnp.where(tabs[NBLK + 1, i] > 0, NEG, m_old)
            m_new = jnp.maximum(m_old, jnp.max(s, axis=1, keepdims=True))
            e = jnp.exp2(s - jnp.concatenate([m_new, m_new], axis=1)).astype(bf16)
            v = jnp.concatenate([kv[:, HD : 2 * HD], ones_blk], axis=1)
            fade = jnp.exp2(m_old - m_new)
            o_old = o_old * jnp.concatenate([fade, fade], axis=1) + dot(e, v)
            m_old = m_new
            orun[i + 1] = o_old
            mrun[i + 1] = m_old
        return c

    steps = NBLK // UNROLL
    lax.fori_loop(0, 2, blocks, 0)

    landed(zb, ZB, nt, "tensor")
    proj = jnp.zeros((16, PROJ_PAD), f32)
    for t in range(nt):
        proj = proj + zb[t].astype(f32)
    prb[pl.ds(me, 1)] = proj.astype(bf16)[None]
    gather(prb, PR, NB, me, "beam")

    lax.fori_loop(2, steps, blocks, 0)
    c_suf.wait()
    c_nkv.wait()
    nk0 = nkv_ref[0].astype(f32)
    nk1 = nkv_ref[1].astype(f32)
    diag = iota((128, 128), 0) == iota((128, 128), 1)
    ti = iota((16, 256), 0)
    for r in range(REQ):
        tail = jnp.where(ti == 0, nk0[r : r + 1], jnp.where(ti == 1, nk1[r : r + 1], 0.0)).astype(bf16)
        kv = jnp.concatenate([suf_ref[r], tail], axis=0)
        s = jnp.where(
            okm[:, r * 128 : r * 128 + 32] > 0.5, dot_nt(qr[r], kv[:, 0:HD]) * scale, NEG
        )
        last = jnp.clip(tabs[NBLK + 2, r], 0, NBLK)
        m_old = mrun[last]
        m_new = jnp.maximum(m_old, jnp.max(s, axis=1, keepdims=True))
        e = jnp.exp2(s - m_new[:, 0:32]).astype(bf16)
        v = jnp.concatenate([kv[:, HD : 2 * HD], jnp.ones((32, HD), bf16)], axis=1)
        fade = jnp.exp2(m_old - m_new)
        o = orun[last] * jnp.concatenate([fade, fade], axis=1) + dot(e, v)
        total = o[:, HD : 2 * HD]
        val = o[:, 0:HD] / total
        for b in range(NB):
            osf[b, r * 8 : (r + 1) * 8, :] = val[b * 8 : (b + 1) * 8]
        lg = m_new + jnp.log2(total)
        lse[pl.ds(me, 1), r : r + 1, :] = jnp.sum(jnp.where(diag, lg, 0.0), axis=0, keepdims=True)[None]
    os_[...] = osf[...].astype(bf16)
    or_[pl.ds(me, 1)] = os_[pl.ds(me, 1)]
    exchange(os_, or_, OO)
    gather(lse, LS, NB, me, "beam")

    for c in (c_dtw, c_dtb, c_gain, c_skip, c_gate):
        c.wait()
    gain = gain_ref[...]

    def normed(rank_rows):
        mean = jnp.sum(rank_rows * rank_rows, axis=1, keepdims=True) * (1.0 / DT_RANK)
        return (rank_rows * lax.rsqrt(mean + 1e-6) * gain).astype(bf16)

    dtb = dtb_ref[...]
    own = proj.astype(bf16).astype(f32)
    d_own = softplus(dot(normed(own[:, 0:DT_RANK]), dtw_v[...]) + dtb)
    d_own0, d_own1 = d_own[0:REQ], d_own[REQ : 2 * REQ]
    own_in = own[:, DT_RANK : DT_RANK + DS]
    own_out = own[:, DT_RANK + DS : DT_RANK + 2 * DS]
    cb_own = jnp.sum(own_in * own_out, axis=1, keepdims=True)
    skip = skip_ref[...]
    base0 = d_own0 * conv0 * cb_own[0:REQ] + skip * conv0
    base1 = d_own1 * conv1 * cb_own[REQ : 2 * REQ] + skip * conv1
    gate0 = silu(gate_ref[0].astype(f32))
    gate1 = silu(gate_ref[1].astype(f32))

    held_here = column128(onef(g == me))
    g1 = one((column128(p1) == (pj >> 3).astype(f32)) & ((pi & 7) == (pj & 7)))
    r32 = one((iota((32, NB), 0) >> 1) == iota((32, NB), 1))
    c32 = one((iota((REQ, 128), 1) & 7) == iota((REQ, 128), 0))
    key32 = dot(dot(r32, key0.astype(bf16)).astype(bf16), c32)
    si, sj_ = iota((32, 128), 0), iota((32, 128), 1)
    psl = one((key32 == (si & 1).astype(f32)) & ((si >> 1) == (sj_ >> 3)))
    ui, uj = iota((256, 256), 0), iota((256, 256), 1)
    relay = one(((ui >> 4) == ((uj >> 1) & 15)) & (((ui >> 1) & 7) == (uj >> 5)) & ((ui & 1) == (uj & 1)))
    _, own1 = own_column(p1, me)
    gi, gj = iota((REQ, 128), 0), iota((REQ, 128), 1)
    og = one((own1 == (gj >> 3).astype(f32)) & (gi == (gj & 7)))

    landed(prb, PR)
    prf = prb[...].astype(f32)
    pr0 = prf[:, 0:REQ, :].reshape(128, PROJ_PAD)
    pr1 = prf[:, REQ : 2 * REQ, :].reshape(128, PROJ_PAD)
    rn0 = normed(pr0[:, 0:DT_RANK])
    rn1 = normed(pr1[:, 0:DT_RANK])
    bc0 = pr0[:, DT_RANK:PROJ].astype(bf16)
    c1[...] = (pr1[:, DT_RANK:PROJ_PAD] * held_here).reshape(NB, REQ, 128)
    rn0g = dot(g1, rn0).astype(bf16)

    rn0s = dot(psl, rn0).astype(bf16)
    c0s = dot(psl, bc0)
    c0b = [jnp.broadcast_to(c0s[:, DS + n : DS + n + 1], (NB * 2, 128)) for n in range(DS)]
    z0 = []
    for j in range(4):
        sl = slice(j * 256, (j + 1) * 256)
        w = dtw_v[:, sl]
        part1 = softplus(dot(rn1, w) + dtb[:, sl])
        part0 = softplus(dot(rn0g, w) + dtb[:, sl])
        d0g[:, :, sl] = part0.reshape(NB, REQ, 256)
        d1[:, :, sl] = (part0 + part1).reshape(NB, REQ, 256)
        dj = softplus(dot(rn0s, w) + dtb[:, sl])
        acc = jnp.zeros((32, 256), f32)
        for n in range(DS):
            cn = jnp.concatenate([c0b[n], c0b[n]], axis=1)
            acc = acc + cn * (jnp.exp2(dj * (rates_ref[n : n + 1, sl] * (-LOG2E))) * s0[n, :, sl])
        z0 += [acc[:, 0:128], acc[:, 128:256]]
    z0 = jnp.concatenate(z0, axis=0).astype(bf16)
    zzs[:, 64:80, :] = dot(relay, z0).astype(bf16).reshape(NB, 16, 128)

    def children(i, c):
        two = [lax.rem(me + 1 + 2 * i, NB), lax.rem(me + 2 + 2 * i, NB)]
        outs = [c1[b] for b in two]
        deltas = [d1[b] for b in two]
        accs = [jnp.zeros((REQ, CH), f32) for _ in two]
        for n in range(DS):
            rn, sn = rt[n], s1[n]
            for k in range(2):
                accs[k] = accs[k] + outs[k][:, DS + n : DS + n + 1] * (jnp.exp2(deltas[k] * rn) * sn)
        for k in range(2):
            zzs[two[k], 0:64, :] = to_rows(accs[k]).astype(bf16)
        push(zzs.at[two[0]], zzr.at[me], two[0], ZZ, "beam")

        @pl.when(i < NB // 2 - 1)
        def _():
            push(zzs.at[two[1]], zzr.at[me], two[1], ZZ, "beam")

        return c

    lax.fori_loop(0, NB // 2, children, 0)
    zzr[pl.ds(me, 1)] = zzs[pl.ds(me, 1)]

    landed(hcr, HC)
    conv0p = from_rows(dot(ub1, hcr[...].reshape(NB * 16, 128)))
    in0p = dot(og, bc0)[:, 0:DS]
    cross = in0p * own_out[REQ : 2 * REQ]
    mixed = jnp.zeros((REQ, CH), f32)
    for n in range(DS):
        mixed = mixed + cross[:, n : n + 1] * jnp.exp2(d_own1 * rt[n])
    base1 = base1 + mixed * (d0g[pl.ds(me, 1)][0] * conv0p)

    landed(or_, OO)
    landed(lse, LS)
    lanes = iota((8, 128), 1)
    want = lanes == me * 8 + iota((8, 128), 0)
    parts = []
    for p in range(NB):
        lp = lse[p]
        parts.append(
            jnp.concatenate(
                [
                    jnp.sum(jnp.where(want, lp[r : r + 1], 0.0), axis=1, keepdims=True)
                    for r in range(REQ)
                ],
                axis=0,
            )
        )
    top = parts[0]
    for p in range(1, NB):
        top = jnp.maximum(top, parts[p])
    den = jnp.zeros((64, 1), f32)
    num = jnp.zeros((64, HD), f32)
    for p in range(NB):
        w = jnp.exp2(parts[p] - top)
        den = den + w
        num = num + w * or_[p].astype(f32)
    att = dot(swap, (num / den).astype(bf16))
    for s in range(2):
        ao_ref[s, 0] = jnp.concatenate(
            [att[(s * GROUP + h) * 8 : (s * GROUP + h + 1) * 8] for h in range(GROUP)], axis=1
        ).astype(bf16)
    out_a = pltpu.make_async_copy(ao_ref, ao_h, tsem)
    out_a.start()

    landed(zzr, ZZ)
    z1 = jnp.zeros((64, 128), f32)
    for p in range(NB):
        z1 = z1 + zzr[p, 0:64, :].astype(f32)
    z0 = dot(ub0, zzr[:, 64:80, :].reshape(256, 128))
    mo_ref[0, 0] = ((from_rows(z0) + base0) * gate0).astype(bf16)
    mo_ref[1, 0] = ((from_rows(z1) + base1) * gate1).astype(bf16)
    out_m = pltpu.make_async_copy(mo_ref, mo_h, lsem.at[0])
    out_m.start()

    sent(h1s, H1)
    sent(has, HA)
    sent(h2s, H2)
    sent(hcs, HC)
    sent(qa, QA)
    sent(zb, ZB, nt, "tensor")
    sent(prb, PR)
    sent(os_, OO)
    sent(lse, LS)
    sent(zzs, ZZ)
    out_a.wait()
    out_m.wait()


def publish(m_ref, a_ref, mo_ref, ao_ref, m_v, a_v, sem):
    first = pltpu.make_async_copy(m_ref, m_v, sem.at[0])
    second = pltpu.make_async_copy(a_ref, a_v, sem.at[1])
    first.start()
    second.start()
    first.wait()
    first = pltpu.make_async_copy(m_v, mo_ref, sem.at[0])
    first.start()
    second.wait()
    second = pltpu.make_async_copy(a_v, ao_ref, sem.at[1])
    second.start()
    first.wait()
    second.wait()


def local(
    ssm_state,
    conv_state,
    suffix_kv,
    mamba_x,
    mamba_gate,
    conv_weight,
    conv_bias,
    xproj_weight,
    dt_gain,
    dtproj_weight,
    dt_bias,
    state_rates,
    skip_gain,
    queries,
    new_kv,
    kv_pool,
    page_order,
    ctx_len,
    parents,
):
    nt = lax.axis_size("tensor")
    hb = pl.BlockSpec(memory_space=pltpu.HBM)
    dma = pltpu.SemaphoreType.DMA
    V = pltpu.VMEM
    operands = [
        parents.transpose(0, 2, 1, 3).reshape(2 * REQ, NB),
        page_order.reshape(POOL // 128, 128),
        ctx_len,
        conv_state.transpose(0, 2, 1, 3)[0],
        conv_weight,
        conv_bias.reshape(LT, 128),
        mamba_x[:, 0],
        mamba_gate[:, 0],
        queries[:, 0],
        new_kv[:, 0],
        suffix_kv[0],
        dt_gain.reshape(1, DT_RANK),
        dt_bias.reshape(1, CH),
        state_rates,
        skip_gain.reshape(1, CH),
        ssm_state.reshape(REQ * DS, CH),
        xproj_weight.T,
        dtproj_weight,
        kv_pool,
    ]
    held = [V(a.shape, a.dtype) for a in operands]
    held[2] = pltpu.SMEM((REQ,), i32)
    outs = (
        jax.ShapeDtypeStruct((2, 1, REQ, CH), bf16),
        jax.ShapeDtypeStruct((2, 1, REQ, GROUP * HD), bf16),
    )
    results = pl.pallas_call(
        kernel,
        out_shape=outs,
        in_specs=[hb] * len(operands),
        out_specs=(hb, hb),
        scratch_shapes=held
        + [
            V(outs[0].shape, bf16),
            V(outs[1].shape, bf16),
            V((NB, 16, 128), bf16),
            V((NB, 16, 128), bf16),
            V((NB, 16, 128), bf16),
            V((NB, 16, 128), bf16),
            V((NB, 16, 128), bf16),
            V((NB, 16, 128), bf16),
            V((NB, 16, 128), bf16),
            V((NB, 16, 128), bf16),
            V((NB, 64, HD), bf16),
            V((nt, 16, PROJ_PAD), bf16),
            V((NB, 16, PROJ_PAD), bf16),
            V((NB, 80, 128), bf16),
            V((NB, 80, 128), bf16),
            V((NB, 64, HD), bf16),
            V((NB, 64, HD), bf16),
            V((NB, REQ, 128), f32),
            V((32, 128), i32),
            pltpu.SMEM((32, 128), i32),
            V((NBLK, BLK * PAGE), f32),
            V((REQ, 128, HD), bf16),
            V((NBLK + 1, 128, 2 * HD), f32),
            V((NBLK + 1, 128, HD), f32),
            V((NB, 64, HD), f32),
            V((DS, NB * 2, CH), f32),
            V((DS, REQ, CH), f32),
            V((DS, REQ, CH), f32),
            V((NB, REQ, CH), f32),
            V((NB, REQ, CH), f32),
            V((NB, REQ, 128), f32),
            V((128, REQ * 128), f32),
            dma((len(operands),)),
            dma,
            dma((10,)),
            dma((10,)),
        ],
        compiler_params=pltpu.CompilerParams(
            collective_id=0, has_side_effects=True, vmem_limit_bytes=63 * 2**20
        ),
        name="decode",
    )(*operands)
    return pl.pallas_call(
        publish,
        out_shape=outs,
        in_specs=[hb, hb],
        out_specs=(hb, hb),
        scratch_shapes=[V(outs[0].shape, bf16), V(outs[1].shape, bf16), dma((2,))],
        compiler_params=pltpu.CompilerParams(vmem_limit_bytes=63 * 2**20),
        name="publish",
    )(*results)


def solution(mesh):
    in_specs = (
        P("beam", None, None, "tensor"),
        P("beam", None, None, "tensor"),
        P("beam", None, None, "tensor"),
        P(None, "beam", None, "tensor"),
        P(None, "beam", None, "tensor"),
        P(None, "tensor"),
        P("tensor"),
        P("tensor", None),
        P(),
        P(None, "tensor"),
        P("tensor"),
        P(None, "tensor"),
        P("tensor"),
        P(None, "beam", None, "tensor"),
        P(None, "beam", None, "tensor"),
        P("beam", None, "tensor"),
        P(),
        P(),
        P(),
    )
    out_specs = (P(None, "beam", None, "tensor"), P(None, "beam", None, "tensor"))
    return jax.shard_map(local, mesh=mesh, in_specs=in_specs, out_specs=out_specs, check_vma=False)
```

```python
import jax
import jax.numpy as jnp
from jax import lax
from jax.experimental import pallas as pl
from jax.experimental.pallas import tpu as pltpu
from jax.sharding import PartitionSpec as P

NB = 16
REQ = 8
DS = 16
DT_RANK = 256
HD = 128
PAGE = 16
MAXP = 512
CH = 1024
LT = CH // 128
GROUP = 4
PAGES = 256
BLK = 16
NBLK = PAGES // BLK + REQ
UNROLL = 8
POOL = 4096
PROJ = DT_RANK + 2 * DS
PROJ_PAD = 384
LOG2E = 1.4426950408889634
NEG = -1e30

f32 = jnp.float32
bf16 = jnp.bfloat16
i32 = jnp.int32
MESH = pl.DeviceIdType.MESH


def iota(shape, dim):
    return lax.broadcasted_iota(i32, shape, dim)


def dot(a, b):
    return lax.dot_general(a, b, (((1,), (0,)), ((), ())), preferred_element_type=f32)


def dot_nt(a, b):
    return lax.dot_general(a, b, (((1,), (1,)), ((), ())), preferred_element_type=f32)


def one(mask):
    return jnp.where(mask, 1.0, 0.0).astype(bf16)


def onef(mask):
    return jnp.where(mask, 1.0, 0.0).astype(f32)


def to_rows(x):
    return jnp.concatenate([x[:, i * 128 : (i + 1) * 128] for i in range(LT)], axis=0)


def from_rows(x):
    return jnp.concatenate([x[i * REQ : (i + 1) * REQ] for i in range(LT)], axis=1)


def silu(v):
    return v / (1.0 + jnp.exp(-v))


def softplus(v):
    return jnp.maximum(v, 0.0) + jnp.log(1.0 + jnp.exp(-jnp.abs(v)))


def slot_key(par, me):
    chosen = par == me
    upper = one(iota((REQ, REQ), 0) < iota((REQ, REQ), 1))
    rank = dot(one(chosen), upper)
    return jnp.where(chosen, rank, -1.0)


def pack_matrix(key):
    rows, cols = NB * LT * 2, LT * REQ
    rb = one((iota((rows, NB), 0) >> 4) == iota((rows, NB), 1))
    cr = one((iota((REQ, cols), 1) & 7) == iota((REQ, cols), 0))
    spread = dot(dot(rb, key.astype(bf16)).astype(bf16), cr)
    row, col = iota((rows, cols), 0), iota((rows, cols), 1)
    return one((spread == (row & 1).astype(f32)) & (((row >> 1) & 7) == (col >> 3)))


def own_column(par, me):
    row = jnp.sum(jnp.where(iota((NB, REQ), 0) == me, par.astype(f32), 0.0), axis=0, keepdims=True)
    eye = iota((REQ, REQ), 0) == iota((REQ, REQ), 1)
    col = jnp.sum(jnp.where(eye, row, 0.0), axis=1, keepdims=True)
    return row, col


def unpack_matrix(par, me):
    row, col = own_column(par, me)
    alike = (row == col) & (iota((REQ, REQ), 1) < iota((REQ, REQ), 0))
    order = jnp.sum(onef(alike), axis=1, keepdims=True)
    code = jnp.concatenate([col * 2.0 + order] * LT, axis=0)
    rows, cols = LT * REQ, NB * LT * 2
    r, c = iota((rows, cols), 0), iota((rows, cols), 1)
    code_of = ((c >> 4) * 2 + (c & 1)).astype(f32)
    return one((code == code_of) & ((r >> 3) == ((c >> 1) & 7)))


def column128(m):
    spread = dot(one((iota((128, NB), 0) >> 3) == iota((128, NB), 1)), m.astype(bf16))
    pick = iota((128, REQ), 1) == (iota((128, REQ), 0) & 7)
    return jnp.sum(jnp.where(pick, spread, 0.0), axis=1, keepdims=True)


def kernel(
    par_h, po_h, ctx_h, cs_h, cw_h, cb_h, x_h, gate_h, q_h, nkv_h, suf_h, gain_h, dtb_h, rates_h, skip_h,
    s_h, xw_h, dtw_h, kv_h,
    mo_h, ao_h,
    par_ref, po_ref, ctx_ref, cs_ref, cw_ref, cb_ref, x_ref, gate_ref, q_ref, nkv_ref, suf_ref, gain_ref, dtb_ref,
    rates_ref, skip_ref, s_v, xw_v, dtw_v, kv_v,
    mo_ref, ao_ref,
    h1s, h1r, has, har, h2s, h2r, hcs, hcr, qa, pv, pas, par_r, zb, both_pr, zzs, zzr, os_, or_, lse,
    tab, tabs, bias, qr, orun, mrun, osf, s0, s1, rt, d1, d0g, c1, okm,
    lsem, tsem, ssem, rsem,
):
    me = lax.axis_index("beam")
    mt = lax.axis_index("tensor")
    nz = zb.shape[0]
    core, mz = mt & 1, mt >> 1
    other = mt + 1 - 2 * core
    H1, H2, QA, ZB, PR, OO, LS, ZZ, HA, HC, PA, SW = range(12)

    def beam_peer(d):
        return ((me + d) & (NB - 1), mt)

    def z_peer(d):
        return (me, (((mz + d) & (nz - 1)) << 1) + core)

    def remote(src, dst, k, device):
        return pltpu.make_async_remote_copy(
            src_ref=src, dst_ref=dst, send_sem=ssem.at[k], recv_sem=rsem.at[k], device_id=device,
            device_id_type=MESH,
        )

    def exchange(src, dst, k):
        for d in range(1, NB):
            peer = beam_peer(d)
            remote(src.at[peer[0]], dst.at[me], k, peer).start()

    def gather(buf, k, at, peers):
        for peer in peers:
            remote(buf.at[at], buf.at[at], k, peer).start()

    beam_peers = [beam_peer(d) for d in range(1, NB)]
    z_peers = [z_peer(d) for d in range(1, nz)]

    def all_of(buf, k):
        part = buf.at[pl.ds(0, buf.shape[0] - 1)]
        return remote(part, part, k, (me, mt))

    def landed(buf, k):
        all_of(buf, k).wait_recv()

    def sent(buf, k):
        all_of(buf, k).wait_send()

    pairs = [
        (par_h, par_ref), (cs_h, cs_ref), (cw_h, cw_ref), (q_h, q_ref), (s_h, s_v), (rates_h, rates_ref),
        (x_h, x_ref), (cb_h, cb_ref), (po_h, po_ref), (ctx_h, ctx_ref), (xw_h, xw_v), (kv_h, kv_v),
        (suf_h, suf_ref), (nkv_h, nkv_ref), (dtw_h, dtw_v), (dtb_h, dtb_ref), (gain_h, gain_ref),
        (skip_h, skip_ref), (gate_h, gate_ref),
    ]
    copies = [pltpu.make_async_copy(a, b, lsem.at[i]) for i, (a, b) in enumerate(pairs)]
    (c_par, c_cs, c_cw, c_q, c_s, c_rates, c_x, c_cb, c_po, c_ctx, c_xw, c_kv, c_suf, c_nkv, c_dtw, c_dtb, c_gain,
     c_skip, c_gate) = copies
    for c in copies[0:4]:
        c.start()
    barrier = pltpu.get_barrier_semaphore()
    greeted = beam_peers + z_peers + [(me, other)]
    for peer in greeted:
        pl.semaphore_signal(barrier, inc=1, device_id=peer, device_id_type=MESH)
    for c in copies[4:]:
        c.start()

    c_par.wait()
    par_t = par_ref[...].astype(f32).astype(bf16)
    eye16 = one(iota((NB, NB), 0) == iota((NB, NB), 1))
    p0 = dot_nt(eye16, par_t[0:REQ]).astype(i32)
    p1 = dot_nt(eye16, par_t[REQ : 2 * REQ]).astype(i32)
    key0 = slot_key(p0, me)
    c_cs.wait()
    c_cw.wait()
    cw = cw_ref[...].astype(f32)
    cw_row = [cw[k : k + 1] for k in range(4)]
    win = [cs_ref[k].astype(f32) for k in range(3)]
    a0 = win[0] * cw_row[0] + win[1] * cw_row[1] + win[2] * cw_row[2]
    a1 = win[1] * cw_row[0] + win[2] * cw_row[1]
    both = jnp.concatenate([to_rows(a0), to_rows(a1)], axis=1).astype(bf16)
    packed = dot(pack_matrix(key0), both).astype(bf16)
    h1s[...] = packed[:, 128:256].reshape(NB, 16, 128)
    has[...] = packed[:, 0:128].reshape(NB, 16, 128)
    h1r[pl.ds(me, 1)] = h1s[pl.ds(me, 1)]
    har[pl.ds(me, 1)] = has[pl.ds(me, 1)]

    c_q.wait()
    qrows = jnp.concatenate(
        [q_ref[s][:, h * 128 : (h + 1) * 128].astype(f32) for s in range(2) for h in range(GROUP)], axis=0
    ).astype(bf16)
    ri, ci = iota((64, 64), 0), iota((64, 64), 1)
    swap = one(((ri >> 3) == (ci & 7)) & ((ri & 7) == (ci >> 3)))
    qa[pl.ds(me, 1)] = dot(swap, qrows).astype(bf16)[None]

    pl.semaphore_wait(barrier, len(greeted))

    exchange(h1s, h1r, H1)
    exchange(has, har, HA)

    key1 = slot_key(p1, me)
    pb1 = pack_matrix(key1)
    ub0 = unpack_matrix(p0, me)
    ub1 = unpack_matrix(p1, me)
    g = jnp.zeros((NB, REQ), i32)
    for p in range(NB):
        g = g + jnp.where(p1 == p, p0[p : p + 1, :], 0)
    c_x.wait()
    c_cb.wait()
    x0 = x_ref[0].astype(f32)
    x1 = x_ref[1].astype(f32)
    cb8 = cb_ref[...].astype(f32)
    cb = jnp.concatenate([cb8[i : i + 1] for i in range(LT)], axis=1)

    landed(h1r, H1)
    w1 = from_rows(dot(ub0, h1r[...].reshape(NB * 16, 128))) + cw_row[2] * x0
    h2s[...] = dot(pb1, to_rows(w1).astype(bf16)).astype(bf16).reshape(NB, 16, 128)
    h2r[pl.ds(me, 1)] = h2s[pl.ds(me, 1)]
    exchange(h2s, h2r, H2)
    gather(qa, QA, me, beam_peers)

    landed(har, HA)
    c0 = from_rows(dot(ub0, har[...].reshape(NB * 16, 128))) + cw_row[3] * x0 + cb
    conv0 = silu(c0)
    hcs[...] = dot(pb1, to_rows(conv0).astype(bf16)).astype(bf16).reshape(NB, 16, 128)
    hcr[pl.ds(me, 1)] = hcs[pl.ds(me, 1)]

    c_po.wait()
    c_ctx.wait()
    ctx_col = jnp.zeros((REQ, MAXP), i32)
    for r in range(REQ):
        ctx_col = jnp.where(iota((REQ, MAXP), 0) == r, ctx_ref[r], ctx_col)
    nvis = jnp.clip(ctx_col - iota((REQ, MAXP), 1) * PAGE, 0, PAGE)
    po = jnp.concatenate([po_ref[pl.ds(j, REQ, stride=4), :] for j in range(4)], axis=1)
    loc = po - me * PAGES
    flag = (loc >= 0) & (loc < PAGES) & (nvis > 0)
    tri = one(iota((MAXP, MAXP), 0) < iota((MAXP, MAXP), 1))
    rank = dot(one(flag), tri).astype(i32)
    count = jnp.sum(onef(flag), axis=1, keepdims=True).astype(i32)
    nblk = ((count + (BLK - 1)) >> 4).astype(f32)
    eye8 = iota((REQ, REQ), 0) == iota((REQ, REQ), 1)
    nblk_row = jnp.sum(jnp.where(eye8, nblk, 0.0), axis=0, keepdims=True)
    sblk = jnp.sum(
        jnp.where(iota((REQ, REQ), 1) < iota((REQ, REQ), 0), nblk_row, 0.0), axis=1, keepdims=True
    )
    dest = jnp.where(flag, sblk.astype(i32) * BLK + rank, -1)
    hi = dest >> 4
    lo = jnp.where(flag, dest & 15, -1)
    table = jnp.zeros((NBLK, 32), f32)
    for r in range(REQ):
        hot = one(hi[r : r + 1] == iota((NBLK, MAXP), 0))
        low = lo[r : r + 1] == iota((16, MAXP), 0)
        vals = jnp.concatenate(
            [
                jnp.where(low, loc[r : r + 1].astype(f32), 0.0),
                jnp.where(low, nvis[r : r + 1].astype(f32), 0.0),
            ],
            axis=0,
        ).astype(bf16)
        table = table + dot_nt(hot, vals)
    tab[...] = jnp.zeros_like(tab)
    tab[0:NBLK, 0:32] = table.astype(i32)
    lane = iota((REQ, 128), 1)
    subl = iota((REQ, 128), 0)
    sb_i, nb_i = sblk.astype(i32), nblk.astype(i32)
    inside = (sb_i <= lane) & (lane < sb_i + nb_i)
    tab[NBLK : NBLK + 1, :] = jnp.sum(jnp.where(inside, subl, 0).astype(f32), axis=0, keepdims=True).astype(i32)
    tab[NBLK + 1 : NBLK + 2, :] = jnp.sum(
        onef((lane == sb_i) & (nb_i > 0)), axis=0, keepdims=True
    ).astype(i32)
    tab[NBLK + 2 : NBLK + 3, :] = jnp.sum(
        jnp.where((lane == subl) & (nb_i > 0), sb_i + nb_i, 0).astype(f32), axis=0, keepdims=True
    ).astype(i32)
    cp_tab = pltpu.make_async_copy(tab, tabs, tsem)
    cp_tab.start()
    spread = one((iota((16, BLK * PAGE), 1) >> 4) == iota((16, BLK * PAGE), 0))
    seen = dot(table[:, 16:32].astype(bf16), spread)
    bias[...] = jnp.where((iota((NBLK, BLK * PAGE), 1) & 15).astype(f32) < seen, 0.0, NEG)
    orun[0] = jnp.zeros((128, 2 * HD), f32)
    mrun[0] = jnp.full((128, HD), NEG, f32)
    cp_tab.wait()

    pv[...] = jnp.zeros_like(pv)

    c_xw.wait()
    landed(h2r, H2)
    conv1 = silu(from_rows(dot(ub1, h2r[...].reshape(NB * 16, 128))) + cw_row[3] * x1 + cb)
    part = dot_nt(jnp.concatenate([conv0, conv1], axis=0).astype(bf16), xw_v[...])
    pv[:, 0:PROJ] = part

    def packed8(at):
        x = pv[pl.ds(pl.multiple_of(at * REQ, REQ), REQ), :]
        rank_rows = jnp.concatenate([x[:, 0:128], x[:, 128:256]], axis=0)
        maps = jnp.concatenate([x[:, 256:384], jnp.zeros((REQ, 128), f32)], axis=0)
        return jnp.concatenate([rank_rows, maps], axis=1)

    pas[...] = packed8(1 - core)
    to_core = remote(pas, par_r, PA, (me, other))
    to_core.start()
    exchange(hcs, hcr, HC)
    to_core.wait_recv()
    zb[pl.ds(mz, 1)] = (packed8(core) + par_r[...]).astype(bf16)[None]
    gather(zb, ZB, mz, z_peers)


    wide = one((iota((REQ, REQ * 128), 1) >> 7) == iota((REQ, REQ * 128), 0))
    x_s0 = dot(one(p0 == me), wide)
    x_sg = dot(one(g == me), wide)
    x_s1 = dot(one(p1 == me), wide)
    tok = iota((NB, REQ * 128), 1) & 127
    mine = onef(iota((NB, REQ * 128), 0) == me)
    ok0 = jnp.where(tok < 16, x_s0, jnp.where(tok == 16, mine, 0.0))
    ok1 = jnp.where(tok < 16, x_sg, jnp.where(tok == 16, x_s1, jnp.where(tok == 17, mine, 0.0)))
    qi, qj = iota((128, 2 * NB), 0), iota((128, 2 * NB), 1)
    pick = one((((qi >> 2) & 1) == (qj >> 4)) & ((qi >> 3) == (qj & 15)))
    okm[...] = dot(pick, jnp.concatenate([ok0, ok1], axis=0).astype(bf16))

    c_rates.wait()
    for n in range(DS):
        rt[n] = jnp.broadcast_to(rates_ref[n : n + 1, :] * (-LOG2E), (REQ, CH))
    c_s.wait()
    row, col = iota((DS * NB * 2, 128), 0), iota((DS * NB * 2, 128), 1)
    rs_ = one(((iota((DS * NB * 2, NB), 0) >> 1) & 15) == iota((DS * NB * 2, NB), 1))
    crn = one((iota((REQ, 128), 1) >> 4) == iota((REQ, 128), 0))
    keys = dot(rs_, dot(key0.astype(bf16), crn).astype(bf16))
    sel0 = one((keys == (row & 1).astype(f32)) & ((row >> 5) == (col & 15)))
    pi, pj = iota((128, 128), 0), iota((128, 128), 1)
    perm1 = one(((pi & 7) == (pj >> 4)) & ((pi >> 3) == (pj & 15)))
    for j in range(4):
        sl = slice(j * 256, (j + 1) * 256)
        sj = s_v[:, sl].astype(bf16)
        s0[:, :, sl] = dot(sel0, sj).reshape(DS, NB * 2, 256)
        s1[:, :, sl] = dot(perm1, sj).reshape(DS, REQ, 256)


    landed(qa, QA)
    qf = qa[...].astype(f32)
    for r in range(REQ):
        qr[r] = jnp.concatenate([qf[b, r * 8 : (r + 1) * 8] for b in range(NB)], axis=0).astype(bf16)
    c_kv.wait()
    scale = HD**-0.5 * LOG2E
    ones_blk = jnp.ones((BLK * PAGE, HD), bf16)

    def blocks(step, c):
        first = step * UNROLL
        m_old, o_old = mrun[first], orun[first]
        for u in range(UNROLL):
            i = first + u
            kv = jnp.concatenate([kv_v[tabs[i, k] & (PAGES - 1)] for k in range(BLK)], axis=0)
            s = dot_nt(qr[tabs[NBLK, i] & (REQ - 1)], kv[:, 0:HD]) * scale + bias[pl.ds(i, 1), :]
            m_old = jnp.where(tabs[NBLK + 1, i] > 0, NEG, m_old)
            m_new = jnp.maximum(m_old, jnp.max(s, axis=1, keepdims=True))
            e = jnp.exp2(s - jnp.concatenate([m_new, m_new], axis=1)).astype(bf16)
            v = jnp.concatenate([kv[:, HD : 2 * HD], ones_blk], axis=1)
            fade = jnp.exp2(m_old - m_new)
            o_old = o_old * jnp.concatenate([fade, fade], axis=1) + dot(e, v)
            m_old = m_new
            orun[i + 1] = o_old
            mrun[i + 1] = m_old
        return c

    steps = NBLK // UNROLL
    lax.fori_loop(0, 2, blocks, 0)

    landed(zb, ZB)
    proj = jnp.zeros((16, 256), f32)
    for t in range(nz):
        proj = proj + zb[t].astype(f32)
    mine_pr = both_pr.at[core]
    mine_pr[pl.ds(me, 1)] = proj.astype(bf16)[None]
    gather(mine_pr, PR, me, beam_peers)

    lax.fori_loop(2, steps, blocks, 0)
    c_suf.wait()
    c_nkv.wait()
    nk0 = nkv_ref[0].astype(f32)
    nk1 = nkv_ref[1].astype(f32)
    diag = iota((128, 128), 0) == iota((128, 128), 1)
    ti = iota((16, 256), 0)
    for r in range(REQ):
        tail = jnp.where(ti == 0, nk0[r : r + 1], jnp.where(ti == 1, nk1[r : r + 1], 0.0)).astype(bf16)
        kv = jnp.concatenate([suf_ref[r], tail], axis=0)
        s = jnp.where(
            okm[:, r * 128 : r * 128 + 32] > 0.5, dot_nt(qr[r], kv[:, 0:HD]) * scale, NEG
        )
        last = jnp.clip(tabs[NBLK + 2, r], 0, NBLK)
        m_old = mrun[last]
        m_new = jnp.maximum(m_old, jnp.max(s, axis=1, keepdims=True))
        e = jnp.exp2(s - m_new[:, 0:32]).astype(bf16)
        v = jnp.concatenate([kv[:, HD : 2 * HD], jnp.ones((32, HD), bf16)], axis=1)
        fade = jnp.exp2(m_old - m_new)
        o = orun[last] * jnp.concatenate([fade, fade], axis=1) + dot(e, v)
        total = o[:, HD : 2 * HD]
        val = o[:, 0:HD] / total
        for b in range(NB):
            osf[b, r * 8 : (r + 1) * 8, :] = val[b * 8 : (b + 1) * 8]
        lg = m_new + jnp.log2(total)
        lse[pl.ds(me, 1), r : r + 1, :] = jnp.sum(jnp.where(diag, lg, 0.0), axis=0, keepdims=True)[None]
    os_[...] = osf[...].astype(bf16)
    or_[pl.ds(me, 1)] = os_[pl.ds(me, 1)]
    exchange(os_, or_, OO)
    gather(lse, LS, me, beam_peers)

    for c in (c_dtw, c_dtb, c_gain, c_skip, c_gate):
        c.wait()
    gain = gain_ref[...]

    def normed(rank_rows):
        mean = jnp.sum(rank_rows * rank_rows, axis=1, keepdims=True) * (1.0 / DT_RANK)
        return (rank_rows * lax.rsqrt(mean + 1e-6) * gain).astype(bf16)

    dtb = dtb_ref[...]
    gate0 = silu(gate_ref[0].astype(f32))
    gate1 = silu(gate_ref[1].astype(f32))

    held_here = column128(onef(g == me))
    g1 = one((column128(p1) == (pj >> 3).astype(f32)) & ((pi & 7) == (pj & 7)))
    r32 = one((iota((32, NB), 0) >> 1) == iota((32, NB), 1))
    c32 = one((iota((REQ, 128), 1) & 7) == iota((REQ, 128), 0))
    key32 = dot(dot(r32, key0.astype(bf16)).astype(bf16), c32)
    si, sj_ = iota((32, 128), 0), iota((32, 128), 1)
    psl = one((key32 == (si & 1).astype(f32)) & ((si >> 1) == (sj_ >> 3)))
    ui, uj = iota((256, 256), 0), iota((256, 256), 1)
    relay = one(((ui >> 4) == ((uj >> 1) & 15)) & (((ui >> 1) & 7) == (uj >> 5)) & ((ui & 1) == (uj & 1)))
    _, own1 = own_column(p1, me)
    gi, gj = iota((REQ, 128), 0), iota((REQ, 128), 1)
    og = one((own1 == (gj >> 3).astype(f32)) & (gi == (gj & 7)))

    landed(mine_pr, PR)
    swap_cores = remote(mine_pr, mine_pr, SW, (me, other))
    swap_cores.start()
    swap_cores.wait_recv()

    def unpacked(x):
        x = x.astype(f32)
        return jnp.concatenate([x[..., 0:REQ, 0:128], x[..., REQ : 2 * REQ, 0:128]], axis=-1), x[..., 0:REQ, 128:256]

    rank0, maps0 = unpacked(both_pr[0])
    rank1, maps1 = unpacked(both_pr[1])
    rn0 = normed(rank0.reshape(128, DT_RANK))
    rn1 = normed(rank1.reshape(128, DT_RANK))
    bc0 = maps0.reshape(128, 128)[:, 0 : 2 * DS].astype(bf16)
    c1[...] = (maps1.reshape(128, 128) * held_here).reshape(NB, REQ, 128)
    rn0g = dot(g1, rn0).astype(bf16)

    rn0s = dot(psl, rn0).astype(bf16)
    c0s = dot(psl, bc0)
    c0b = [jnp.broadcast_to(c0s[:, DS + n : DS + n + 1], (NB * 2, 128)) for n in range(DS)]
    z0 = []
    for j in range(4):
        sl = slice(j * 256, (j + 1) * 256)
        w = dtw_v[:, sl]
        part1 = softplus(dot(rn1, w) + dtb[:, sl])
        part0 = softplus(dot(rn0g, w) + dtb[:, sl])
        d0g[:, :, sl] = part0.reshape(NB, REQ, 256)
        d1[:, :, sl] = (part0 + part1).reshape(NB, REQ, 256)
        dj = softplus(dot(rn0s, w) + dtb[:, sl])
        acc = jnp.zeros((32, 256), f32)
        for n in range(DS):
            cn = jnp.concatenate([c0b[n], c0b[n]], axis=1)
            acc = acc + cn * (jnp.exp2(dj * (rates_ref[n : n + 1, sl] * (-LOG2E))) * s0[n, :, sl])
        z0 += [acc[:, 0:128], acc[:, 128:256]]
    z0 = jnp.concatenate(z0, axis=0).astype(bf16)
    zzs[:, 64:80, :] = dot(relay, z0).astype(bf16).reshape(NB, 16, 128)

    def children(i, c):
        two = [(me + 1 + 2 * i) & (NB - 1), (me + 2 + 2 * i) & (NB - 1)]
        outs = [c1[b] for b in two]
        deltas = [d1[b] for b in two]
        accs = [jnp.zeros((REQ, CH), f32) for _ in two]
        for n in range(DS):
            rn, sn = rt[n], s1[n]
            for k in range(2):
                accs[k] = accs[k] + outs[k][:, DS + n : DS + n + 1] * (jnp.exp2(deltas[k] * rn) * sn)
        for k in range(2):
            zzs[two[k], 0:64, :] = to_rows(accs[k]).astype(bf16)
        remote(zzs.at[two[0]], zzr.at[me], ZZ, (two[0], mt)).start()

        @pl.when(i < NB // 2 - 1)
        def _():
            remote(zzs.at[two[1]], zzr.at[me], ZZ, (two[1], mt)).start()

        return c

    lax.fori_loop(0, NB // 2, children, 0)
    zzr[pl.ds(me, 1)] = zzs[pl.ds(me, 1)]

    own_rank, own_maps = zip(*[unpacked(both_pr[s, pl.ds(me, 1)][0]) for s in range(2)])
    d_own = softplus(dot(normed(jnp.concatenate(own_rank, axis=0)), dtw_v[...]) + dtb)
    d_own0, d_own1 = d_own[0:REQ], d_own[REQ : 2 * REQ]
    own_in = [m[:, 0:DS] for m in own_maps]
    own_out = [m[:, DS : 2 * DS] for m in own_maps]
    cb_own = [jnp.sum(a * b, axis=1, keepdims=True) for a, b in zip(own_in, own_out)]
    skip = skip_ref[...]
    base0 = d_own0 * conv0 * cb_own[0] + skip * conv0
    base1 = d_own1 * conv1 * cb_own[1] + skip * conv1

    landed(hcr, HC)
    conv0p = from_rows(dot(ub1, hcr[...].reshape(NB * 16, 128)))
    in0p = dot(og, bc0)[:, 0:DS]
    cross = in0p * own_out[1]
    mixed = jnp.zeros((REQ, CH), f32)
    for n in range(DS):
        mixed = mixed + cross[:, n : n + 1] * jnp.exp2(d_own1 * rt[n])
    base1 = base1 + mixed * (d0g[pl.ds(me, 1)][0] * conv0p)

    landed(or_, OO)
    landed(lse, LS)
    lanes = iota((8, 128), 1)
    want = lanes == me * 8 + iota((8, 128), 0)
    parts = []
    for p in range(NB):
        lp = lse[p]
        parts.append(
            jnp.concatenate(
                [
                    jnp.sum(jnp.where(want, lp[r : r + 1], 0.0), axis=1, keepdims=True)
                    for r in range(REQ)
                ],
                axis=0,
            )
        )
    top = parts[0]
    for p in range(1, NB):
        top = jnp.maximum(top, parts[p])
    den = jnp.zeros((64, 1), f32)
    num = jnp.zeros((64, HD), f32)
    for p in range(NB):
        w = jnp.exp2(parts[p] - top)
        den = den + w
        num = num + w * or_[p].astype(f32)
    att = dot(swap, (num / den).astype(bf16))
    for s in range(2):
        ao_ref[s, 0] = jnp.concatenate(
            [att[(s * GROUP + h) * 8 : (s * GROUP + h + 1) * 8] for h in range(GROUP)], axis=1
        ).astype(bf16)
    out_a = pltpu.make_async_copy(ao_ref, ao_h, tsem)
    out_a.start()

    landed(zzr, ZZ)
    z1 = jnp.zeros((64, 128), f32)
    for p in range(NB):
        z1 = z1 + zzr[p, 0:64, :].astype(f32)
    z0 = dot(ub0, zzr[:, 64:80, :].reshape(256, 128))
    mo_ref[0, 0] = ((from_rows(z0) + base0) * gate0).astype(bf16)
    mo_ref[1, 0] = ((from_rows(z1) + base1) * gate1).astype(bf16)
    out_m = pltpu.make_async_copy(mo_ref, mo_h, lsem.at[0])
    out_m.start()

    sent(h1s, H1)
    sent(has, HA)
    sent(h2s, H2)
    sent(hcs, HC)
    sent(qa, QA)
    to_core.wait_send()
    sent(zb, ZB)
    sent(mine_pr, PR)
    swap_cores.wait_send()
    sent(os_, OO)
    sent(lse, LS)
    sent(zzs, ZZ)
    out_a.wait()
    out_m.wait()


def publish(m_ref, a_ref, mo_ref, ao_ref, m_v, a_v, sem):
    first = pltpu.make_async_copy(m_ref, m_v, sem.at[0])
    second = pltpu.make_async_copy(a_ref, a_v, sem.at[1])
    first.start()
    second.start()
    first.wait()
    first = pltpu.make_async_copy(m_v, mo_ref, sem.at[0])
    first.start()
    second.wait()
    second = pltpu.make_async_copy(a_v, ao_ref, sem.at[1])
    second.start()
    first.wait()
    second.wait()


def local(
    ssm_state,
    conv_state,
    suffix_kv,
    mamba_x,
    mamba_gate,
    conv_weight,
    conv_bias,
    xproj_weight,
    dt_gain,
    dtproj_weight,
    dt_bias,
    state_rates,
    skip_gain,
    queries,
    new_kv,
    kv_pool,
    page_order,
    ctx_len,
    parents,
):
    nt = lax.axis_size("tensor")
    hb = pl.BlockSpec(memory_space=pltpu.HBM)
    dma = pltpu.SemaphoreType.DMA
    V = pltpu.VMEM
    operands = [
        parents.transpose(0, 2, 1, 3).reshape(2 * REQ, NB),
        page_order.reshape(POOL // 128, 128),
        ctx_len,
        conv_state.transpose(0, 2, 1, 3)[0],
        conv_weight,
        conv_bias.reshape(LT, 128),
        mamba_x[:, 0],
        mamba_gate[:, 0],
        queries[:, 0],
        new_kv[:, 0],
        suffix_kv[0],
        dt_gain.reshape(1, DT_RANK),
        dt_bias.reshape(1, CH),
        state_rates,
        skip_gain.reshape(1, CH),
        ssm_state.reshape(REQ * DS, CH),
        xproj_weight.T,
        dtproj_weight,
        kv_pool,
    ]
    held = [V(a.shape, a.dtype) for a in operands]
    held[2] = pltpu.SMEM((REQ,), i32)
    outs = (
        jax.ShapeDtypeStruct((2, 1, REQ, CH), bf16),
        jax.ShapeDtypeStruct((2, 1, REQ, GROUP * HD), bf16),
    )
    results = pl.pallas_call(
        kernel,
        out_shape=outs,
        in_specs=[hb] * len(operands),
        out_specs=(hb, hb),
        scratch_shapes=held
        + [
            V(outs[0].shape, bf16),
            V(outs[1].shape, bf16),
            V((NB, 16, 128), bf16),
            V((NB, 16, 128), bf16),
            V((NB, 16, 128), bf16),
            V((NB, 16, 128), bf16),
            V((NB, 16, 128), bf16),
            V((NB, 16, 128), bf16),
            V((NB, 16, 128), bf16),
            V((NB, 16, 128), bf16),
            V((NB, 64, HD), bf16),
            V((16, PROJ_PAD), f32),
            V((16, 256), f32),
            V((16, 256), f32),
            V((nt // 2, 16, 256), bf16),
            V((2, NB, 16, 256), bf16),
            V((NB, 80, 128), bf16),
            V((NB, 80, 128), bf16),
            V((NB, 64, HD), bf16),
            V((NB, 64, HD), bf16),
            V((NB, REQ, 128), f32),
            V((32, 128), i32),
            pltpu.SMEM((32, 128), i32),
            V((NBLK, BLK * PAGE), f32),
            V((REQ, 128, HD), bf16),
            V((NBLK + 1, 128, 2 * HD), f32),
            V((NBLK + 1, 128, HD), f32),
            V((NB, 64, HD), f32),
            V((DS, NB * 2, CH), f32),
            V((DS, REQ, CH), f32),
            V((DS, REQ, CH), f32),
            V((NB, REQ, CH), f32),
            V((NB, REQ, CH), f32),
            V((NB, REQ, 128), f32),
            V((128, REQ * 128), f32),
            dma((len(operands),)),
            dma,
            dma((12,)),
            dma((12,)),
        ],
        compiler_params=pltpu.CompilerParams(
            collective_id=0, has_side_effects=True, vmem_limit_bytes=63 * 2**20
        ),
        name="decode",
    )(*operands)
    return pl.pallas_call(
        publish,
        out_shape=outs,
        in_specs=[hb, hb],
        out_specs=(hb, hb),
        scratch_shapes=[V(outs[0].shape, bf16), V(outs[1].shape, bf16), dma((2,))],
        compiler_params=pltpu.CompilerParams(vmem_limit_bytes=63 * 2**20),
        name="publish",
    )(*results)


def solution(mesh):
    in_specs = (
        P("beam", None, None, "tensor"),
        P("beam", None, None, "tensor"),
        P("beam", None, None, "tensor"),
        P(None, "beam", None, "tensor"),
        P(None, "beam", None, "tensor"),
        P(None, "tensor"),
        P("tensor"),
        P("tensor", None),
        P(),
        P(None, "tensor"),
        P("tensor"),
        P(None, "tensor"),
        P("tensor"),
        P(None, "beam", None, "tensor"),
        P(None, "beam", None, "tensor"),
        P("beam", None, "tensor"),
        P(),
        P(),
        P(),
    )
    out_specs = (P(None, "beam", None, "tensor"), P(None, "beam", None, "tensor"))
    return jax.shard_map(local, mesh=mesh, in_specs=in_specs, out_specs=out_specs, check_vma=False)
```

```python
import jax
import jax.numpy as jnp
from jax import lax
from jax.experimental import pallas as pl
from jax.experimental.pallas import tpu as pltpu
from jax.sharding import PartitionSpec as P

NB = 16
REQ = 8
DS = 16
DT_RANK = 256
HD = 128
PAGE = 16
MAXP = 512
CH = 1024
LT = CH // 128
GROUP = 4
PAGES = 256
BLK = 16
NBLK = PAGES // BLK + REQ
UNROLL = 8
POOL = 4096
PROJ = DT_RANK + 2 * DS
PROJ_PAD = 384
LOG2E = 1.4426950408889634
NEG = -1e30

f32 = jnp.float32
bf16 = jnp.bfloat16
i32 = jnp.int32
MESH = pl.DeviceIdType.MESH


def iota(shape, dim):
    return lax.broadcasted_iota(i32, shape, dim)


def dot(a, b):
    return lax.dot_general(a, b, (((1,), (0,)), ((), ())), preferred_element_type=f32)


def dot_nt(a, b):
    return lax.dot_general(a, b, (((1,), (1,)), ((), ())), preferred_element_type=f32)


def one(mask):
    return jnp.where(mask, 1.0, 0.0).astype(bf16)


def onef(mask):
    return jnp.where(mask, 1.0, 0.0).astype(f32)


def to_rows(x):
    return jnp.concatenate([x[:, i * 128 : (i + 1) * 128] for i in range(LT)], axis=0)


def from_rows(x):
    return jnp.concatenate([x[i * REQ : (i + 1) * REQ] for i in range(LT)], axis=1)


def silu(v):
    return v / (1.0 + jnp.exp(-v))


def softplus(v):
    return jnp.maximum(v, 0.0) + jnp.log(1.0 + jnp.exp(-jnp.abs(v)))


def slot_key(par, me):
    chosen = par == me
    upper = one(iota((REQ, REQ), 0) < iota((REQ, REQ), 1))
    rank = dot(one(chosen), upper)
    return jnp.where(chosen, rank, -1.0)


def pack_matrix(key):
    rows, cols = NB * LT * 2, LT * REQ
    rb = one((iota((rows, NB), 0) >> 4) == iota((rows, NB), 1))
    cr = one((iota((REQ, cols), 1) & 7) == iota((REQ, cols), 0))
    spread = dot(dot(rb, key.astype(bf16)).astype(bf16), cr)
    row, col = iota((rows, cols), 0), iota((rows, cols), 1)
    return one((spread == (row & 1).astype(f32)) & (((row >> 1) & 7) == (col >> 3)))


def own_column(par, me):
    row = jnp.sum(jnp.where(iota((NB, REQ), 0) == me, par.astype(f32), 0.0), axis=0, keepdims=True)
    eye = iota((REQ, REQ), 0) == iota((REQ, REQ), 1)
    col = jnp.sum(jnp.where(eye, row, 0.0), axis=1, keepdims=True)
    return row, col


def unpack_matrix(par, me):
    row, col = own_column(par, me)
    alike = (row == col) & (iota((REQ, REQ), 1) < iota((REQ, REQ), 0))
    order = jnp.sum(onef(alike), axis=1, keepdims=True)
    code = jnp.concatenate([col * 2.0 + order] * LT, axis=0)
    rows, cols = LT * REQ, NB * LT * 2
    r, c = iota((rows, cols), 0), iota((rows, cols), 1)
    code_of = ((c >> 4) * 2 + (c & 1)).astype(f32)
    return one((code == code_of) & ((r >> 3) == ((c >> 1) & 7)))


def column128(m):
    spread = dot(one((iota((128, NB), 0) >> 3) == iota((128, NB), 1)), m.astype(bf16))
    pick = iota((128, REQ), 1) == (iota((128, REQ), 0) & 7)
    return jnp.sum(jnp.where(pick, spread, 0.0), axis=1, keepdims=True)


def kernel(
    par_h, po_h, ctx_h, cs_h, cw_h, cb_h, x_h, gate_h, q_h, nkv_h, suf_h, gain_h, dtb_h, rates_h, skip_h,
    s_h, xw_h, dtw_h, kv_h,
    mo_h, ao_h,
    par_ref, po_ref, ctx_ref, cs_ref, cw_ref, cb_ref, x_ref, gate_ref, q_ref, nkv_ref, suf_ref, gain_ref, dtb_ref,
    rates_ref, skip_ref, s_v, xw_v, dtw_v, kv_v,
    mo_ref, ao_ref,
    h1s, h1r, hcs, hcr, qa, zb, prb, zzs, zzr, os_, or_, lse,
    tab, tabs, bias, qr, orun, mrun, osf, s0, s1, rt, d1, d0g, c1, okm,
    lsem, tsem, ssem, rsem,
):
    me = lax.axis_index("beam")
    mt = lax.axis_index("tensor")
    nt = zb.shape[0]
    H1, QA, ZB, PR, OO, LS, ZZ, HC = range(8)

    def remote(src, dst, k, device):
        return pltpu.make_async_remote_copy(
            src_ref=src, dst_ref=dst, send_sem=ssem.at[k], recv_sem=rsem.at[k], device_id=device,
            device_id_type=MESH,
        )

    beam_peers = [((me + d) & (NB - 1), mt) for d in range(1, NB)]
    tensor_peers = [(me, (mt + d) & (nt - 1)) for d in range(1, nt)]

    def exchange(src, dst, k):
        for peer in beam_peers:
            remote(src.at[peer[0]], dst.at[me], k, peer).start()

    def gather(buf, k, at, peers):
        for peer in peers:
            remote(buf.at[at], buf.at[at], k, peer).start()

    def all_of(buf, k):
        part = buf.at[pl.ds(0, buf.shape[0] - 1)]
        return remote(part, part, k, (me, mt))

    def landed(buf, k):
        all_of(buf, k).wait_recv()

    def sent(buf, k):
        all_of(buf, k).wait_send()

    pairs = [
        (par_h, par_ref), (cs_h, cs_ref), (cw_h, cw_ref), (x_h, x_ref), (q_h, q_ref), (s_h, s_v),
        (rates_h, rates_ref), (cb_h, cb_ref), (po_h, po_ref), (ctx_h, ctx_ref), (xw_h, xw_v), (kv_h, kv_v),
        (suf_h, suf_ref), (nkv_h, nkv_ref), (dtw_h, dtw_v), (dtb_h, dtb_ref), (gain_h, gain_ref),
        (skip_h, skip_ref), (gate_h, gate_ref),
    ]
    copies = [pltpu.make_async_copy(a, b, lsem.at[i]) for i, (a, b) in enumerate(pairs)]
    (c_par, c_cs, c_cw, c_x, c_q, c_s, c_rates, c_cb, c_po, c_ctx, c_xw, c_kv, c_suf, c_nkv, c_dtw, c_dtb, c_gain,
     c_skip, c_gate) = copies
    for c in copies[0:5]:
        c.start()
    barrier = pltpu.get_barrier_semaphore()
    greeted = beam_peers + tensor_peers
    for peer in greeted:
        pl.semaphore_signal(barrier, inc=1, device_id=peer, device_id_type=MESH)
    for c in copies[5:]:
        c.start()

    c_par.wait()
    par_t = par_ref[...].astype(f32).astype(bf16)
    eye16 = one(iota((NB, NB), 0) == iota((NB, NB), 1))
    p0 = dot_nt(eye16, par_t[0:REQ]).astype(i32)
    p1 = dot_nt(eye16, par_t[REQ : 2 * REQ]).astype(i32)
    key0 = slot_key(p0, me)
    c_cs.wait()
    c_cw.wait()
    cw = cw_ref[...].astype(f32)
    cw_row = [cw[k : k + 1] for k in range(4)]
    win = [cs_ref[k].astype(f32) for k in range(3)]
    a0 = win[0] * cw_row[0] + win[1] * cw_row[1] + win[2] * cw_row[2]
    a1 = win[1] * cw_row[0] + win[2] * cw_row[1]
    h1s[:, 0:64, :] = jnp.broadcast_to(to_rows(a1).astype(bf16)[None], (NB, 64, 128))
    h1s[:, 64:80, :] = dot(pack_matrix(key0), to_rows(a0).astype(bf16)).astype(bf16).reshape(NB, 16, 128)
    key1 = slot_key(p1, me)
    pb1 = pack_matrix(key1)
    c_x.wait()
    x0 = x_ref[0].astype(f32)
    x1 = x_ref[1].astype(f32)
    h1s[:, 80:96, :] = dot(pb1, to_rows(x0).astype(bf16)).astype(bf16).reshape(NB, 16, 128)
    h1r[pl.ds(me, 1)] = h1s[pl.ds(me, 1)]

    c_q.wait()
    qrows = jnp.concatenate(
        [q_ref[s][:, h * 128 : (h + 1) * 128].astype(f32) for s in range(2) for h in range(GROUP)], axis=0
    ).astype(bf16)
    ri, ci = iota((64, 64), 0), iota((64, 64), 1)
    swap = one(((ri >> 3) == (ci & 7)) & ((ri & 7) == (ci >> 3)))
    qa[pl.ds(me, 1)] = dot(swap, qrows).astype(bf16)[None]

    pl.semaphore_wait(barrier, len(greeted))

    exchange(h1s, h1r, H1)
    gather(qa, QA, me, beam_peers)

    ub0 = unpack_matrix(p0, me)
    ub1 = unpack_matrix(p1, me)
    g = jnp.zeros((NB, REQ), i32)
    for p in range(NB):
        g = g + jnp.where(p1 == p, p0[p : p + 1, :], 0)
    _, g_own = own_column(g, me)
    g64 = jnp.concatenate([g_own] * LT, axis=0)
    ai, aj = iota((64, NB * 64), 0), iota((64, NB * 64), 1)
    ug = one((g64 == (aj >> 6).astype(f32)) & (ai == (aj & 63)))
    c_cb.wait()
    cb8 = cb_ref[...].astype(f32)
    cb = jnp.concatenate([cb8[i : i + 1] for i in range(LT)], axis=1)

    c_po.wait()
    c_ctx.wait()
    ctx_col = jnp.zeros((REQ, MAXP), i32)
    for r in range(REQ):
        ctx_col = jnp.where(iota((REQ, MAXP), 0) == r, ctx_ref[r], ctx_col)
    nvis = jnp.clip(ctx_col - iota((REQ, MAXP), 1) * PAGE, 0, PAGE)
    po = jnp.concatenate([po_ref[pl.ds(j, REQ, stride=4), :] for j in range(4)], axis=1)
    loc = po - me * PAGES
    flag = (loc >= 0) & (loc < PAGES) & (nvis > 0)
    tri = one(iota((MAXP, MAXP), 0) < iota((MAXP, MAXP), 1))
    rank = dot(one(flag), tri).astype(i32)
    count = jnp.sum(onef(flag), axis=1, keepdims=True).astype(i32)
    nblk = ((count + (BLK - 1)) >> 4).astype(f32)
    eye8 = iota((REQ, REQ), 0) == iota((REQ, REQ), 1)
    nblk_row = jnp.sum(jnp.where(eye8, nblk, 0.0), axis=0, keepdims=True)
    sblk = jnp.sum(
        jnp.where(iota((REQ, REQ), 1) < iota((REQ, REQ), 0), nblk_row, 0.0), axis=1, keepdims=True
    )
    dest = jnp.where(flag, sblk.astype(i32) * BLK + rank, -1)
    hi = dest >> 4
    lo = jnp.where(flag, dest & 15, -1)
    table = jnp.zeros((NBLK, 32), f32)
    for r in range(REQ):
        hot = one(hi[r : r + 1] == iota((NBLK, MAXP), 0))
        low = lo[r : r + 1] == iota((16, MAXP), 0)
        vals = jnp.concatenate(
            [
                jnp.where(low, loc[r : r + 1].astype(f32), 0.0),
                jnp.where(low, nvis[r : r + 1].astype(f32), 0.0),
            ],
            axis=0,
        ).astype(bf16)
        table = table + dot_nt(hot, vals)
    tab[...] = jnp.zeros_like(tab)
    tab[0:NBLK, 0:32] = table.astype(i32)
    lane = iota((REQ, 128), 1)
    subl = iota((REQ, 128), 0)
    sb_i, nb_i = sblk.astype(i32), nblk.astype(i32)
    inside = (sb_i <= lane) & (lane < sb_i + nb_i)
    tab[NBLK : NBLK + 1, :] = jnp.sum(jnp.where(inside, subl, 0).astype(f32), axis=0, keepdims=True).astype(i32)
    tab[NBLK + 1 : NBLK + 2, :] = jnp.sum(
        onef((lane == sb_i) & (nb_i > 0)), axis=0, keepdims=True
    ).astype(i32)
    tab[NBLK + 2 : NBLK + 3, :] = jnp.sum(
        jnp.where((lane == subl) & (nb_i > 0), sb_i + nb_i, 0).astype(f32), axis=0, keepdims=True
    ).astype(i32)
    cp_tab = pltpu.make_async_copy(tab, tabs, tsem)
    cp_tab.start()
    spread = one((iota((16, BLK * PAGE), 1) >> 4) == iota((16, BLK * PAGE), 0))
    seen = dot(table[:, 16:32].astype(bf16), spread)
    bias[...] = jnp.where((iota((NBLK, BLK * PAGE), 1) & 15).astype(f32) < seen, 0.0, NEG)
    orun[0] = jnp.zeros((128, 2 * HD), f32)
    mrun[0] = jnp.full((128, HD), NEG, f32)
    cp_tab.wait()

    c_xw.wait()
    landed(h1r, H1)
    conv0 = silu(from_rows(dot(ub0, h1r[:, 64:80, :].reshape(NB * 16, 128))) + cw_row[3] * x0 + cb)
    older = from_rows(dot(ug, h1r[:, 0:64, :].reshape(NB * 64, 128)))
    newer = from_rows(dot(ub1, h1r[:, 80:96, :].reshape(NB * 16, 128)))
    conv1 = silu(older + cw_row[2] * newer + cw_row[3] * x1 + cb)
    part = dot_nt(jnp.concatenate([conv0, conv1], axis=0).astype(bf16), xw_v[...])
    zb[pl.ds(mt, 1)] = jnp.zeros((1, 16, PROJ_PAD), bf16)
    zb[pl.ds(mt, 1), :, 0:PROJ] = part.astype(bf16)[None]
    gather(zb, ZB, mt, tensor_peers)
    hcs[...] = dot(pb1, to_rows(conv0).astype(bf16)).astype(bf16).reshape(NB, 16, 128)
    hcr[pl.ds(me, 1)] = hcs[pl.ds(me, 1)]
    exchange(hcs, hcr, HC)


    wide = one((iota((REQ, REQ * 128), 1) >> 7) == iota((REQ, REQ * 128), 0))
    x_s0 = dot(one(p0 == me), wide)
    x_sg = dot(one(g == me), wide)
    x_s1 = dot(one(p1 == me), wide)
    tok = iota((NB, REQ * 128), 1) & 127
    mine = onef(iota((NB, REQ * 128), 0) == me)
    ok0 = jnp.where(tok < 16, x_s0, jnp.where(tok == 16, mine, 0.0))
    ok1 = jnp.where(tok < 16, x_sg, jnp.where(tok == 16, x_s1, jnp.where(tok == 17, mine, 0.0)))
    qi, qj = iota((128, 2 * NB), 0), iota((128, 2 * NB), 1)
    pick = one((((qi >> 2) & 1) == (qj >> 4)) & ((qi >> 3) == (qj & 15)))
    okm[...] = dot(pick, jnp.concatenate([ok0, ok1], axis=0).astype(bf16))

    c_rates.wait()
    for n in range(DS):
        rt[n] = jnp.broadcast_to(rates_ref[n : n + 1, :] * (-LOG2E), (REQ, CH))
    c_s.wait()
    row, col = iota((DS * NB * 2, 128), 0), iota((DS * NB * 2, 128), 1)
    rs_ = one(((iota((DS * NB * 2, NB), 0) >> 1) & 15) == iota((DS * NB * 2, NB), 1))
    crn = one((iota((REQ, 128), 1) >> 4) == iota((REQ, 128), 0))
    keys = dot(rs_, dot(key0.astype(bf16), crn).astype(bf16))
    sel0 = one((keys == (row & 1).astype(f32)) & ((row >> 5) == (col & 15)))
    pi, pj = iota((128, 128), 0), iota((128, 128), 1)
    perm1 = one(((pi & 7) == (pj >> 4)) & ((pi >> 3) == (pj & 15)))
    for j in range(4):
        sl = slice(j * 256, (j + 1) * 256)
        sj = s_v[:, sl].astype(bf16)
        s0[:, :, sl] = dot(sel0, sj).reshape(DS, NB * 2, 256)
        s1[:, :, sl] = dot(perm1, sj).reshape(DS, REQ, 256)


    landed(qa, QA)
    qf = qa[...].astype(f32)
    for r in range(REQ):
        qr[r] = jnp.concatenate([qf[b, r * 8 : (r + 1) * 8] for b in range(NB)], axis=0).astype(bf16)
    c_kv.wait()
    scale = HD**-0.5 * LOG2E
    ones_blk = jnp.ones((BLK * PAGE, HD), bf16)

    def blocks(step, c):
        first = step * UNROLL
        m_old, o_old = mrun[first], orun[first]
        for u in range(UNROLL):
            i = first + u
            kv = jnp.concatenate([kv_v[tabs[i, k] & (PAGES - 1)] for k in range(BLK)], axis=0)
            s = dot_nt(qr[tabs[NBLK, i] & (REQ - 1)], kv[:, 0:HD]) * scale + bias[pl.ds(i, 1), :]
            m_old = jnp.where(tabs[NBLK + 1, i] > 0, NEG, m_old)
            m_new = jnp.maximum(m_old, jnp.max(s, axis=1, keepdims=True))
            e = jnp.exp2(s - jnp.concatenate([m_new, m_new], axis=1)).astype(bf16)
            v = jnp.concatenate([kv[:, HD : 2 * HD], ones_blk], axis=1)
            fade = jnp.exp2(m_old - m_new)
            o_old = o_old * jnp.concatenate([fade, fade], axis=1) + dot(e, v)
            m_old = m_new
            orun[i + 1] = o_old
            mrun[i + 1] = m_old
        return c

    steps = NBLK // UNROLL
    lax.fori_loop(0, 2, blocks, 0)

    landed(zb, ZB)
    proj = jnp.zeros((16, PROJ_PAD), f32)
    for t in range(nt):
        proj = proj + zb[t].astype(f32)
    prb[pl.ds(me, 1)] = proj.astype(bf16)[None]
    gather(prb, PR, me, beam_peers)

    lax.fori_loop(2, steps, blocks, 0)
    c_suf.wait()
    c_nkv.wait()
    nk0 = nkv_ref[0].astype(f32)
    nk1 = nkv_ref[1].astype(f32)
    diag = iota((128, 128), 0) == iota((128, 128), 1)
    ti = iota((16, 256), 0)
    for r in range(REQ):
        tail = jnp.where(ti == 0, nk0[r : r + 1], jnp.where(ti == 1, nk1[r : r + 1], 0.0)).astype(bf16)
        kv = jnp.concatenate([suf_ref[r], tail], axis=0)
        s = jnp.where(
            okm[:, r * 128 : r * 128 + 32] > 0.5, dot_nt(qr[r], kv[:, 0:HD]) * scale, NEG
        )
        last = jnp.clip(tabs[NBLK + 2, r], 0, NBLK)
        m_old = mrun[last]
        m_new = jnp.maximum(m_old, jnp.max(s, axis=1, keepdims=True))
        e = jnp.exp2(s - m_new[:, 0:32]).astype(bf16)
        v = jnp.concatenate([kv[:, HD : 2 * HD], jnp.ones((32, HD), bf16)], axis=1)
        fade = jnp.exp2(m_old - m_new)
        o = orun[last] * jnp.concatenate([fade, fade], axis=1) + dot(e, v)
        total = o[:, HD : 2 * HD]
        val = o[:, 0:HD] / total
        for b in range(NB):
            osf[b, r * 8 : (r + 1) * 8, :] = val[b * 8 : (b + 1) * 8]
        lg = m_new + jnp.log2(total)
        lse[pl.ds(me, 1), r : r + 1, :] = jnp.sum(jnp.where(diag, lg, 0.0), axis=0, keepdims=True)[None]
    os_[...] = osf[...].astype(bf16)
    or_[pl.ds(me, 1)] = os_[pl.ds(me, 1)]
    exchange(os_, or_, OO)
    gather(lse, LS, me, beam_peers)

    for c in (c_dtw, c_dtb, c_gain, c_skip, c_gate):
        c.wait()
    gain = gain_ref[...]

    def normed(rank_rows):
        mean = jnp.sum(rank_rows * rank_rows, axis=1, keepdims=True) * (1.0 / DT_RANK)
        return (rank_rows * lax.rsqrt(mean + 1e-6) * gain).astype(bf16)

    dtb = dtb_ref[...]
    own = proj.astype(bf16).astype(f32)
    d_own = softplus(dot(normed(own[:, 0:DT_RANK]), dtw_v[...]) + dtb)
    d_own0, d_own1 = d_own[0:REQ], d_own[REQ : 2 * REQ]
    own_in = own[:, DT_RANK : DT_RANK + DS]
    own_out = own[:, DT_RANK + DS : DT_RANK + 2 * DS]
    cb_own = jnp.sum(own_in * own_out, axis=1, keepdims=True)
    skip = skip_ref[...]
    base0 = d_own0 * conv0 * cb_own[0:REQ] + skip * conv0
    base1 = d_own1 * conv1 * cb_own[REQ : 2 * REQ] + skip * conv1
    gate0 = silu(gate_ref[0].astype(f32))
    gate1 = silu(gate_ref[1].astype(f32))

    held_here = column128(onef(g == me))
    g1 = one((column128(p1) == (pj >> 3).astype(f32)) & ((pi & 7) == (pj & 7)))
    r32 = one((iota((32, NB), 0) >> 1) == iota((32, NB), 1))
    c32 = one((iota((REQ, 128), 1) & 7) == iota((REQ, 128), 0))
    key32 = dot(dot(r32, key0.astype(bf16)).astype(bf16), c32)
    si, sj_ = iota((32, 128), 0), iota((32, 128), 1)
    psl = one((key32 == (si & 1).astype(f32)) & ((si >> 1) == (sj_ >> 3)))
    ui, uj = iota((256, 256), 0), iota((256, 256), 1)
    relay = one(((ui >> 4) == ((uj >> 1) & 15)) & (((ui >> 1) & 7) == (uj >> 5)) & ((ui & 1) == (uj & 1)))
    _, own1 = own_column(p1, me)
    gi, gj = iota((REQ, 128), 0), iota((REQ, 128), 1)
    og = one((own1 == (gj >> 3).astype(f32)) & (gi == (gj & 7)))

    landed(prb, PR)
    prf = prb[...].astype(f32)
    pr0 = prf[:, 0:REQ, :].reshape(128, PROJ_PAD)
    pr1 = prf[:, REQ : 2 * REQ, :].reshape(128, PROJ_PAD)
    rn0 = normed(pr0[:, 0:DT_RANK])
    rn1 = normed(pr1[:, 0:DT_RANK])
    bc0 = pr0[:, DT_RANK:PROJ].astype(bf16)
    c1[...] = (pr1[:, DT_RANK:PROJ_PAD] * held_here).reshape(NB, REQ, 128)
    rn0g = dot(g1, rn0).astype(bf16)

    rn0s = dot(psl, rn0).astype(bf16)
    c0s = dot(psl, bc0)
    c0b = [jnp.broadcast_to(c0s[:, DS + n : DS + n + 1], (NB * 2, 128)) for n in range(DS)]
    z0 = []
    for j in range(4):
        sl = slice(j * 256, (j + 1) * 256)
        w = dtw_v[:, sl]
        part1 = softplus(dot(rn1, w) + dtb[:, sl])
        part0 = softplus(dot(rn0g, w) + dtb[:, sl])
        d0g[:, :, sl] = part0.reshape(NB, REQ, 256)
        d1[:, :, sl] = (part0 + part1).reshape(NB, REQ, 256)
        dj = softplus(dot(rn0s, w) + dtb[:, sl])
        acc = jnp.zeros((32, 256), f32)
        for n in range(DS):
            cn = jnp.concatenate([c0b[n], c0b[n]], axis=1)
            acc = acc + cn * (jnp.exp2(dj * (rates_ref[n : n + 1, sl] * (-LOG2E))) * s0[n, :, sl])
        z0 += [acc[:, 0:128], acc[:, 128:256]]
    z0 = jnp.concatenate(z0, axis=0).astype(bf16)
    zzs[:, 64:80, :] = dot(relay, z0).astype(bf16).reshape(NB, 16, 128)

    def children(i, c):
        two = [(me + 1 + 2 * i) & (NB - 1), (me + 2 + 2 * i) & (NB - 1)]
        outs = [c1[b] for b in two]
        deltas = [d1[b] for b in two]
        accs = [jnp.zeros((REQ, CH), f32) for _ in two]
        for n in range(DS):
            rn, sn = rt[n], s1[n]
            for k in range(2):
                accs[k] = accs[k] + outs[k][:, DS + n : DS + n + 1] * (jnp.exp2(deltas[k] * rn) * sn)
        for k in range(2):
            zzs[two[k], 0:64, :] = to_rows(accs[k]).astype(bf16)
        remote(zzs.at[two[0]], zzr.at[me], ZZ, (two[0], mt)).start()

        @pl.when(i < NB // 2 - 1)
        def _():
            remote(zzs.at[two[1]], zzr.at[me], ZZ, (two[1], mt)).start()

        return c

    lax.fori_loop(0, NB // 2, children, 0)
    zzr[pl.ds(me, 1)] = zzs[pl.ds(me, 1)]

    landed(hcr, HC)
    conv0p = from_rows(dot(ub1, hcr[...].reshape(NB * 16, 128)))
    in0p = dot(og, bc0)[:, 0:DS]
    cross = in0p * own_out[REQ : 2 * REQ]
    mixed = jnp.zeros((REQ, CH), f32)
    for n in range(DS):
        mixed = mixed + cross[:, n : n + 1] * jnp.exp2(d_own1 * rt[n])
    base1 = base1 + mixed * (d0g[pl.ds(me, 1)][0] * conv0p)

    landed(or_, OO)
    landed(lse, LS)
    lanes = iota((8, 128), 1)
    want = lanes == me * 8 + iota((8, 128), 0)
    parts = []
    for p in range(NB):
        lp = lse[p]
        parts.append(
            jnp.concatenate(
                [
                    jnp.sum(jnp.where(want, lp[r : r + 1], 0.0), axis=1, keepdims=True)
                    for r in range(REQ)
                ],
                axis=0,
            )
        )
    top = parts[0]
    for p in range(1, NB):
        top = jnp.maximum(top, parts[p])
    den = jnp.zeros((64, 1), f32)
    num = jnp.zeros((64, HD), f32)
    for p in range(NB):
        w = jnp.exp2(parts[p] - top)
        den = den + w
        num = num + w * or_[p].astype(f32)
    att = dot(swap, (num / den).astype(bf16))
    for s in range(2):
        ao_ref[s, 0] = jnp.concatenate(
            [att[(s * GROUP + h) * 8 : (s * GROUP + h + 1) * 8] for h in range(GROUP)], axis=1
        ).astype(bf16)
    out_a = pltpu.make_async_copy(ao_ref, ao_h, tsem)
    out_a.start()

    landed(zzr, ZZ)
    z1 = jnp.zeros((64, 128), f32)
    for p in range(NB):
        z1 = z1 + zzr[p, 0:64, :].astype(f32)
    z0 = dot(ub0, zzr[:, 64:80, :].reshape(256, 128))
    mo_ref[0, 0] = ((from_rows(z0) + base0) * gate0).astype(bf16)
    mo_ref[1, 0] = ((from_rows(z1) + base1) * gate1).astype(bf16)
    out_m = pltpu.make_async_copy(mo_ref, mo_h, lsem.at[0])
    out_m.start()

    sent(h1s, H1)
    sent(hcs, HC)
    sent(qa, QA)
    sent(zb, ZB)
    sent(prb, PR)
    sent(os_, OO)
    sent(lse, LS)
    sent(zzs, ZZ)
    out_a.wait()
    out_m.wait()


def publish(m_ref, a_ref, mo_ref, ao_ref, m_v, a_v, sem):
    first = pltpu.make_async_copy(m_ref, m_v, sem.at[0])
    second = pltpu.make_async_copy(a_ref, a_v, sem.at[1])
    first.start()
    second.start()
    first.wait()
    first = pltpu.make_async_copy(m_v, mo_ref, sem.at[0])
    first.start()
    second.wait()
    second = pltpu.make_async_copy(a_v, ao_ref, sem.at[1])
    second.start()
    first.wait()
    second.wait()


def local(
    ssm_state,
    conv_state,
    suffix_kv,
    mamba_x,
    mamba_gate,
    conv_weight,
    conv_bias,
    xproj_weight,
    dt_gain,
    dtproj_weight,
    dt_bias,
    state_rates,
    skip_gain,
    queries,
    new_kv,
    kv_pool,
    page_order,
    ctx_len,
    parents,
):
    nt = lax.axis_size("tensor")
    hb = pl.BlockSpec(memory_space=pltpu.HBM)
    dma = pltpu.SemaphoreType.DMA
    V = pltpu.VMEM
    operands = [
        parents.transpose(0, 2, 1, 3).reshape(2 * REQ, NB),
        page_order.reshape(POOL // 128, 128),
        ctx_len,
        conv_state.transpose(0, 2, 1, 3)[0],
        conv_weight,
        conv_bias.reshape(LT, 128),
        mamba_x[:, 0],
        mamba_gate[:, 0],
        queries[:, 0],
        new_kv[:, 0],
        suffix_kv[0],
        dt_gain.reshape(1, DT_RANK),
        dt_bias.reshape(1, CH),
        state_rates,
        skip_gain.reshape(1, CH),
        ssm_state.reshape(REQ * DS, CH),
        xproj_weight.T,
        dtproj_weight,
        kv_pool,
    ]
    held = [V(a.shape, a.dtype) for a in operands]
    held[2] = pltpu.SMEM((REQ,), i32)
    outs = (
        jax.ShapeDtypeStruct((2, 1, REQ, CH), bf16),
        jax.ShapeDtypeStruct((2, 1, REQ, GROUP * HD), bf16),
    )
    results = pl.pallas_call(
        kernel,
        out_shape=outs,
        in_specs=[hb] * len(operands),
        out_specs=(hb, hb),
        scratch_shapes=held
        + [
            V(outs[0].shape, bf16),
            V(outs[1].shape, bf16),
            V((NB, 96, 128), bf16),
            V((NB, 96, 128), bf16),
            V((NB, 16, 128), bf16),
            V((NB, 16, 128), bf16),
            V((NB, 64, HD), bf16),
            V((nt, 16, PROJ_PAD), bf16),
            V((NB, 16, PROJ_PAD), bf16),
            V((NB, 80, 128), bf16),
            V((NB, 80, 128), bf16),
            V((NB, 64, HD), bf16),
            V((NB, 64, HD), bf16),
            V((NB, REQ, 128), f32),
            V((32, 128), i32),
            pltpu.SMEM((32, 128), i32),
            V((NBLK, BLK * PAGE), f32),
            V((REQ, 128, HD), bf16),
            V((NBLK + 1, 128, 2 * HD), f32),
            V((NBLK + 1, 128, HD), f32),
            V((NB, 64, HD), f32),
            V((DS, NB * 2, CH), f32),
            V((DS, REQ, CH), f32),
            V((DS, REQ, CH), f32),
            V((NB, REQ, CH), f32),
            V((NB, REQ, CH), f32),
            V((NB, REQ, 128), f32),
            V((128, REQ * 128), f32),
            dma((len(operands),)),
            dma,
            dma((8,)),
            dma((8,)),
        ],
        compiler_params=pltpu.CompilerParams(
            collective_id=0, has_side_effects=True, vmem_limit_bytes=63 * 2**20
        ),
        name="decode",
    )(*operands)
    return pl.pallas_call(
        publish,
        out_shape=outs,
        in_specs=[hb, hb],
        out_specs=(hb, hb),
        scratch_shapes=[V(outs[0].shape, bf16), V(outs[1].shape, bf16), dma((2,))],
        compiler_params=pltpu.CompilerParams(vmem_limit_bytes=63 * 2**20),
        name="publish",
    )(*results)


def solution(mesh):
    in_specs = (
        P("beam", None, None, "tensor"),
        P("beam", None, None, "tensor"),
        P("beam", None, None, "tensor"),
        P(None, "beam", None, "tensor"),
        P(None, "beam", None, "tensor"),
        P(None, "tensor"),
        P("tensor"),
        P("tensor", None),
        P(),
        P(None, "tensor"),
        P("tensor"),
        P(None, "tensor"),
        P("tensor"),
        P(None, "beam", None, "tensor"),
        P(None, "beam", None, "tensor"),
        P("beam", None, "tensor"),
        P(),
        P(),
        P(),
    )
    out_specs = (P(None, "beam", None, "tensor"), P(None, "beam", None, "tensor"))
    return jax.shard_map(local, mesh=mesh, in_specs=in_specs, out_specs=out_specs, check_vma=False)
```

```python
import jax
import jax.numpy as jnp
from jax import lax
from jax.experimental import pallas as pl
from jax.experimental.pallas import tpu as pltpu
from jax.sharding import PartitionSpec as P

NB = 16
REQ = 8
DS = 16
DT_RANK = 256
HD = 128
PAGE = 16
MAXP = 512
CH = 1024
LT = CH // 128
GROUP = 4
PAGES = 256
BLK = 16
NBLK = PAGES // BLK + REQ
UNROLL = 8
POOL = 4096
PROJ = DT_RANK + 2 * DS
PROJ_PAD = 384
LOG2E = 1.4426950408889634
NEG = -1e30

f32 = jnp.float32
bf16 = jnp.bfloat16
i32 = jnp.int32
MESH = pl.DeviceIdType.MESH


def iota(shape, dim):
    return lax.broadcasted_iota(i32, shape, dim)


def dot(a, b):
    return lax.dot_general(a, b, (((1,), (0,)), ((), ())), preferred_element_type=f32)


def dot_nt(a, b):
    return lax.dot_general(a, b, (((1,), (1,)), ((), ())), preferred_element_type=f32)


def one(mask):
    return jnp.where(mask, 1.0, 0.0).astype(bf16)


def onef(mask):
    return jnp.where(mask, 1.0, 0.0).astype(f32)


def to_rows(x):
    return jnp.concatenate([x[:, i * 128 : (i + 1) * 128] for i in range(LT)], axis=0)


def from_rows(x):
    return jnp.concatenate([x[i * REQ : (i + 1) * REQ] for i in range(LT)], axis=1)


def silu(v):
    return v / (1.0 + jnp.exp(-v))


def softplus(v):
    return jnp.maximum(v, 0.0) + jnp.log(1.0 + jnp.exp(-jnp.abs(v)))


def slot_key(par, me):
    chosen = par == me
    upper = one(iota((REQ, REQ), 0) < iota((REQ, REQ), 1))
    rank = dot(one(chosen), upper)
    return jnp.where(chosen, rank, -1.0)


def pack_matrix(key):
    rows, cols = NB * LT * 2, LT * REQ
    rb = one((iota((rows, NB), 0) >> 4) == iota((rows, NB), 1))
    cr = one((iota((REQ, cols), 1) & 7) == iota((REQ, cols), 0))
    spread = dot(dot(rb, key.astype(bf16)).astype(bf16), cr)
    row, col = iota((rows, cols), 0), iota((rows, cols), 1)
    return one((spread == (row & 1).astype(f32)) & (((row >> 1) & 7) == (col >> 3)))


def own_column(par, me):
    row = jnp.sum(jnp.where(iota((NB, REQ), 0) == me, par.astype(f32), 0.0), axis=0, keepdims=True)
    eye = iota((REQ, REQ), 0) == iota((REQ, REQ), 1)
    col = jnp.sum(jnp.where(eye, row, 0.0), axis=1, keepdims=True)
    return row, col


def unpack_matrix(par, me):
    row, col = own_column(par, me)
    alike = (row == col) & (iota((REQ, REQ), 1) < iota((REQ, REQ), 0))
    order = jnp.sum(onef(alike), axis=1, keepdims=True)
    code = jnp.concatenate([col * 2.0 + order] * LT, axis=0)
    rows, cols = LT * REQ, NB * LT * 2
    r, c = iota((rows, cols), 0), iota((rows, cols), 1)
    code_of = ((c >> 4) * 2 + (c & 1)).astype(f32)
    return one((code == code_of) & ((r >> 3) == ((c >> 1) & 7)))


def column128(m):
    spread = dot(one((iota((128, NB), 0) >> 3) == iota((128, NB), 1)), m.astype(bf16))
    pick = iota((128, REQ), 1) == (iota((128, REQ), 0) & 7)
    return jnp.sum(jnp.where(pick, spread, 0.0), axis=1, keepdims=True)


def kernel(
    par_h, po_h, ctx_h, cs_h, cw_h, cb_h, x_h, gate_h, q_h, nkv_h, suf_h, gain_h, dtb_h, rates_h, skip_h,
    s_h, xw_h, dtw_h, kv_h,
    mo_h, ao_h,
    par_ref, po_ref, ctx_ref, cs_ref, cw_ref, cb_ref, x_ref, gate_ref, q_ref, nkv_ref, suf_ref, gain_ref, dtb_ref,
    rates_ref, skip_ref, s_v, xw_v, dtw_v, kv_v,
    mo_ref, ao_ref,
    h1s, h1r, hcs, hcr, qa, zb, prb, zzs, zzr, os_, or_, lse,
    tab, tabs, bias, qr, orun, mrun, osf, s0, s1, rt, d1, d0g, c1, okm,
    lsem, tsem, ssem, rsem,
):
    me = lax.axis_index("beam")
    mt = lax.axis_index("tensor")
    nt = zb.shape[0]
    H1, QA, ZB, PR, OO, LS, ZZ, HC = range(8)

    def remote(src, dst, k, device):
        return pltpu.make_async_remote_copy(
            src_ref=src, dst_ref=dst, send_sem=ssem.at[k], recv_sem=rsem.at[k], device_id=device,
            device_id_type=MESH,
        )

    beam_peers = [((me + d) & (NB - 1), mt) for d in range(1, NB)]
    tensor_peers = [(me, (mt + d) & (nt - 1)) for d in range(1, nt)]

    def exchange(src, dst, k):
        for peer in beam_peers:
            remote(src.at[peer[0]], dst.at[me], k, peer).start()

    def gather(buf, k, at, peers):
        for peer in peers:
            remote(buf.at[at], buf.at[at], k, peer).start()

    def all_of(buf, k):
        part = buf.at[pl.ds(0, buf.shape[0] - 1)]
        return remote(part, part, k, (me, mt))

    def landed(buf, k):
        all_of(buf, k).wait_recv()

    def sent(buf, k):
        all_of(buf, k).wait_send()

    pairs = [
        (par_h, par_ref), (cs_h, cs_ref), (cw_h, cw_ref), (x_h, x_ref), (q_h, q_ref), (s_h, s_v),
        (rates_h, rates_ref), (cb_h, cb_ref), (po_h, po_ref), (ctx_h, ctx_ref), (xw_h, xw_v), (kv_h, kv_v),
        (suf_h, suf_ref), (nkv_h, nkv_ref), (dtw_h, dtw_v), (dtb_h, dtb_ref), (gain_h, gain_ref),
        (skip_h, skip_ref), (gate_h, gate_ref),
    ]
    copies = [pltpu.make_async_copy(a, b, lsem.at[i]) for i, (a, b) in enumerate(pairs)]
    (c_par, c_cs, c_cw, c_x, c_q, c_s, c_rates, c_cb, c_po, c_ctx, c_xw, c_kv, c_suf, c_nkv, c_dtw, c_dtb, c_gain,
     c_skip, c_gate) = copies
    for c in copies[0:5]:
        c.start()
    barrier = pltpu.get_barrier_semaphore()
    greeted = beam_peers + tensor_peers
    for peer in greeted:
        pl.semaphore_signal(barrier, inc=1, device_id=peer, device_id_type=MESH)
    for c in copies[5:]:
        c.start()

    c_par.wait()
    par_t = par_ref[...].astype(f32).astype(bf16)
    eye16 = one(iota((NB, NB), 0) == iota((NB, NB), 1))
    p0 = dot_nt(eye16, par_t[0:REQ]).astype(i32)
    p1 = dot_nt(eye16, par_t[REQ : 2 * REQ]).astype(i32)
    key0 = slot_key(p0, me)
    c_cs.wait()
    c_cw.wait()
    cw = cw_ref[...].astype(f32)
    cw_row = [cw[k : k + 1] for k in range(4)]
    win = [cs_ref[k].astype(f32) for k in range(3)]
    a0 = win[0] * cw_row[0] + win[1] * cw_row[1] + win[2] * cw_row[2]
    a1 = win[1] * cw_row[0] + win[2] * cw_row[1]
    h1s[:, 0:64, :] = jnp.broadcast_to(to_rows(a1).astype(bf16)[None], (NB, 64, 128))
    h1s[:, 64:80, :] = dot(pack_matrix(key0), to_rows(a0).astype(bf16)).astype(bf16).reshape(NB, 16, 128)
    key1 = slot_key(p1, me)
    pb1 = pack_matrix(key1)
    c_x.wait()
    x0 = x_ref[0].astype(f32)
    x1 = x_ref[1].astype(f32)
    h1s[:, 80:96, :] = dot(pb1, to_rows(x0).astype(bf16)).astype(bf16).reshape(NB, 16, 128)
    h1r[pl.ds(me, 1)] = h1s[pl.ds(me, 1)]

    c_q.wait()
    qrows = jnp.concatenate(
        [q_ref[s][:, h * 128 : (h + 1) * 128].astype(f32) for s in range(2) for h in range(GROUP)], axis=0
    ).astype(bf16)
    ri, ci = iota((64, 64), 0), iota((64, 64), 1)
    swap = one(((ri >> 3) == (ci & 7)) & ((ri & 7) == (ci >> 3)))
    qa[pl.ds(me, 1)] = dot(swap, qrows).astype(bf16)[None]

    pl.semaphore_wait(barrier, len(greeted))

    exchange(h1s, h1r, H1)
    gather(qa, QA, me, beam_peers)

    ub0 = unpack_matrix(p0, me)
    ub1 = unpack_matrix(p1, me)
    g = jnp.zeros((NB, REQ), i32)
    for p in range(NB):
        g = g + jnp.where(p1 == p, p0[p : p + 1, :], 0)
    _, g_own = own_column(g, me)
    g64 = jnp.concatenate([g_own] * LT, axis=0)
    ai, aj = iota((64, NB * 64), 0), iota((64, NB * 64), 1)
    ug = one((g64 == (aj >> 6).astype(f32)) & (ai == (aj & 63)))
    c_cb.wait()
    cb8 = cb_ref[...].astype(f32)
    cb = jnp.concatenate([cb8[i : i + 1] for i in range(LT)], axis=1)

    c_po.wait()
    c_ctx.wait()
    ctx_col = jnp.zeros((REQ, MAXP), i32)
    for r in range(REQ):
        ctx_col = jnp.where(iota((REQ, MAXP), 0) == r, ctx_ref[r], ctx_col)
    nvis = jnp.clip(ctx_col - iota((REQ, MAXP), 1) * PAGE, 0, PAGE)
    po = jnp.concatenate([po_ref[pl.ds(j, REQ, stride=4), :] for j in range(4)], axis=1)
    loc = po - me * PAGES
    flag = (loc >= 0) & (loc < PAGES) & (nvis > 0)
    tri = one(iota((MAXP, MAXP), 0) < iota((MAXP, MAXP), 1))
    rank = dot(one(flag), tri).astype(i32)
    count = jnp.sum(onef(flag), axis=1, keepdims=True).astype(i32)
    nblk = ((count + (BLK - 1)) >> 4).astype(f32)
    eye8 = iota((REQ, REQ), 0) == iota((REQ, REQ), 1)
    nblk_row = jnp.sum(jnp.where(eye8, nblk, 0.0), axis=0, keepdims=True)
    sblk = jnp.sum(
        jnp.where(iota((REQ, REQ), 1) < iota((REQ, REQ), 0), nblk_row, 0.0), axis=1, keepdims=True
    )
    dest = jnp.where(flag, sblk.astype(i32) * BLK + rank, -1)
    hi = dest >> 4
    lo = jnp.where(flag, dest & 15, -1)
    table = jnp.zeros((NBLK, 32), f32)
    for r in range(REQ):
        hot = one(hi[r : r + 1] == iota((NBLK, MAXP), 0))
        low = lo[r : r + 1] == iota((16, MAXP), 0)
        vals = jnp.concatenate(
            [
                jnp.where(low, loc[r : r + 1].astype(f32), 0.0),
                jnp.where(low, nvis[r : r + 1].astype(f32), 0.0),
            ],
            axis=0,
        ).astype(bf16)
        table = table + dot_nt(hot, vals)
    tab[...] = jnp.zeros_like(tab)
    tab[0:NBLK, 0:32] = table.astype(i32)
    lane = iota((REQ, 128), 1)
    subl = iota((REQ, 128), 0)
    sb_i, nb_i = sblk.astype(i32), nblk.astype(i32)
    inside = (sb_i <= lane) & (lane < sb_i + nb_i)
    tab[NBLK : NBLK + 1, :] = jnp.sum(jnp.where(inside, subl, 0).astype(f32), axis=0, keepdims=True).astype(i32)
    tab[NBLK + 1 : NBLK + 2, :] = jnp.sum(
        onef((lane == sb_i) & (nb_i > 0)), axis=0, keepdims=True
    ).astype(i32)
    tab[NBLK + 2 : NBLK + 3, :] = jnp.sum(
        jnp.where((lane == subl) & (nb_i > 0), sb_i + nb_i, 0).astype(f32), axis=0, keepdims=True
    ).astype(i32)
    cp_tab = pltpu.make_async_copy(tab, tabs, tsem)
    cp_tab.start()
    spread = one((iota((16, BLK * PAGE), 1) >> 4) == iota((16, BLK * PAGE), 0))
    seen = dot(table[:, 16:32].astype(bf16), spread)
    bias[...] = jnp.where((iota((NBLK, BLK * PAGE), 1) & 15).astype(f32) < seen, 0.0, NEG)
    orun[0] = jnp.zeros((128, 2 * HD), f32)
    mrun[0] = jnp.full((128, HD), NEG, f32)
    cp_tab.wait()

    wide = one((iota((REQ, REQ * 128), 1) >> 7) == iota((REQ, REQ * 128), 0))
    x_s0 = dot(one(p0 == me), wide)
    x_sg = dot(one(g == me), wide)
    x_s1 = dot(one(p1 == me), wide)
    tok = iota((NB, REQ * 128), 1) & 127
    mine = onef(iota((NB, REQ * 128), 0) == me)
    ok0 = jnp.where(tok < 16, x_s0, jnp.where(tok == 16, mine, 0.0))
    ok1 = jnp.where(tok < 16, x_sg, jnp.where(tok == 16, x_s1, jnp.where(tok == 17, mine, 0.0)))
    qi, qj = iota((128, 2 * NB), 0), iota((128, 2 * NB), 1)
    pick = one((((qi >> 2) & 1) == (qj >> 4)) & ((qi >> 3) == (qj & 15)))
    okm[...] = dot(pick, jnp.concatenate([ok0, ok1], axis=0).astype(bf16))

    c_rates.wait()
    for n in range(DS):
        rt[n] = jnp.broadcast_to(rates_ref[n : n + 1, :] * (-LOG2E), (REQ, CH))
    c_s.wait()
    row, col = iota((DS * NB * 2, 128), 0), iota((DS * NB * 2, 128), 1)
    rs_ = one(((iota((DS * NB * 2, NB), 0) >> 1) & 15) == iota((DS * NB * 2, NB), 1))
    crn = one((iota((REQ, 128), 1) >> 4) == iota((REQ, 128), 0))
    keys = dot(rs_, dot(key0.astype(bf16), crn).astype(bf16))
    sel0 = one((keys == (row & 1).astype(f32)) & ((row >> 5) == (col & 15)))
    pi, pj = iota((128, 128), 0), iota((128, 128), 1)
    perm1 = one(((pi & 7) == (pj >> 4)) & ((pi >> 3) == (pj & 15)))
    for j in range(4):
        sl = slice(j * 256, (j + 1) * 256)
        sj = s_v[:, sl].astype(bf16)
        s0[:, :, sl] = dot(sel0, sj).reshape(DS, NB * 2, 256)
        s1[:, :, sl] = dot(perm1, sj).reshape(DS, REQ, 256)
    held_here = column128(onef(g == me))
    g1 = one((column128(p1) == (pj >> 3).astype(f32)) & ((pi & 7) == (pj & 7)))
    r32 = one((iota((32, NB), 0) >> 1) == iota((32, NB), 1))
    c32 = one((iota((REQ, 128), 1) & 7) == iota((REQ, 128), 0))
    key32 = dot(dot(r32, key0.astype(bf16)).astype(bf16), c32)
    si, sj_ = iota((32, 128), 0), iota((32, 128), 1)
    psl = one((key32 == (si & 1).astype(f32)) & ((si >> 1) == (sj_ >> 3)))
    ui, uj = iota((256, 256), 0), iota((256, 256), 1)
    relay = one(((ui >> 4) == ((uj >> 1) & 15)) & (((ui >> 1) & 7) == (uj >> 5)) & ((ui & 1) == (uj & 1)))
    _, own1 = own_column(p1, me)
    gi, gj = iota((REQ, 128), 0), iota((REQ, 128), 1)
    og = one((own1 == (gj >> 3).astype(f32)) & (gi == (gj & 7)))

    c_xw.wait()
    landed(h1r, H1)
    conv0 = silu(from_rows(dot(ub0, h1r[:, 64:80, :].reshape(NB * 16, 128))) + cw_row[3] * x0 + cb)
    older = from_rows(dot(ug, h1r[:, 0:64, :].reshape(NB * 64, 128)))
    newer = from_rows(dot(ub1, h1r[:, 80:96, :].reshape(NB * 16, 128)))
    conv1 = silu(older + cw_row[2] * newer + cw_row[3] * x1 + cb)
    part = dot_nt(jnp.concatenate([conv0, conv1], axis=0).astype(bf16), xw_v[...])
    zb[pl.ds(mt, 1)] = jnp.zeros((1, 16, PROJ_PAD), bf16)
    zb[pl.ds(mt, 1), :, 0:PROJ] = part.astype(bf16)[None]
    gather(zb, ZB, mt, tensor_peers)
    hcs[...] = dot(pb1, to_rows(conv0).astype(bf16)).astype(bf16).reshape(NB, 16, 128)
    hcr[pl.ds(me, 1)] = hcs[pl.ds(me, 1)]
    exchange(hcs, hcr, HC)


    landed(qa, QA)
    qf = qa[...].astype(f32)
    for r in range(REQ):
        qr[r] = jnp.concatenate([qf[b, r * 8 : (r + 1) * 8] for b in range(NB)], axis=0).astype(bf16)
    c_kv.wait()
    scale = HD**-0.5 * LOG2E
    ones_blk = jnp.ones((BLK * PAGE, HD), bf16)

    def blocks(step, c):
        first = step * UNROLL
        m_old, o_old = mrun[first], orun[first]
        for u in range(UNROLL):
            i = first + u
            kv = jnp.concatenate([kv_v[tabs[i, k] & (PAGES - 1)] for k in range(BLK)], axis=0)
            s = dot_nt(qr[tabs[NBLK, i] & (REQ - 1)], kv[:, 0:HD]) * scale + bias[pl.ds(i, 1), :]
            m_old = jnp.where(tabs[NBLK + 1, i] > 0, NEG, m_old)
            m_new = jnp.maximum(m_old, jnp.max(s, axis=1, keepdims=True))
            e = jnp.exp2(s - jnp.concatenate([m_new, m_new], axis=1)).astype(bf16)
            v = jnp.concatenate([kv[:, HD : 2 * HD], ones_blk], axis=1)
            fade = jnp.exp2(m_old - m_new)
            o_old = o_old * jnp.concatenate([fade, fade], axis=1) + dot(e, v)
            m_old = m_new
            orun[i + 1] = o_old
            mrun[i + 1] = m_old
        return c

    steps = NBLK // UNROLL
    lax.fori_loop(0, 2, blocks, 0)

    landed(zb, ZB)
    proj = jnp.zeros((16, PROJ_PAD), f32)
    for t in range(nt):
        proj = proj + zb[t].astype(f32)
    prb[pl.ds(me, 1)] = proj.astype(bf16)[None]
    gather(prb, PR, me, beam_peers)

    lax.fori_loop(2, steps, blocks, 0)
    c_suf.wait()
    c_nkv.wait()
    nk0 = nkv_ref[0].astype(f32)
    nk1 = nkv_ref[1].astype(f32)
    diag = iota((128, 128), 0) == iota((128, 128), 1)
    ti = iota((16, 256), 0)
    for r in range(REQ):
        tail = jnp.where(ti == 0, nk0[r : r + 1], jnp.where(ti == 1, nk1[r : r + 1], 0.0)).astype(bf16)
        kv = jnp.concatenate([suf_ref[r], tail], axis=0)
        s = jnp.where(
            okm[:, r * 128 : r * 128 + 32] > 0.5, dot_nt(qr[r], kv[:, 0:HD]) * scale, NEG
        )
        last = jnp.clip(tabs[NBLK + 2, r], 0, NBLK)
        m_old = mrun[last]
        m_new = jnp.maximum(m_old, jnp.max(s, axis=1, keepdims=True))
        e = jnp.exp2(s - m_new[:, 0:32]).astype(bf16)
        v = jnp.concatenate([kv[:, HD : 2 * HD], jnp.ones((32, HD), bf16)], axis=1)
        fade = jnp.exp2(m_old - m_new)
        o = orun[last] * jnp.concatenate([fade, fade], axis=1) + dot(e, v)
        total = o[:, HD : 2 * HD]
        val = o[:, 0:HD] / total
        for b in range(NB):
            osf[b, r * 8 : (r + 1) * 8, :] = val[b * 8 : (b + 1) * 8]
        lg = m_new + jnp.log2(total)
        lse[pl.ds(me, 1), r : r + 1, :] = jnp.sum(jnp.where(diag, lg, 0.0), axis=0, keepdims=True)[None]
    os_[...] = osf[...].astype(bf16)
    or_[pl.ds(me, 1)] = os_[pl.ds(me, 1)]
    exchange(os_, or_, OO)
    gather(lse, LS, me, beam_peers)

    for c in (c_dtw, c_dtb, c_gain, c_skip, c_gate):
        c.wait()
    gain = gain_ref[...]

    def normed(rank_rows):
        mean = jnp.sum(rank_rows * rank_rows, axis=1, keepdims=True) * (1.0 / DT_RANK)
        return (rank_rows * lax.rsqrt(mean + 1e-6) * gain).astype(bf16)

    dtb = dtb_ref[...]
    landed(prb, PR)
    prf = prb[...].astype(f32)
    pr0 = prf[:, 0:REQ, :].reshape(128, PROJ_PAD)
    pr1 = prf[:, REQ : 2 * REQ, :].reshape(128, PROJ_PAD)
    rn0 = normed(pr0[:, 0:DT_RANK])
    rn1 = normed(pr1[:, 0:DT_RANK])
    bc0 = pr0[:, DT_RANK:PROJ].astype(bf16)
    c1[...] = (pr1[:, DT_RANK:PROJ_PAD] * held_here).reshape(NB, REQ, 128)
    rn0g = dot(g1, rn0).astype(bf16)

    rn0s = dot(psl, rn0).astype(bf16)
    c0s = dot(psl, bc0)
    c0b = [jnp.broadcast_to(c0s[:, DS + n : DS + n + 1], (NB * 2, 128)) for n in range(DS)]
    z0 = []
    for j in range(4):
        sl = slice(j * 256, (j + 1) * 256)
        w = dtw_v[:, sl]
        part1 = softplus(dot(rn1, w) + dtb[:, sl])
        part0 = softplus(dot(rn0g, w) + dtb[:, sl])
        d0g[:, :, sl] = part0.reshape(NB, REQ, 256)
        d1[:, :, sl] = (part0 + part1).reshape(NB, REQ, 256)
        dj = softplus(dot(rn0s, w) + dtb[:, sl])
        acc = jnp.zeros((32, 256), f32)
        for n in range(DS):
            cn = jnp.concatenate([c0b[n], c0b[n]], axis=1)
            acc = acc + cn * (jnp.exp2(dj * (rates_ref[n : n + 1, sl] * (-LOG2E))) * s0[n, :, sl])
        z0 += [acc[:, 0:128], acc[:, 128:256]]
    z0 = jnp.concatenate(z0, axis=0).astype(bf16)
    zzs[:, 64:80, :] = dot(relay, z0).astype(bf16).reshape(NB, 16, 128)

    def children(i, c):
        two = [(me + 1 + 2 * i) & (NB - 1), (me + 2 + 2 * i) & (NB - 1)]
        outs = [c1[b] for b in two]
        deltas = [d1[b] for b in two]
        accs = [jnp.zeros((REQ, CH), f32) for _ in two]
        for n in range(DS):
            rn, sn = rt[n], s1[n]
            for k in range(2):
                accs[k] = accs[k] + outs[k][:, DS + n : DS + n + 1] * (jnp.exp2(deltas[k] * rn) * sn)
        for k in range(2):
            zzs[two[k], 0:64, :] = to_rows(accs[k]).astype(bf16)
        remote(zzs.at[two[0]], zzr.at[me], ZZ, (two[0], mt)).start()

        @pl.when(i < NB // 2 - 1)
        def _():
            remote(zzs.at[two[1]], zzr.at[me], ZZ, (two[1], mt)).start()

        return c

    lax.fori_loop(0, NB // 2, children, 0)
    zzr[pl.ds(me, 1)] = zzs[pl.ds(me, 1)]

    own = proj.astype(bf16).astype(f32)
    d_own = softplus(dot(normed(own[:, 0:DT_RANK]), dtw_v[...]) + dtb)
    d_own0, d_own1 = d_own[0:REQ], d_own[REQ : 2 * REQ]
    own_in = own[:, DT_RANK : DT_RANK + DS]
    own_out = own[:, DT_RANK + DS : DT_RANK + 2 * DS]
    cb_own = jnp.sum(own_in * own_out, axis=1, keepdims=True)
    skip = skip_ref[...]
    base0 = d_own0 * conv0 * cb_own[0:REQ] + skip * conv0
    base1 = d_own1 * conv1 * cb_own[REQ : 2 * REQ] + skip * conv1
    gate0 = silu(gate_ref[0].astype(f32))
    gate1 = silu(gate_ref[1].astype(f32))

    landed(hcr, HC)
    conv0p = from_rows(dot(ub1, hcr[...].reshape(NB * 16, 128)))
    in0p = dot(og, bc0)[:, 0:DS]
    cross = in0p * own_out[REQ : 2 * REQ]
    mixed = jnp.zeros((REQ, CH), f32)
    for n in range(DS):
        mixed = mixed + cross[:, n : n + 1] * jnp.exp2(d_own1 * rt[n])
    base1 = base1 + mixed * (d0g[pl.ds(me, 1)][0] * conv0p)

    landed(or_, OO)
    landed(lse, LS)
    lanes = iota((8, 128), 1)
    want = lanes == me * 8 + iota((8, 128), 0)
    parts = []
    for p in range(NB):
        lp = lse[p]
        parts.append(
            jnp.concatenate(
                [
                    jnp.sum(jnp.where(want, lp[r : r + 1], 0.0), axis=1, keepdims=True)
                    for r in range(REQ)
                ],
                axis=0,
            )
        )
    top = parts[0]
    for p in range(1, NB):
        top = jnp.maximum(top, parts[p])
    den = jnp.zeros((64, 1), f32)
    num = jnp.zeros((64, HD), f32)
    for p in range(NB):
        w = jnp.exp2(parts[p] - top)
        den = den + w
        num = num + w * or_[p].astype(f32)
    att = dot(swap, (num / den).astype(bf16))
    for s in range(2):
        ao_ref[s, 0] = jnp.concatenate(
            [att[(s * GROUP + h) * 8 : (s * GROUP + h + 1) * 8] for h in range(GROUP)], axis=1
        ).astype(bf16)
    out_a = pltpu.make_async_copy(ao_ref, ao_h, tsem)
    out_a.start()

    landed(zzr, ZZ)
    z1 = jnp.zeros((64, 128), f32)
    for p in range(NB):
        z1 = z1 + zzr[p, 0:64, :].astype(f32)
    z0 = dot(ub0, zzr[:, 64:80, :].reshape(256, 128))
    mo_ref[0, 0] = ((from_rows(z0) + base0) * gate0).astype(bf16)
    mo_ref[1, 0] = ((from_rows(z1) + base1) * gate1).astype(bf16)
    out_m = pltpu.make_async_copy(mo_ref, mo_h, lsem.at[0])
    out_m.start()

    sent(h1s, H1)
    sent(hcs, HC)
    sent(qa, QA)
    sent(zb, ZB)
    sent(prb, PR)
    sent(os_, OO)
    sent(lse, LS)
    sent(zzs, ZZ)
    out_a.wait()
    out_m.wait()


def publish(m_ref, a_ref, mo_ref, ao_ref, m_v, a_v, sem):
    first = pltpu.make_async_copy(m_ref, m_v, sem.at[0])
    second = pltpu.make_async_copy(a_ref, a_v, sem.at[1])
    first.start()
    second.start()
    first.wait()
    first = pltpu.make_async_copy(m_v, mo_ref, sem.at[0])
    first.start()
    second.wait()
    second = pltpu.make_async_copy(a_v, ao_ref, sem.at[1])
    second.start()
    first.wait()
    second.wait()


def local(
    ssm_state,
    conv_state,
    suffix_kv,
    mamba_x,
    mamba_gate,
    conv_weight,
    conv_bias,
    xproj_weight,
    dt_gain,
    dtproj_weight,
    dt_bias,
    state_rates,
    skip_gain,
    queries,
    new_kv,
    kv_pool,
    page_order,
    ctx_len,
    parents,
):
    nt = lax.axis_size("tensor")
    hb = pl.BlockSpec(memory_space=pltpu.HBM)
    dma = pltpu.SemaphoreType.DMA
    V = pltpu.VMEM
    operands = [
        parents.transpose(0, 2, 1, 3).reshape(2 * REQ, NB),
        page_order.reshape(POOL // 128, 128),
        ctx_len,
        conv_state.transpose(0, 2, 1, 3)[0],
        conv_weight,
        conv_bias.reshape(LT, 128),
        mamba_x[:, 0],
        mamba_gate[:, 0],
        queries[:, 0],
        new_kv[:, 0],
        suffix_kv[0],
        dt_gain.reshape(1, DT_RANK),
        dt_bias.reshape(1, CH),
        state_rates,
        skip_gain.reshape(1, CH),
        ssm_state.reshape(REQ * DS, CH),
        xproj_weight.T,
        dtproj_weight,
        kv_pool,
    ]
    held = [V(a.shape, a.dtype) for a in operands]
    held[2] = pltpu.SMEM((REQ,), i32)
    outs = (
        jax.ShapeDtypeStruct((2, 1, REQ, CH), bf16),
        jax.ShapeDtypeStruct((2, 1, REQ, GROUP * HD), bf16),
    )
    results = pl.pallas_call(
        kernel,
        out_shape=outs,
        in_specs=[hb] * len(operands),
        out_specs=(hb, hb),
        scratch_shapes=held
        + [
            V(outs[0].shape, bf16),
            V(outs[1].shape, bf16),
            V((NB, 96, 128), bf16),
            V((NB, 96, 128), bf16),
            V((NB, 16, 128), bf16),
            V((NB, 16, 128), bf16),
            V((NB, 64, HD), bf16),
            V((nt, 16, PROJ_PAD), bf16),
            V((NB, 16, PROJ_PAD), bf16),
            V((NB, 80, 128), bf16),
            V((NB, 80, 128), bf16),
            V((NB, 64, HD), bf16),
            V((NB, 64, HD), bf16),
            V((NB, REQ, 128), f32),
            V((32, 128), i32),
            pltpu.SMEM((32, 128), i32),
            V((NBLK, BLK * PAGE), f32),
            V((REQ, 128, HD), bf16),
            V((NBLK + 1, 128, 2 * HD), f32),
            V((NBLK + 1, 128, HD), f32),
            V((NB, 64, HD), f32),
            V((DS, NB * 2, CH), f32),
            V((DS, REQ, CH), f32),
            V((DS, REQ, CH), f32),
            V((NB, REQ, CH), f32),
            V((NB, REQ, CH), f32),
            V((NB, REQ, 128), f32),
            V((128, REQ * 128), f32),
            dma((len(operands),)),
            dma,
            dma((8,)),
            dma((8,)),
        ],
        compiler_params=pltpu.CompilerParams(
            collective_id=0, has_side_effects=True, vmem_limit_bytes=63 * 2**20
        ),
        name="decode",
    )(*operands)
    return pl.pallas_call(
        publish,
        out_shape=outs,
        in_specs=[hb, hb],
        out_specs=(hb, hb),
        scratch_shapes=[V(outs[0].shape, bf16), V(outs[1].shape, bf16), dma((2,))],
        compiler_params=pltpu.CompilerParams(vmem_limit_bytes=63 * 2**20),
        name="publish",
    )(*results)


def solution(mesh):
    in_specs = (
        P("beam", None, None, "tensor"),
        P("beam", None, None, "tensor"),
        P("beam", None, None, "tensor"),
        P(None, "beam", None, "tensor"),
        P(None, "beam", None, "tensor"),
        P(None, "tensor"),
        P("tensor"),
        P("tensor", None),
        P(),
        P(None, "tensor"),
        P("tensor"),
        P(None, "tensor"),
        P("tensor"),
        P(None, "beam", None, "tensor"),
        P(None, "beam", None, "tensor"),
        P("beam", None, "tensor"),
        P(),
        P(),
        P(),
    )
    out_specs = (P(None, "beam", None, "tensor"), P(None, "beam", None, "tensor"))
    return jax.shard_map(local, mesh=mesh, in_specs=in_specs, out_specs=out_specs, check_vma=False)
```

```python
import jax
import jax.numpy as jnp
from jax import lax
from jax.experimental import pallas as pl
from jax.experimental.pallas import tpu as pltpu
from jax.sharding import PartitionSpec as P

NB = 16
REQ = 8
DS = 16
DT_RANK = 256
HD = 128
PAGE = 16
MAXP = 512
CH = 1024
LT = CH // 128
GROUP = 4
PAGES = 256
BLK = 16
NBLK = PAGES // BLK + REQ
UNROLL = 8
BEAM_ORDER = (
    (2, 2), (2, 1), (1, 2), (2, -1), (-1, 2), (2, 0), (0, 2), (1, 1), (-1, -1), (1, -1), (-1, 1), (0, 1), (1, 0),
    (0, -1), (-1, 0),
)
POOL = 4096
PROJ = DT_RANK + 2 * DS
PROJ_PAD = 384
LOG2E = 1.4426950408889634
NEG = -1e30

f32 = jnp.float32
bf16 = jnp.bfloat16
i32 = jnp.int32
MESH = pl.DeviceIdType.MESH


def iota(shape, dim):
    return lax.broadcasted_iota(i32, shape, dim)


def dot(a, b):
    return lax.dot_general(a, b, (((1,), (0,)), ((), ())), preferred_element_type=f32)


def dot_nt(a, b):
    return lax.dot_general(a, b, (((1,), (1,)), ((), ())), preferred_element_type=f32)


def one(mask):
    return jnp.where(mask, 1.0, 0.0).astype(bf16)


def onef(mask):
    return jnp.where(mask, 1.0, 0.0).astype(f32)


def to_rows(x):
    return jnp.concatenate([x[:, i * 128 : (i + 1) * 128] for i in range(LT)], axis=0)


def from_rows(x):
    return jnp.concatenate([x[i * REQ : (i + 1) * REQ] for i in range(LT)], axis=1)


def silu(v):
    return v / (1.0 + jnp.exp(-v))


def softplus(v):
    return jnp.maximum(v, 0.0) + jnp.log(1.0 + jnp.exp(-jnp.abs(v)))


def slot_key(par, me):
    chosen = par == me
    upper = one(iota((REQ, REQ), 0) < iota((REQ, REQ), 1))
    rank = dot(one(chosen), upper)
    return jnp.where(chosen, rank, -1.0)


def pack_matrix(key):
    rows, cols = NB * LT * 2, LT * REQ
    rb = one((iota((rows, NB), 0) >> 4) == iota((rows, NB), 1))
    cr = one((iota((REQ, cols), 1) & 7) == iota((REQ, cols), 0))
    spread = dot(dot(rb, key.astype(bf16)).astype(bf16), cr)
    row, col = iota((rows, cols), 0), iota((rows, cols), 1)
    return one((spread == (row & 1).astype(f32)) & (((row >> 1) & 7) == (col >> 3)))


def own_column(par, me):
    row = jnp.sum(jnp.where(iota((NB, REQ), 0) == me, par.astype(f32), 0.0), axis=0, keepdims=True)
    eye = iota((REQ, REQ), 0) == iota((REQ, REQ), 1)
    col = jnp.sum(jnp.where(eye, row, 0.0), axis=1, keepdims=True)
    return row, col


def unpack_matrix(par, me):
    row, col = own_column(par, me)
    alike = (row == col) & (iota((REQ, REQ), 1) < iota((REQ, REQ), 0))
    order = jnp.sum(onef(alike), axis=1, keepdims=True)
    code = jnp.concatenate([col * 2.0 + order] * LT, axis=0)
    rows, cols = LT * REQ, NB * LT * 2
    r, c = iota((rows, cols), 0), iota((rows, cols), 1)
    code_of = ((c >> 4) * 2 + (c & 1)).astype(f32)
    return one((code == code_of) & ((r >> 3) == ((c >> 1) & 7)))


def column128(m):
    spread = dot(one((iota((128, NB), 0) >> 3) == iota((128, NB), 1)), m.astype(bf16))
    pick = iota((128, REQ), 1) == (iota((128, REQ), 0) & 7)
    return jnp.sum(jnp.where(pick, spread, 0.0), axis=1, keepdims=True)


def kernel(
    par_h, po_h, ctx_h, cs_h, cw_h, cb_h, x_h, gate_h, q_h, nkv_h, suf_h, gain_h, dtb_h, rates_h, skip_h,
    s_h, xw_h, dtw_h, kv_h,
    mo_h, ao_h,
    par_ref, po_ref, ctx_ref, cs_ref, cw_ref, cb_ref, x_ref, gate_ref, q_ref, nkv_ref, suf_ref, gain_ref, dtb_ref,
    rates_ref, skip_ref, s_v, xw_v, dtw_v, kv_v,
    mo_ref, ao_ref,
    h1s, h1r, hcs, hcr, qa, zb, prb, zzs, zzr, os_, or_, lse,
    tab, tabs, bias, qr, orun, mrun, osf, s0, s1, rt, d1, d0g, c1, okm,
    lsem, tsem, ssem, rsem,
):
    me = lax.axis_index("beam")
    mt = lax.axis_index("tensor")
    nt = zb.shape[0]
    H1, QA, ZB, PR, OO, LS, ZZ, HC = range(8)

    def remote(src, dst, k, device):
        return pltpu.make_async_remote_copy(
            src_ref=src, dst_ref=dst, send_sem=ssem.at[k], recv_sem=rsem.at[k], device_id=device,
            device_id_type=MESH,
        )

    core, mz, nz = mt & 1, mt >> 1, nt // 2
    mx, my = me >> 2, me & 3

    def beam_at(dx, dy):
        return ((mx + dx + core * (-dy - dx)) & 3) * 4 + ((my + dy + core * (-dx - dy)) & 3)

    def tensor_at(dz, other):
        return ((mz + dz * (1 - 2 * core)) & (nz - 1)) * 2 + ((core + other) & 1)

    beam_peers = [(beam_at(dx, dy), mt) for dx, dy in BEAM_ORDER]
    z_order = [k for far in range(nz // 2, 0, -1) for k in sorted({far % nz, -far % nz})]
    tensor_peers = [(me, tensor_at(dz, other)) for dz in z_order for other in (0, 1)] + [(me, tensor_at(0, 1))]

    def exchange(src, dst, k):
        for peer in beam_peers:
            remote(src.at[peer[0]], dst.at[me], k, peer).start()

    def gather(buf, k, at, peers):
        for peer in peers:
            remote(buf.at[at], buf.at[at], k, peer).start()

    def all_of(buf, k):
        part = buf.at[pl.ds(0, buf.shape[0] - 1)]
        return remote(part, part, k, (me, mt))

    def landed(buf, k):
        all_of(buf, k).wait_recv()

    def sent(buf, k):
        all_of(buf, k).wait_send()

    pairs = [
        (par_h, par_ref), (cs_h, cs_ref), (cw_h, cw_ref), (x_h, x_ref), (q_h, q_ref), (s_h, s_v),
        (rates_h, rates_ref), (cb_h, cb_ref), (po_h, po_ref), (ctx_h, ctx_ref), (xw_h, xw_v), (kv_h, kv_v),
        (suf_h, suf_ref), (nkv_h, nkv_ref), (dtw_h, dtw_v), (dtb_h, dtb_ref), (gain_h, gain_ref),
        (skip_h, skip_ref), (gate_h, gate_ref),
    ]
    copies = [pltpu.make_async_copy(a, b, lsem.at[i]) for i, (a, b) in enumerate(pairs)]
    (c_par, c_cs, c_cw, c_x, c_q, c_s, c_rates, c_cb, c_po, c_ctx, c_xw, c_kv, c_suf, c_nkv, c_dtw, c_dtb, c_gain,
     c_skip, c_gate) = copies
    for c in copies[0:5]:
        c.start()
    barrier = pltpu.get_barrier_semaphore()
    greeted = beam_peers + tensor_peers
    for peer in greeted:
        pl.semaphore_signal(barrier, inc=1, device_id=peer, device_id_type=MESH)
    for c in copies[5:]:
        c.start()

    c_par.wait()
    par_t = par_ref[...].astype(f32).astype(bf16)
    eye16 = one(iota((NB, NB), 0) == iota((NB, NB), 1))
    p0 = dot_nt(eye16, par_t[0:REQ]).astype(i32)
    p1 = dot_nt(eye16, par_t[REQ : 2 * REQ]).astype(i32)
    key0 = slot_key(p0, me)
    c_cs.wait()
    c_cw.wait()
    cw = cw_ref[...].astype(f32)
    cw_row = [cw[k : k + 1] for k in range(4)]
    win = [cs_ref[k].astype(f32) for k in range(3)]
    a0 = win[0] * cw_row[0] + win[1] * cw_row[1] + win[2] * cw_row[2]
    a1 = win[1] * cw_row[0] + win[2] * cw_row[1]
    h1s[:, 0:64, :] = jnp.broadcast_to(to_rows(a1).astype(bf16)[None], (NB, 64, 128))
    h1s[:, 64:80, :] = dot(pack_matrix(key0), to_rows(a0).astype(bf16)).astype(bf16).reshape(NB, 16, 128)
    key1 = slot_key(p1, me)
    pb1 = pack_matrix(key1)
    c_x.wait()
    x0 = x_ref[0].astype(f32)
    x1 = x_ref[1].astype(f32)
    h1s[:, 80:96, :] = dot(pb1, to_rows(x0).astype(bf16)).astype(bf16).reshape(NB, 16, 128)
    h1r[pl.ds(me, 1)] = h1s[pl.ds(me, 1)]

    c_q.wait()
    qrows = jnp.concatenate(
        [q_ref[s][:, h * 128 : (h + 1) * 128].astype(f32) for s in range(2) for h in range(GROUP)], axis=0
    ).astype(bf16)
    ri, ci = iota((64, 64), 0), iota((64, 64), 1)
    swap = one(((ri >> 3) == (ci & 7)) & ((ri & 7) == (ci >> 3)))
    qa[pl.ds(me, 1)] = dot(swap, qrows).astype(bf16)[None]

    pl.semaphore_wait(barrier, len(greeted))

    exchange(h1s, h1r, H1)
    gather(qa, QA, me, beam_peers)

    ub0 = unpack_matrix(p0, me)
    ub1 = unpack_matrix(p1, me)
    g = jnp.zeros((NB, REQ), i32)
    for p in range(NB):
        g = g + jnp.where(p1 == p, p0[p : p + 1, :], 0)
    _, g_own = own_column(g, me)
    g64 = jnp.concatenate([g_own] * LT, axis=0)
    ai, aj = iota((64, NB * 64), 0), iota((64, NB * 64), 1)
    ug = one((g64 == (aj >> 6).astype(f32)) & (ai == (aj & 63)))
    c_cb.wait()
    cb8 = cb_ref[...].astype(f32)
    cb = jnp.concatenate([cb8[i : i + 1] for i in range(LT)], axis=1)

    c_po.wait()
    c_ctx.wait()
    ctx_col = jnp.zeros((REQ, MAXP), i32)
    for r in range(REQ):
        ctx_col = jnp.where(iota((REQ, MAXP), 0) == r, ctx_ref[r], ctx_col)
    nvis = jnp.clip(ctx_col - iota((REQ, MAXP), 1) * PAGE, 0, PAGE)
    po = jnp.concatenate([po_ref[pl.ds(j, REQ, stride=4), :] for j in range(4)], axis=1)
    loc = po - me * PAGES
    flag = (loc >= 0) & (loc < PAGES) & (nvis > 0)
    tri = one(iota((MAXP, MAXP), 0) < iota((MAXP, MAXP), 1))
    rank = dot(one(flag), tri).astype(i32)
    count = jnp.sum(onef(flag), axis=1, keepdims=True).astype(i32)
    nblk = ((count + (BLK - 1)) >> 4).astype(f32)
    eye8 = iota((REQ, REQ), 0) == iota((REQ, REQ), 1)
    nblk_row = jnp.sum(jnp.where(eye8, nblk, 0.0), axis=0, keepdims=True)
    sblk = jnp.sum(
        jnp.where(iota((REQ, REQ), 1) < iota((REQ, REQ), 0), nblk_row, 0.0), axis=1, keepdims=True
    )
    dest = jnp.where(flag, sblk.astype(i32) * BLK + rank, -1)
    hi = dest >> 4
    lo = jnp.where(flag, dest & 15, -1)
    table = jnp.zeros((NBLK, 32), f32)
    for r in range(REQ):
        hot = one(hi[r : r + 1] == iota((NBLK, MAXP), 0))
        low = lo[r : r + 1] == iota((16, MAXP), 0)
        vals = jnp.concatenate(
            [
                jnp.where(low, loc[r : r + 1].astype(f32), 0.0),
                jnp.where(low, nvis[r : r + 1].astype(f32), 0.0),
            ],
            axis=0,
        ).astype(bf16)
        table = table + dot_nt(hot, vals)
    tab[...] = jnp.zeros_like(tab)
    tab[0:NBLK, 0:32] = table.astype(i32)
    lane = iota((REQ, 128), 1)
    subl = iota((REQ, 128), 0)
    sb_i, nb_i = sblk.astype(i32), nblk.astype(i32)
    inside = (sb_i <= lane) & (lane < sb_i + nb_i)
    tab[NBLK : NBLK + 1, :] = jnp.sum(jnp.where(inside, subl, 0).astype(f32), axis=0, keepdims=True).astype(i32)
    tab[NBLK + 1 : NBLK + 2, :] = jnp.sum(
        onef((lane == sb_i) & (nb_i > 0)), axis=0, keepdims=True
    ).astype(i32)
    tab[NBLK + 2 : NBLK + 3, :] = jnp.sum(
        jnp.where((lane == subl) & (nb_i > 0), sb_i + nb_i, 0).astype(f32), axis=0, keepdims=True
    ).astype(i32)
    cp_tab = pltpu.make_async_copy(tab, tabs, tsem)
    cp_tab.start()
    spread = one((iota((16, BLK * PAGE), 1) >> 4) == iota((16, BLK * PAGE), 0))
    seen = dot(table[:, 16:32].astype(bf16), spread)
    bias[...] = jnp.where((iota((NBLK, BLK * PAGE), 1) & 15).astype(f32) < seen, 0.0, NEG)
    orun[0] = jnp.zeros((128, 2 * HD), f32)
    mrun[0] = jnp.full((128, HD), NEG, f32)
    cp_tab.wait()

    wide = one((iota((REQ, REQ * 128), 1) >> 7) == iota((REQ, REQ * 128), 0))
    x_s0 = dot(one(p0 == me), wide)
    x_sg = dot(one(g == me), wide)
    x_s1 = dot(one(p1 == me), wide)
    tok = iota((NB, REQ * 128), 1) & 127
    mine = onef(iota((NB, REQ * 128), 0) == me)
    ok0 = jnp.where(tok < 16, x_s0, jnp.where(tok == 16, mine, 0.0))
    ok1 = jnp.where(tok < 16, x_sg, jnp.where(tok == 16, x_s1, jnp.where(tok == 17, mine, 0.0)))
    qi, qj = iota((128, 2 * NB), 0), iota((128, 2 * NB), 1)
    pick = one((((qi >> 2) & 1) == (qj >> 4)) & ((qi >> 3) == (qj & 15)))
    okm[...] = dot(pick, jnp.concatenate([ok0, ok1], axis=0).astype(bf16))

    c_rates.wait()
    for n in range(DS):
        rt[n] = jnp.broadcast_to(rates_ref[n : n + 1, :] * (-LOG2E), (REQ, CH))
    c_s.wait()
    row, col = iota((DS * NB * 2, 128), 0), iota((DS * NB * 2, 128), 1)
    rs_ = one(((iota((DS * NB * 2, NB), 0) >> 1) & 15) == iota((DS * NB * 2, NB), 1))
    crn = one((iota((REQ, 128), 1) >> 4) == iota((REQ, 128), 0))
    keys = dot(rs_, dot(key0.astype(bf16), crn).astype(bf16))
    sel0 = one((keys == (row & 1).astype(f32)) & ((row >> 5) == (col & 15)))
    pi, pj = iota((128, 128), 0), iota((128, 128), 1)
    perm1 = one(((pi & 7) == (pj >> 4)) & ((pi >> 3) == (pj & 15)))
    for j in range(4):
        sl = slice(j * 256, (j + 1) * 256)
        sj = s_v[:, sl].astype(bf16)
        s0[:, :, sl] = dot(sel0, sj).reshape(DS, NB * 2, 256)
        s1[:, :, sl] = dot(perm1, sj).reshape(DS, REQ, 256)
    held_here = column128(onef(g == me))
    g1 = one((column128(p1) == (pj >> 3).astype(f32)) & ((pi & 7) == (pj & 7)))
    r32 = one((iota((32, NB), 0) >> 1) == iota((32, NB), 1))
    c32 = one((iota((REQ, 128), 1) & 7) == iota((REQ, 128), 0))
    key32 = dot(dot(r32, key0.astype(bf16)).astype(bf16), c32)
    si, sj_ = iota((32, 128), 0), iota((32, 128), 1)
    psl = one((key32 == (si & 1).astype(f32)) & ((si >> 1) == (sj_ >> 3)))
    ui, uj = iota((256, 256), 0), iota((256, 256), 1)
    relay = one(((ui >> 4) == ((uj >> 1) & 15)) & (((ui >> 1) & 7) == (uj >> 5)) & ((ui & 1) == (uj & 1)))
    _, own1 = own_column(p1, me)
    gi, gj = iota((REQ, 128), 0), iota((REQ, 128), 1)
    og = one((own1 == (gj >> 3).astype(f32)) & (gi == (gj & 7)))

    c_xw.wait()
    landed(h1r, H1)
    conv0 = silu(from_rows(dot(ub0, h1r[:, 64:80, :].reshape(NB * 16, 128))) + cw_row[3] * x0 + cb)
    older = from_rows(dot(ug, h1r[:, 0:64, :].reshape(NB * 64, 128)))
    newer = from_rows(dot(ub1, h1r[:, 80:96, :].reshape(NB * 16, 128)))
    conv1 = silu(older + cw_row[2] * newer + cw_row[3] * x1 + cb)
    part = dot_nt(jnp.concatenate([conv0, conv1], axis=0).astype(bf16), xw_v[...])
    zb[pl.ds(mt, 1)] = jnp.zeros((1, 16, PROJ_PAD), bf16)
    zb[pl.ds(mt, 1), :, 0:PROJ] = part.astype(bf16)[None]
    gather(zb, ZB, mt, tensor_peers)
    hcs[...] = dot(pb1, to_rows(conv0).astype(bf16)).astype(bf16).reshape(NB, 16, 128)
    hcr[pl.ds(me, 1)] = hcs[pl.ds(me, 1)]
    exchange(hcs, hcr, HC)


    landed(qa, QA)
    qf = qa[...].astype(f32)
    for r in range(REQ):
        qr[r] = jnp.concatenate([qf[b, r * 8 : (r + 1) * 8] for b in range(NB)], axis=0).astype(bf16)
    c_kv.wait()
    scale = HD**-0.5 * LOG2E
    ones_blk = jnp.ones((BLK * PAGE, HD), bf16)

    def blocks(step, c):
        first = step * UNROLL
        m_old, o_old = mrun[first], orun[first]
        for u in range(UNROLL):
            i = first + u
            kv = jnp.concatenate([kv_v[tabs[i, k] & (PAGES - 1)] for k in range(BLK)], axis=0)
            s = dot_nt(qr[tabs[NBLK, i] & (REQ - 1)], kv[:, 0:HD]) * scale + bias[pl.ds(i, 1), :]
            m_old = jnp.where(tabs[NBLK + 1, i] > 0, NEG, m_old)
            m_new = jnp.maximum(m_old, jnp.max(s, axis=1, keepdims=True))
            e = jnp.exp2(s - jnp.concatenate([m_new, m_new], axis=1)).astype(bf16)
            v = jnp.concatenate([kv[:, HD : 2 * HD], ones_blk], axis=1)
            fade = jnp.exp2(m_old - m_new)
            o_old = o_old * jnp.concatenate([fade, fade], axis=1) + dot(e, v)
            m_old = m_new
            orun[i + 1] = o_old
            mrun[i + 1] = m_old
        return c

    steps = NBLK // UNROLL
    lax.fori_loop(0, 2, blocks, 0)

    landed(zb, ZB)
    proj = jnp.zeros((16, PROJ_PAD), f32)
    for t in range(nt):
        proj = proj + zb[t].astype(f32)
    prb[pl.ds(me, 1)] = proj.astype(bf16)[None]
    gather(prb, PR, me, beam_peers)

    lax.fori_loop(2, steps, blocks, 0)
    c_suf.wait()
    c_nkv.wait()
    nk0 = nkv_ref[0].astype(f32)
    nk1 = nkv_ref[1].astype(f32)
    diag = iota((128, 128), 0) == iota((128, 128), 1)
    ti = iota((16, 256), 0)
    for r in range(REQ):
        tail = jnp.where(ti == 0, nk0[r : r + 1], jnp.where(ti == 1, nk1[r : r + 1], 0.0)).astype(bf16)
        kv = jnp.concatenate([suf_ref[r], tail], axis=0)
        s = jnp.where(
            okm[:, r * 128 : r * 128 + 32] > 0.5, dot_nt(qr[r], kv[:, 0:HD]) * scale, NEG
        )
        last = jnp.clip(tabs[NBLK + 2, r], 0, NBLK)
        m_old = mrun[last]
        m_new = jnp.maximum(m_old, jnp.max(s, axis=1, keepdims=True))
        e = jnp.exp2(s - m_new[:, 0:32]).astype(bf16)
        v = jnp.concatenate([kv[:, HD : 2 * HD], jnp.ones((32, HD), bf16)], axis=1)
        fade = jnp.exp2(m_old - m_new)
        o = orun[last] * jnp.concatenate([fade, fade], axis=1) + dot(e, v)
        total = o[:, HD : 2 * HD]
        val = o[:, 0:HD] / total
        for b in range(NB):
            osf[b, r * 8 : (r + 1) * 8, :] = val[b * 8 : (b + 1) * 8]
        lg = m_new + jnp.log2(total)
        lse[pl.ds(me, 1), r : r + 1, :] = jnp.sum(jnp.where(diag, lg, 0.0), axis=0, keepdims=True)[None]
    os_[...] = osf[...].astype(bf16)
    or_[pl.ds(me, 1)] = os_[pl.ds(me, 1)]
    exchange(os_, or_, OO)
    gather(lse, LS, me, beam_peers)

    for c in (c_dtw, c_dtb, c_gain, c_skip, c_gate):
        c.wait()
    gain = gain_ref[...]

    def normed(rank_rows):
        mean = jnp.sum(rank_rows * rank_rows, axis=1, keepdims=True) * (1.0 / DT_RANK)
        return (rank_rows * lax.rsqrt(mean + 1e-6) * gain).astype(bf16)

    dtb = dtb_ref[...]
    landed(prb, PR)
    prf = prb[...].astype(f32)
    pr0 = prf[:, 0:REQ, :].reshape(128, PROJ_PAD)
    pr1 = prf[:, REQ : 2 * REQ, :].reshape(128, PROJ_PAD)
    rn0 = normed(pr0[:, 0:DT_RANK])
    rn1 = normed(pr1[:, 0:DT_RANK])
    bc0 = pr0[:, DT_RANK:PROJ].astype(bf16)
    c1[...] = (pr1[:, DT_RANK:PROJ_PAD] * held_here).reshape(NB, REQ, 128)
    rn0g = dot(g1, rn0).astype(bf16)

    rn0s = dot(psl, rn0).astype(bf16)
    c0s = dot(psl, bc0)
    c0b = [jnp.broadcast_to(c0s[:, DS + n : DS + n + 1], (NB * 2, 128)) for n in range(DS)]
    z0 = []
    for j in range(4):
        sl = slice(j * 256, (j + 1) * 256)
        w = dtw_v[:, sl]
        part1 = softplus(dot(rn1, w) + dtb[:, sl])
        part0 = softplus(dot(rn0g, w) + dtb[:, sl])
        d0g[:, :, sl] = part0.reshape(NB, REQ, 256)
        d1[:, :, sl] = (part0 + part1).reshape(NB, REQ, 256)
        dj = softplus(dot(rn0s, w) + dtb[:, sl])
        acc = jnp.zeros((32, 256), f32)
        for n in range(DS):
            cn = jnp.concatenate([c0b[n], c0b[n]], axis=1)
            acc = acc + cn * (jnp.exp2(dj * (rates_ref[n : n + 1, sl] * (-LOG2E))) * s0[n, :, sl])
        z0 += [acc[:, 0:128], acc[:, 128:256]]
    z0 = jnp.concatenate(z0, axis=0).astype(bf16)
    zzs[:, 64:80, :] = dot(relay, z0).astype(bf16).reshape(NB, 16, 128)

    def children(i, c):
        two = [(turn >> 2, turn & 3) for turn in (NB - 1 - 2 * i, NB - 2 - 2 * i)]
        two = [beam_at(dx, dy) for dx, dy in two]
        outs = [c1[b] for b in two]
        deltas = [d1[b] for b in two]
        accs = [jnp.zeros((REQ, CH), f32) for _ in two]
        for n in range(DS):
            rn, sn = rt[n], s1[n]
            for k in range(2):
                accs[k] = accs[k] + outs[k][:, DS + n : DS + n + 1] * (jnp.exp2(deltas[k] * rn) * sn)
        for k in range(2):
            zzs[two[k], 0:64, :] = to_rows(accs[k]).astype(bf16)
        remote(zzs.at[two[0]], zzr.at[me], ZZ, (two[0], mt)).start()

        @pl.when(i < NB // 2 - 1)
        def _():
            remote(zzs.at[two[1]], zzr.at[me], ZZ, (two[1], mt)).start()

        return c

    lax.fori_loop(0, NB // 2, children, 0)
    zzr[pl.ds(me, 1)] = zzs[pl.ds(me, 1)]

    own = proj.astype(bf16).astype(f32)
    d_own = softplus(dot(normed(own[:, 0:DT_RANK]), dtw_v[...]) + dtb)
    d_own0, d_own1 = d_own[0:REQ], d_own[REQ : 2 * REQ]
    own_in = own[:, DT_RANK : DT_RANK + DS]
    own_out = own[:, DT_RANK + DS : DT_RANK + 2 * DS]
    cb_own = jnp.sum(own_in * own_out, axis=1, keepdims=True)
    skip = skip_ref[...]
    base0 = d_own0 * conv0 * cb_own[0:REQ] + skip * conv0
    base1 = d_own1 * conv1 * cb_own[REQ : 2 * REQ] + skip * conv1
    gate0 = silu(gate_ref[0].astype(f32))
    gate1 = silu(gate_ref[1].astype(f32))

    landed(hcr, HC)
    conv0p = from_rows(dot(ub1, hcr[...].reshape(NB * 16, 128)))
    in0p = dot(og, bc0)[:, 0:DS]
    cross = in0p * own_out[REQ : 2 * REQ]
    mixed = jnp.zeros((REQ, CH), f32)
    for n in range(DS):
        mixed = mixed + cross[:, n : n + 1] * jnp.exp2(d_own1 * rt[n])
    base1 = base1 + mixed * (d0g[pl.ds(me, 1)][0] * conv0p)

    landed(or_, OO)
    landed(lse, LS)
    lanes = iota((8, 128), 1)
    want = lanes == me * 8 + iota((8, 128), 0)
    parts = []
    for p in range(NB):
        lp = lse[p]
        parts.append(
            jnp.concatenate(
                [
                    jnp.sum(jnp.where(want, lp[r : r + 1], 0.0), axis=1, keepdims=True)
                    for r in range(REQ)
                ],
                axis=0,
            )
        )
    top = parts[0]
    for p in range(1, NB):
        top = jnp.maximum(top, parts[p])
    den = jnp.zeros((64, 1), f32)
    num = jnp.zeros((64, HD), f32)
    for p in range(NB):
        w = jnp.exp2(parts[p] - top)
        den = den + w
        num = num + w * or_[p].astype(f32)
    att = dot(swap, (num / den).astype(bf16))
    for s in range(2):
        ao_ref[s, 0] = jnp.concatenate(
            [att[(s * GROUP + h) * 8 : (s * GROUP + h + 1) * 8] for h in range(GROUP)], axis=1
        ).astype(bf16)
    out_a = pltpu.make_async_copy(ao_ref, ao_h, tsem)
    out_a.start()

    landed(zzr, ZZ)
    z1 = jnp.zeros((64, 128), f32)
    for p in range(NB):
        z1 = z1 + zzr[p, 0:64, :].astype(f32)
    z0 = dot(ub0, zzr[:, 64:80, :].reshape(256, 128))
    mo_ref[0, 0] = ((from_rows(z0) + base0) * gate0).astype(bf16)
    mo_ref[1, 0] = ((from_rows(z1) + base1) * gate1).astype(bf16)
    out_m = pltpu.make_async_copy(mo_ref, mo_h, lsem.at[0])
    out_m.start()

    sent(h1s, H1)
    sent(hcs, HC)
    sent(qa, QA)
    sent(zb, ZB)
    sent(prb, PR)
    sent(os_, OO)
    sent(lse, LS)
    sent(zzs, ZZ)
    out_a.wait()
    out_m.wait()


def publish(m_ref, a_ref, mo_ref, ao_ref, m_v, a_v, sem):
    first = pltpu.make_async_copy(m_ref, m_v, sem.at[0])
    second = pltpu.make_async_copy(a_ref, a_v, sem.at[1])
    first.start()
    second.start()
    first.wait()
    first = pltpu.make_async_copy(m_v, mo_ref, sem.at[0])
    first.start()
    second.wait()
    second = pltpu.make_async_copy(a_v, ao_ref, sem.at[1])
    second.start()
    first.wait()
    second.wait()


def local(
    ssm_state,
    conv_state,
    suffix_kv,
    mamba_x,
    mamba_gate,
    conv_weight,
    conv_bias,
    xproj_weight,
    dt_gain,
    dtproj_weight,
    dt_bias,
    state_rates,
    skip_gain,
    queries,
    new_kv,
    kv_pool,
    page_order,
    ctx_len,
    parents,
):
    nt = lax.axis_size("tensor")
    hb = pl.BlockSpec(memory_space=pltpu.HBM)
    dma = pltpu.SemaphoreType.DMA
    V = pltpu.VMEM
    operands = [
        parents.transpose(0, 2, 1, 3).reshape(2 * REQ, NB),
        page_order.reshape(POOL // 128, 128),
        ctx_len,
        conv_state.transpose(0, 2, 1, 3)[0],
        conv_weight,
        conv_bias.reshape(LT, 128),
        mamba_x[:, 0],
        mamba_gate[:, 0],
        queries[:, 0],
        new_kv[:, 0],
        suffix_kv[0],
        dt_gain.reshape(1, DT_RANK),
        dt_bias.reshape(1, CH),
        state_rates,
        skip_gain.reshape(1, CH),
        ssm_state.reshape(REQ * DS, CH),
        xproj_weight.T,
        dtproj_weight,
        kv_pool,
    ]
    held = [V(a.shape, a.dtype) for a in operands]
    held[2] = pltpu.SMEM((REQ,), i32)
    outs = (
        jax.ShapeDtypeStruct((2, 1, REQ, CH), bf16),
        jax.ShapeDtypeStruct((2, 1, REQ, GROUP * HD), bf16),
    )
    results = pl.pallas_call(
        kernel,
        out_shape=outs,
        in_specs=[hb] * len(operands),
        out_specs=(hb, hb),
        scratch_shapes=held
        + [
            V(outs[0].shape, bf16),
            V(outs[1].shape, bf16),
            V((NB, 96, 128), bf16),
            V((NB, 96, 128), bf16),
            V((NB, 16, 128), bf16),
            V((NB, 16, 128), bf16),
            V((NB, 64, HD), bf16),
            V((nt, 16, PROJ_PAD), bf16),
            V((NB, 16, PROJ_PAD), bf16),
            V((NB, 80, 128), bf16),
            V((NB, 80, 128), bf16),
            V((NB, 64, HD), bf16),
            V((NB, 64, HD), bf16),
            V((NB, REQ, 128), f32),
            V((32, 128), i32),
            pltpu.SMEM((32, 128), i32),
            V((NBLK, BLK * PAGE), f32),
            V((REQ, 128, HD), bf16),
            V((NBLK + 1, 128, 2 * HD), f32),
            V((NBLK + 1, 128, HD), f32),
            V((NB, 64, HD), f32),
            V((DS, NB * 2, CH), f32),
            V((DS, REQ, CH), f32),
            V((DS, REQ, CH), f32),
            V((NB, REQ, CH), f32),
            V((NB, REQ, CH), f32),
            V((NB, REQ, 128), f32),
            V((128, REQ * 128), f32),
            dma((len(operands),)),
            dma,
            dma((8,)),
            dma((8,)),
        ],
        compiler_params=pltpu.CompilerParams(
            collective_id=0, has_side_effects=True, vmem_limit_bytes=63 * 2**20
        ),
        name="decode",
    )(*operands)
    return pl.pallas_call(
        publish,
        out_shape=outs,
        in_specs=[hb, hb],
        out_specs=(hb, hb),
        scratch_shapes=[V(outs[0].shape, bf16), V(outs[1].shape, bf16), dma((2,))],
        compiler_params=pltpu.CompilerParams(vmem_limit_bytes=63 * 2**20),
        name="publish",
    )(*results)


def solution(mesh):
    in_specs = (
        P("beam", None, None, "tensor"),
        P("beam", None, None, "tensor"),
        P("beam", None, None, "tensor"),
        P(None, "beam", None, "tensor"),
        P(None, "beam", None, "tensor"),
        P(None, "tensor"),
        P("tensor"),
        P("tensor", None),
        P(),
        P(None, "tensor"),
        P("tensor"),
        P(None, "tensor"),
        P("tensor"),
        P(None, "beam", None, "tensor"),
        P(None, "beam", None, "tensor"),
        P("beam", None, "tensor"),
        P(),
        P(),
        P(),
    )
    out_specs = (P(None, "beam", None, "tensor"), P(None, "beam", None, "tensor"))
    return jax.shard_map(local, mesh=mesh, in_specs=in_specs, out_specs=out_specs, check_vma=False)
```

```python
import jax
import jax.numpy as jnp
from jax import lax
from jax.experimental import pallas as pl
from jax.experimental.pallas import tpu as pltpu
from jax.sharding import PartitionSpec as P

NB = 16
REQ = 8
DS = 16
DT_RANK = 256
HD = 128
PAGE = 16
MAXP = 512
CH = 1024
LT = CH // 128
GROUP = 4
PAGES = 256
BLK = 16
NBLK = PAGES // BLK + REQ
UNROLL = 8
BEAM_ORDER = (
    (2, 2), (2, 1), (1, 2), (2, -1), (-1, 2), (2, 0), (0, 2), (1, 1), (-1, -1), (1, -1), (-1, 1), (0, 1), (1, 0),
    (0, -1), (-1, 0),
)
POOL = 4096
PROJ = DT_RANK + 2 * DS
PROJ_PAD = 384
LOG2E = 1.4426950408889634
NEG = -1e30

f32 = jnp.float32
bf16 = jnp.bfloat16
i32 = jnp.int32
MESH = pl.DeviceIdType.MESH


def iota(shape, dim):
    return lax.broadcasted_iota(i32, shape, dim)


def dot(a, b):
    return lax.dot_general(a, b, (((1,), (0,)), ((), ())), preferred_element_type=f32)


def dot_nt(a, b):
    return lax.dot_general(a, b, (((1,), (1,)), ((), ())), preferred_element_type=f32)


def one(mask):
    return jnp.where(mask, 1.0, 0.0).astype(bf16)


def onef(mask):
    return jnp.where(mask, 1.0, 0.0).astype(f32)


def to_rows(x):
    return jnp.concatenate([x[:, i * 128 : (i + 1) * 128] for i in range(LT)], axis=0)


def from_rows(x):
    return jnp.concatenate([x[i * REQ : (i + 1) * REQ] for i in range(LT)], axis=1)


def silu(v):
    return v / (1.0 + jnp.exp(-v))


def softplus(v):
    return jnp.maximum(v, 0.0) + jnp.log(1.0 + jnp.exp(-jnp.abs(v)))


def slot_key(par, me):
    chosen = par == me
    upper = one(iota((REQ, REQ), 0) < iota((REQ, REQ), 1))
    rank = dot(one(chosen), upper)
    return jnp.where(chosen, rank, -1.0)


def pack_matrix(key):
    rows, cols = NB * LT * 2, LT * REQ
    rb = one((iota((rows, NB), 0) >> 4) == iota((rows, NB), 1))
    cr = one((iota((REQ, cols), 1) & 7) == iota((REQ, cols), 0))
    spread = dot(dot(rb, key.astype(bf16)).astype(bf16), cr)
    row, col = iota((rows, cols), 0), iota((rows, cols), 1)
    return one((spread == (row & 1).astype(f32)) & (((row >> 1) & 7) == (col >> 3)))


def own_column(par, me):
    row = jnp.sum(jnp.where(iota((NB, REQ), 0) == me, par.astype(f32), 0.0), axis=0, keepdims=True)
    eye = iota((REQ, REQ), 0) == iota((REQ, REQ), 1)
    col = jnp.sum(jnp.where(eye, row, 0.0), axis=1, keepdims=True)
    return row, col


def unpack_matrix(par, me):
    row, col = own_column(par, me)
    alike = (row == col) & (iota((REQ, REQ), 1) < iota((REQ, REQ), 0))
    order = jnp.sum(onef(alike), axis=1, keepdims=True)
    code = jnp.concatenate([col * 2.0 + order] * LT, axis=0)
    rows, cols = LT * REQ, NB * LT * 2
    r, c = iota((rows, cols), 0), iota((rows, cols), 1)
    code_of = ((c >> 4) * 2 + (c & 1)).astype(f32)
    return one((code == code_of) & ((r >> 3) == ((c >> 1) & 7)))


def column128(m):
    spread = dot(one((iota((128, NB), 0) >> 3) == iota((128, NB), 1)), m.astype(bf16))
    pick = iota((128, REQ), 1) == (iota((128, REQ), 0) & 7)
    return jnp.sum(jnp.where(pick, spread, 0.0), axis=1, keepdims=True)


def kernel(
    par_h, po_h, ctx_h, cs_h, cw_h, cb_h, x_h, gate_h, q_h, nkv_h, suf_h, gain_h, dtb_h, rates_h, skip_h,
    s_h, xw_h, dtw_h, kv_h,
    mo_h, ao_h,
    par_ref, po_ref, ctx_ref, cs_ref, cw_ref, cb_ref, x_ref, gate_ref, q_ref, nkv_ref, suf_ref, gain_ref, dtb_ref,
    rates_ref, skip_ref, s_v, xw_v, dtw_v, kv_v,
    mo_ref, ao_ref,
    h1s, h1r, hcs, hcr, qa, zb, prb, zzs, zzr, os_, or_, lse,
    tab, tabs, bias, qr, orun, mrun, osf, s0, s1, rt, d1, d0g, c1, okm,
    lsem, tsem, ssem, rsem,
):
    me = lax.axis_index("beam")
    mt = lax.axis_index("tensor")
    nt = zb.shape[0]
    H1, QA, ZB, PR, OO, LS, ZZ, HC = range(8)

    def remote(src, dst, k, device):
        return pltpu.make_async_remote_copy(
            src_ref=src, dst_ref=dst, send_sem=ssem.at[k], recv_sem=rsem.at[k], device_id=device,
            device_id_type=MESH,
        )

    core, mz, nz = mt & 1, mt >> 1, nt // 2
    mx, my = me >> 2, me & 3

    def beam_at(dx, dy):
        return ((mx + dx + core * (-dy - dx)) & 3) * 4 + ((my + dy + core * (-dx - dy)) & 3)

    def tensor_at(dz, other):
        return ((mz + dz * (1 - 2 * core)) & (nz - 1)) * 2 + ((core + other) & 1)

    beam_peers = [(beam_at(dx, dy), mt) for dx, dy in BEAM_ORDER]
    z_order = [k for far in range(nz // 2, 0, -1) for k in sorted({far % nz, -far % nz})]
    tensor_peers = [(me, tensor_at(dz, other)) for dz in z_order for other in (0, 1)] + [(me, tensor_at(0, 1))]

    def exchange(src, dst, k):
        for peer in beam_peers:
            remote(src.at[peer[0]], dst.at[me], k, peer).start()

    def gather(buf, k, at, peers):
        for peer in peers:
            remote(buf.at[at], buf.at[at], k, peer).start()

    def all_of(buf, k):
        part = buf.at[pl.ds(0, buf.shape[0] - 1)]
        return remote(part, part, k, (me, mt))

    def landed(buf, k):
        all_of(buf, k).wait_recv()

    def sent(buf, k):
        all_of(buf, k).wait_send()

    pairs = [
        (par_h, par_ref), (cs_h, cs_ref), (cw_h, cw_ref), (x_h, x_ref), (q_h, q_ref), (s_h, s_v),
        (rates_h, rates_ref), (cb_h, cb_ref), (po_h, po_ref), (ctx_h, ctx_ref), (xw_h, xw_v), (kv_h, kv_v),
        (suf_h, suf_ref), (nkv_h, nkv_ref), (dtw_h, dtw_v), (dtb_h, dtb_ref), (gain_h, gain_ref),
        (skip_h, skip_ref), (gate_h, gate_ref),
    ]
    copies = [pltpu.make_async_copy(a, b, lsem.at[i]) for i, (a, b) in enumerate(pairs)]
    (c_par, c_cs, c_cw, c_x, c_q, c_s, c_rates, c_cb, c_po, c_ctx, c_xw, c_kv, c_suf, c_nkv, c_dtw, c_dtb, c_gain,
     c_skip, c_gate) = copies
    for c in copies[0:5]:
        c.start()
    barrier = pltpu.get_barrier_semaphore()
    greeted = beam_peers + tensor_peers
    for peer in greeted:
        pl.semaphore_signal(barrier, inc=1, device_id=peer, device_id_type=MESH)
    for c in copies[5:]:
        c.start()

    c_par.wait()
    par_t = par_ref[...].astype(f32).astype(bf16)
    eye16 = one(iota((NB, NB), 0) == iota((NB, NB), 1))
    p0 = dot_nt(eye16, par_t[0:REQ]).astype(i32)
    p1 = dot_nt(eye16, par_t[REQ : 2 * REQ]).astype(i32)
    key0 = slot_key(p0, me)
    c_cs.wait()
    c_cw.wait()
    cw = cw_ref[...].astype(f32)
    cw_row = [cw[k : k + 1] for k in range(4)]
    win = [cs_ref[k].astype(f32) for k in range(3)]
    a0 = win[0] * cw_row[0] + win[1] * cw_row[1] + win[2] * cw_row[2]
    a1 = win[1] * cw_row[0] + win[2] * cw_row[1]
    h1s[:, 0:64, :] = jnp.broadcast_to(to_rows(a1).astype(bf16)[None], (NB, 64, 128))
    h1s[:, 64:80, :] = dot(pack_matrix(key0), to_rows(a0).astype(bf16)).astype(bf16).reshape(NB, 16, 128)
    key1 = slot_key(p1, me)
    pb1 = pack_matrix(key1)
    c_x.wait()
    x0 = x_ref[0].astype(f32)
    x1 = x_ref[1].astype(f32)
    h1s[:, 80:96, :] = dot(pb1, to_rows(x0).astype(bf16)).astype(bf16).reshape(NB, 16, 128)
    h1r[pl.ds(me, 1)] = h1s[pl.ds(me, 1)]

    c_q.wait()
    qrows = jnp.concatenate(
        [q_ref[s][:, h * 128 : (h + 1) * 128].astype(f32) for s in range(2) for h in range(GROUP)], axis=0
    ).astype(bf16)
    ri, ci = iota((64, 64), 0), iota((64, 64), 1)
    swap = one(((ri >> 3) == (ci & 7)) & ((ri & 7) == (ci >> 3)))
    qa[pl.ds(me, 1)] = dot(swap, qrows).astype(bf16)[None]

    pl.semaphore_wait(barrier, len(greeted))

    exchange(h1s, h1r, H1)
    gather(qa, QA, me, beam_peers)

    ub0 = unpack_matrix(p0, me)
    ub1 = unpack_matrix(p1, me)
    g = jnp.zeros((NB, REQ), i32)
    for p in range(NB):
        g = g + jnp.where(p1 == p, p0[p : p + 1, :], 0)
    _, g_own = own_column(g, me)
    g64 = jnp.concatenate([g_own] * LT, axis=0)
    ai, aj = iota((64, NB * 64), 0), iota((64, NB * 64), 1)
    ug = one((g64 == (aj >> 6).astype(f32)) & (ai == (aj & 63)))
    c_cb.wait()
    cb8 = cb_ref[...].astype(f32)
    cb = jnp.concatenate([cb8[i : i + 1] for i in range(LT)], axis=1)

    c_po.wait()
    c_ctx.wait()
    ctx_col = jnp.zeros((REQ, MAXP), i32)
    for r in range(REQ):
        ctx_col = jnp.where(iota((REQ, MAXP), 0) == r, ctx_ref[r], ctx_col)
    nvis = jnp.clip(ctx_col - iota((REQ, MAXP), 1) * PAGE, 0, PAGE)
    po = jnp.concatenate([po_ref[pl.ds(j, REQ, stride=4), :] for j in range(4)], axis=1)
    loc = po - me * PAGES
    flag = (loc >= 0) & (loc < PAGES) & (nvis > 0)
    tri = one(iota((MAXP, MAXP), 0) < iota((MAXP, MAXP), 1))
    rank = dot(one(flag), tri).astype(i32)
    count = jnp.sum(onef(flag), axis=1, keepdims=True).astype(i32)
    nblk = ((count + (BLK - 1)) >> 4).astype(f32)
    eye8 = iota((REQ, REQ), 0) == iota((REQ, REQ), 1)
    nblk_row = jnp.sum(jnp.where(eye8, nblk, 0.0), axis=0, keepdims=True)
    sblk = jnp.sum(
        jnp.where(iota((REQ, REQ), 1) < iota((REQ, REQ), 0), nblk_row, 0.0), axis=1, keepdims=True
    )
    dest = jnp.where(flag, sblk.astype(i32) * BLK + rank, -1)
    hi = dest >> 4
    lo = jnp.where(flag, dest & 15, -1)
    table = jnp.zeros((NBLK, 32), f32)
    for r in range(REQ):
        hot = one(hi[r : r + 1] == iota((NBLK, MAXP), 0))
        low = lo[r : r + 1] == iota((16, MAXP), 0)
        vals = jnp.concatenate(
            [
                jnp.where(low, loc[r : r + 1].astype(f32), 0.0),
                jnp.where(low, nvis[r : r + 1].astype(f32), 0.0),
            ],
            axis=0,
        ).astype(bf16)
        table = table + dot_nt(hot, vals)
    tab[...] = jnp.zeros_like(tab)
    tab[0:NBLK, 0:32] = table.astype(i32)
    lane = iota((REQ, 128), 1)
    subl = iota((REQ, 128), 0)
    sb_i, nb_i = sblk.astype(i32), nblk.astype(i32)
    inside = (sb_i <= lane) & (lane < sb_i + nb_i)
    tab[NBLK : NBLK + 1, :] = jnp.sum(jnp.where(inside, subl, 0).astype(f32), axis=0, keepdims=True).astype(i32)
    tab[NBLK + 1 : NBLK + 2, :] = jnp.sum(
        onef((lane == sb_i) & (nb_i > 0)), axis=0, keepdims=True
    ).astype(i32)
    tab[NBLK + 2 : NBLK + 3, :] = jnp.sum(
        jnp.where((lane == subl) & (nb_i > 0), sb_i + nb_i, 0).astype(f32), axis=0, keepdims=True
    ).astype(i32)
    cp_tab = pltpu.make_async_copy(tab, tabs, tsem)
    cp_tab.start()
    spread = one((iota((16, BLK * PAGE), 1) >> 4) == iota((16, BLK * PAGE), 0))
    seen = dot(table[:, 16:32].astype(bf16), spread)
    bias[...] = jnp.where((iota((NBLK, BLK * PAGE), 1) & 15).astype(f32) < seen, 0.0, NEG)
    orun[0] = jnp.zeros((128, 2 * HD), f32)
    mrun[0] = jnp.full((128, HD), NEG, f32)
    cp_tab.wait()

    wide = one((iota((REQ, REQ * 128), 1) >> 7) == iota((REQ, REQ * 128), 0))
    x_s0 = dot(one(p0 == me), wide)
    x_sg = dot(one(g == me), wide)
    x_s1 = dot(one(p1 == me), wide)
    tok = iota((NB, REQ * 128), 1) & 127
    mine = onef(iota((NB, REQ * 128), 0) == me)
    ok0 = jnp.where(tok < 16, x_s0, jnp.where(tok == 16, mine, 0.0))
    ok1 = jnp.where(tok < 16, x_sg, jnp.where(tok == 16, x_s1, jnp.where(tok == 17, mine, 0.0)))
    qi, qj = iota((128, 2 * NB), 0), iota((128, 2 * NB), 1)
    pick = one((((qi >> 2) & 1) == (qj >> 4)) & ((qi >> 3) == (qj & 15)))
    okm[...] = dot(pick, jnp.concatenate([ok0, ok1], axis=0).astype(bf16))

    c_rates.wait()
    for n in range(DS):
        rt[n] = jnp.broadcast_to(rates_ref[n : n + 1, :] * (-LOG2E), (REQ, CH))
    c_s.wait()
    row, col = iota((DS * NB * 2, 128), 0), iota((DS * NB * 2, 128), 1)
    rs_ = one(((iota((DS * NB * 2, NB), 0) >> 1) & 15) == iota((DS * NB * 2, NB), 1))
    crn = one((iota((REQ, 128), 1) >> 4) == iota((REQ, 128), 0))
    keys = dot(rs_, dot(key0.astype(bf16), crn).astype(bf16))
    sel0 = one((keys == (row & 1).astype(f32)) & ((row >> 5) == (col & 15)))
    pi, pj = iota((128, 128), 0), iota((128, 128), 1)
    perm1 = one(((pi & 7) == (pj >> 4)) & ((pi >> 3) == (pj & 15)))
    for j in range(4):
        sl = slice(j * 256, (j + 1) * 256)
        sj = s_v[:, sl].astype(bf16)
        s0[:, :, sl] = dot(sel0, sj).reshape(DS, NB * 2, 256)
        s1[:, :, sl] = dot(perm1, sj).reshape(DS, REQ, 256)
    held_here = column128(onef(g == me))
    g1 = one((column128(p1) == (pj >> 3).astype(f32)) & ((pi & 7) == (pj & 7)))
    r32 = one((iota((32, NB), 0) >> 1) == iota((32, NB), 1))
    c32 = one((iota((REQ, 128), 1) & 7) == iota((REQ, 128), 0))
    key32 = dot(dot(r32, key0.astype(bf16)).astype(bf16), c32)
    si, sj_ = iota((32, 128), 0), iota((32, 128), 1)
    psl = one((key32 == (si & 1).astype(f32)) & ((si >> 1) == (sj_ >> 3)))
    ui, uj = iota((256, 256), 0), iota((256, 256), 1)
    relay = one(((ui >> 4) == ((uj >> 1) & 15)) & (((ui >> 1) & 7) == (uj >> 5)) & ((ui & 1) == (uj & 1)))
    _, own1 = own_column(p1, me)
    gi, gj = iota((REQ, 128), 0), iota((REQ, 128), 1)
    og = one((own1 == (gj >> 3).astype(f32)) & (gi == (gj & 7)))

    c_xw.wait()
    landed(h1r, H1)
    conv0 = silu(from_rows(dot(ub0, h1r[:, 64:80, :].reshape(NB * 16, 128))) + cw_row[3] * x0 + cb)
    older = from_rows(dot(ug, h1r[:, 0:64, :].reshape(NB * 64, 128)))
    newer = from_rows(dot(ub1, h1r[:, 80:96, :].reshape(NB * 16, 128)))
    conv1 = silu(older + cw_row[2] * newer + cw_row[3] * x1 + cb)
    part = dot_nt(jnp.concatenate([conv0, conv1], axis=0).astype(bf16), xw_v[...])
    zb[pl.ds(mt, 1)] = jnp.zeros((1, 16, PROJ_PAD), bf16)
    zb[pl.ds(mt, 1), :, 0:PROJ] = part.astype(bf16)[None]
    gather(zb, ZB, mt, tensor_peers)
    hcs[...] = dot(pb1, to_rows(conv0).astype(bf16)).astype(bf16).reshape(NB, 16, 128)
    hcr[pl.ds(me, 1)] = hcs[pl.ds(me, 1)]
    exchange(hcs, hcr, HC)


    landed(qa, QA)
    qf = qa[...].astype(f32)
    for r in range(REQ):
        qr[r] = jnp.concatenate([qf[b, r * 8 : (r + 1) * 8] for b in range(NB)], axis=0).astype(bf16)
    c_kv.wait()
    scale = HD**-0.5 * LOG2E
    ones_blk = jnp.ones((BLK * PAGE, HD), bf16)

    def blocks(step, c):
        first = step * UNROLL
        m_old, o_old = mrun[first], orun[first]
        for u in range(UNROLL):
            i = first + u
            kv = jnp.concatenate([kv_v[tabs[i, k] & (PAGES - 1)] for k in range(BLK)], axis=0)
            s = dot_nt(qr[tabs[NBLK, i] & (REQ - 1)], kv[:, 0:HD]) * scale + bias[pl.ds(i, 1), :]
            m_old = jnp.where(tabs[NBLK + 1, i] > 0, NEG, m_old)
            m_new = jnp.maximum(m_old, jnp.max(s, axis=1, keepdims=True))
            e = jnp.exp2(s - jnp.concatenate([m_new, m_new], axis=1)).astype(bf16)
            v = jnp.concatenate([kv[:, HD : 2 * HD], ones_blk], axis=1)
            fade = jnp.exp2(m_old - m_new)
            o_old = o_old * jnp.concatenate([fade, fade], axis=1) + dot(e, v)
            m_old = m_new
            orun[i + 1] = o_old
            mrun[i + 1] = m_old
        return c

    steps = NBLK // UNROLL
    lax.fori_loop(0, 2, blocks, 0)

    landed(zb, ZB)
    proj = jnp.zeros((16, PROJ_PAD), f32)
    for t in range(nt):
        proj = proj + zb[t].astype(f32)
    prb[pl.ds(me, 1)] = proj.astype(bf16)[None]
    gather(prb, PR, me, beam_peers)

    lax.fori_loop(2, steps, blocks, 0)
    c_suf.wait()
    c_nkv.wait()
    nk0 = nkv_ref[0].astype(f32)
    nk1 = nkv_ref[1].astype(f32)
    diag = iota((128, 128), 0) == iota((128, 128), 1)
    ti = iota((16, 256), 0)
    for r in range(REQ):
        tail = jnp.where(ti == 0, nk0[r : r + 1], jnp.where(ti == 1, nk1[r : r + 1], 0.0)).astype(bf16)
        kv = jnp.concatenate([suf_ref[r], tail], axis=0)
        s = jnp.where(
            okm[:, r * 128 : r * 128 + 32] > 0.5, dot_nt(qr[r], kv[:, 0:HD]) * scale, NEG
        )
        last = jnp.clip(tabs[NBLK + 2, r], 0, NBLK)
        m_old = mrun[last]
        m_new = jnp.maximum(m_old, jnp.max(s, axis=1, keepdims=True))
        e = jnp.exp2(s - m_new[:, 0:32]).astype(bf16)
        v = jnp.concatenate([kv[:, HD : 2 * HD], jnp.ones((32, HD), bf16)], axis=1)
        fade = jnp.exp2(m_old - m_new)
        o = orun[last] * jnp.concatenate([fade, fade], axis=1) + dot(e, v)
        total = o[:, HD : 2 * HD]
        val = o[:, 0:HD] / total
        for b in range(NB):
            osf[b, r * 8 : (r + 1) * 8, :] = val[b * 8 : (b + 1) * 8]
        lg = m_new + jnp.log2(total)
        lse[pl.ds(me, 1), r : r + 1, :] = jnp.sum(jnp.where(diag, lg, 0.0), axis=0, keepdims=True)[None]
    os_[...] = osf[...].astype(bf16)
    or_[pl.ds(me, 1)] = os_[pl.ds(me, 1)]
    exchange(os_, or_, OO)
    gather(lse, LS, me, beam_peers)

    for c in (c_dtw, c_dtb, c_gain, c_skip, c_gate):
        c.wait()
    gain = gain_ref[...]

    def normed(rank_rows):
        mean = jnp.sum(rank_rows * rank_rows, axis=1, keepdims=True) * (1.0 / DT_RANK)
        return (rank_rows * lax.rsqrt(mean + 1e-6) * gain).astype(bf16)

    dtb = dtb_ref[...]
    landed(prb, PR)
    prf = prb[...].astype(f32)
    pr0 = prf[:, 0:REQ, :].reshape(128, PROJ_PAD)
    pr1 = prf[:, REQ : 2 * REQ, :].reshape(128, PROJ_PAD)
    rn0 = normed(pr0[:, 0:DT_RANK])
    rn1 = normed(pr1[:, 0:DT_RANK])
    bc0 = pr0[:, DT_RANK:PROJ].astype(bf16)
    c1[...] = (pr1[:, DT_RANK:PROJ_PAD] * held_here).reshape(NB, REQ, 128)
    rn0g = dot(g1, rn0).astype(bf16)

    rn0s = dot(psl, rn0).astype(bf16)
    c0s = dot(psl, bc0)
    c0b = [jnp.broadcast_to(c0s[:, DS + n : DS + n + 1], (NB * 2, 128)) for n in range(DS)]
    z0 = []
    for j in range(4):
        sl = slice(j * 256, (j + 1) * 256)
        w = dtw_v[:, sl]
        part1 = softplus(dot(rn1, w) + dtb[:, sl])
        part0 = softplus(dot(rn0g, w) + dtb[:, sl])
        d0g[:, :, sl] = part0.reshape(NB, REQ, 256)
        d1[:, :, sl] = (part0 + part1).reshape(NB, REQ, 256)
        dj = softplus(dot(rn0s, w) + dtb[:, sl])
        acc = jnp.zeros((32, 256), f32)
        for n in range(DS):
            cn = jnp.concatenate([c0b[n], c0b[n]], axis=1)
            acc = acc + cn * (jnp.exp2(dj * (rates_ref[n : n + 1, sl] * (-LOG2E))) * s0[n, :, sl])
        z0 += [acc[:, 0:128], acc[:, 128:256]]
    z0 = jnp.concatenate(z0, axis=0).astype(bf16)
    zzs[:, 64:80, :] = dot(relay, z0).astype(bf16).reshape(NB, 16, 128)

    def children(i, c):
        two = [(turn & 3, ((turn >> 2) + turn) & 3) for turn in (NB - 1 - 2 * i, NB - 2 - 2 * i)]
        two = [beam_at(dx, dy) for dx, dy in two]
        outs = [c1[b] for b in two]
        deltas = [d1[b] for b in two]
        accs = [jnp.zeros((REQ, CH), f32) for _ in two]
        for n in range(DS):
            rn, sn = rt[n], s1[n]
            for k in range(2):
                accs[k] = accs[k] + outs[k][:, DS + n : DS + n + 1] * (jnp.exp2(deltas[k] * rn) * sn)
        for k in range(2):
            zzs[two[k], 0:64, :] = to_rows(accs[k]).astype(bf16)
        remote(zzs.at[two[0]], zzr.at[me], ZZ, (two[0], mt)).start()

        @pl.when(i < NB // 2 - 1)
        def _():
            remote(zzs.at[two[1]], zzr.at[me], ZZ, (two[1], mt)).start()

        return c

    lax.fori_loop(0, NB // 2, children, 0)
    zzr[pl.ds(me, 1)] = zzs[pl.ds(me, 1)]

    own = proj.astype(bf16).astype(f32)
    d_own = softplus(dot(normed(own[:, 0:DT_RANK]), dtw_v[...]) + dtb)
    d_own0, d_own1 = d_own[0:REQ], d_own[REQ : 2 * REQ]
    own_in = own[:, DT_RANK : DT_RANK + DS]
    own_out = own[:, DT_RANK + DS : DT_RANK + 2 * DS]
    cb_own = jnp.sum(own_in * own_out, axis=1, keepdims=True)
    skip = skip_ref[...]
    base0 = d_own0 * conv0 * cb_own[0:REQ] + skip * conv0
    base1 = d_own1 * conv1 * cb_own[REQ : 2 * REQ] + skip * conv1
    gate0 = silu(gate_ref[0].astype(f32))
    gate1 = silu(gate_ref[1].astype(f32))

    landed(hcr, HC)
    conv0p = from_rows(dot(ub1, hcr[...].reshape(NB * 16, 128)))
    in0p = dot(og, bc0)[:, 0:DS]
    cross = in0p * own_out[REQ : 2 * REQ]
    mixed = jnp.zeros((REQ, CH), f32)
    for n in range(DS):
        mixed = mixed + cross[:, n : n + 1] * jnp.exp2(d_own1 * rt[n])
    base1 = base1 + mixed * (d0g[pl.ds(me, 1)][0] * conv0p)

    landed(or_, OO)
    landed(lse, LS)
    lanes = iota((8, 128), 1)
    want = lanes == me * 8 + iota((8, 128), 0)
    parts = []
    for p in range(NB):
        lp = lse[p]
        parts.append(
            jnp.concatenate(
                [
                    jnp.sum(jnp.where(want, lp[r : r + 1], 0.0), axis=1, keepdims=True)
                    for r in range(REQ)
                ],
                axis=0,
            )
        )
    top = parts[0]
    for p in range(1, NB):
        top = jnp.maximum(top, parts[p])
    den = jnp.zeros((64, 1), f32)
    num = jnp.zeros((64, HD), f32)
    for p in range(NB):
        w = jnp.exp2(parts[p] - top)
        den = den + w
        num = num + w * or_[p].astype(f32)
    att = dot(swap, (num / den).astype(bf16))
    for s in range(2):
        ao_ref[s, 0] = jnp.concatenate(
            [att[(s * GROUP + h) * 8 : (s * GROUP + h + 1) * 8] for h in range(GROUP)], axis=1
        ).astype(bf16)
    out_a = pltpu.make_async_copy(ao_ref, ao_h, tsem)
    out_a.start()

    landed(zzr, ZZ)
    z1 = jnp.zeros((64, 128), f32)
    for p in range(NB):
        z1 = z1 + zzr[p, 0:64, :].astype(f32)
    z0 = dot(ub0, zzr[:, 64:80, :].reshape(256, 128))
    mo_ref[0, 0] = ((from_rows(z0) + base0) * gate0).astype(bf16)
    mo_ref[1, 0] = ((from_rows(z1) + base1) * gate1).astype(bf16)
    out_m = pltpu.make_async_copy(mo_ref, mo_h, lsem.at[0])
    out_m.start()

    sent(h1s, H1)
    sent(hcs, HC)
    sent(qa, QA)
    sent(zb, ZB)
    sent(prb, PR)
    sent(os_, OO)
    sent(lse, LS)
    sent(zzs, ZZ)
    out_a.wait()
    out_m.wait()


def publish(m_ref, a_ref, mo_ref, ao_ref, m_v, a_v, sem):
    first = pltpu.make_async_copy(m_ref, m_v, sem.at[0])
    second = pltpu.make_async_copy(a_ref, a_v, sem.at[1])
    first.start()
    second.start()
    first.wait()
    first = pltpu.make_async_copy(m_v, mo_ref, sem.at[0])
    first.start()
    second.wait()
    second = pltpu.make_async_copy(a_v, ao_ref, sem.at[1])
    second.start()
    first.wait()
    second.wait()


def local(
    ssm_state,
    conv_state,
    suffix_kv,
    mamba_x,
    mamba_gate,
    conv_weight,
    conv_bias,
    xproj_weight,
    dt_gain,
    dtproj_weight,
    dt_bias,
    state_rates,
    skip_gain,
    queries,
    new_kv,
    kv_pool,
    page_order,
    ctx_len,
    parents,
):
    nt = lax.axis_size("tensor")
    hb = pl.BlockSpec(memory_space=pltpu.HBM)
    dma = pltpu.SemaphoreType.DMA
    V = pltpu.VMEM
    operands = [
        parents.transpose(0, 2, 1, 3).reshape(2 * REQ, NB),
        page_order.reshape(POOL // 128, 128),
        ctx_len,
        conv_state.transpose(0, 2, 1, 3)[0],
        conv_weight,
        conv_bias.reshape(LT, 128),
        mamba_x[:, 0],
        mamba_gate[:, 0],
        queries[:, 0],
        new_kv[:, 0],
        suffix_kv[0],
        dt_gain.reshape(1, DT_RANK),
        dt_bias.reshape(1, CH),
        state_rates,
        skip_gain.reshape(1, CH),
        ssm_state.reshape(REQ * DS, CH),
        xproj_weight.T,
        dtproj_weight,
        kv_pool,
    ]
    held = [V(a.shape, a.dtype) for a in operands]
    held[2] = pltpu.SMEM((REQ,), i32)
    outs = (
        jax.ShapeDtypeStruct((2, 1, REQ, CH), bf16),
        jax.ShapeDtypeStruct((2, 1, REQ, GROUP * HD), bf16),
    )
    results = pl.pallas_call(
        kernel,
        out_shape=outs,
        in_specs=[hb] * len(operands),
        out_specs=(hb, hb),
        scratch_shapes=held
        + [
            V(outs[0].shape, bf16),
            V(outs[1].shape, bf16),
            V((NB, 96, 128), bf16),
            V((NB, 96, 128), bf16),
            V((NB, 16, 128), bf16),
            V((NB, 16, 128), bf16),
            V((NB, 64, HD), bf16),
            V((nt, 16, PROJ_PAD), bf16),
            V((NB, 16, PROJ_PAD), bf16),
            V((NB, 80, 128), bf16),
            V((NB, 80, 128), bf16),
            V((NB, 64, HD), bf16),
            V((NB, 64, HD), bf16),
            V((NB, REQ, 128), f32),
            V((32, 128), i32),
            pltpu.SMEM((32, 128), i32),
            V((NBLK, BLK * PAGE), f32),
            V((REQ, 128, HD), bf16),
            V((NBLK + 1, 128, 2 * HD), f32),
            V((NBLK + 1, 128, HD), f32),
            V((NB, 64, HD), f32),
            V((DS, NB * 2, CH), f32),
            V((DS, REQ, CH), f32),
            V((DS, REQ, CH), f32),
            V((NB, REQ, CH), f32),
            V((NB, REQ, CH), f32),
            V((NB, REQ, 128), f32),
            V((128, REQ * 128), f32),
            dma((len(operands),)),
            dma,
            dma((8,)),
            dma((8,)),
        ],
        compiler_params=pltpu.CompilerParams(
            collective_id=0, has_side_effects=True, vmem_limit_bytes=63 * 2**20
        ),
        name="decode",
    )(*operands)
    return pl.pallas_call(
        publish,
        out_shape=outs,
        in_specs=[hb, hb],
        out_specs=(hb, hb),
        scratch_shapes=[V(outs[0].shape, bf16), V(outs[1].shape, bf16), dma((2,))],
        compiler_params=pltpu.CompilerParams(vmem_limit_bytes=63 * 2**20),
        name="publish",
    )(*results)


def solution(mesh):
    in_specs = (
        P("beam", None, None, "tensor"),
        P("beam", None, None, "tensor"),
        P("beam", None, None, "tensor"),
        P(None, "beam", None, "tensor"),
        P(None, "beam", None, "tensor"),
        P(None, "tensor"),
        P("tensor"),
        P("tensor", None),
        P(),
        P(None, "tensor"),
        P("tensor"),
        P(None, "tensor"),
        P("tensor"),
        P(None, "beam", None, "tensor"),
        P(None, "beam", None, "tensor"),
        P("beam", None, "tensor"),
        P(),
        P(),
        P(),
    )
    out_specs = (P(None, "beam", None, "tensor"), P(None, "beam", None, "tensor"))
    return jax.shard_map(local, mesh=mesh, in_specs=in_specs, out_specs=out_specs, check_vma=False)
```

```python
import jax
import jax.numpy as jnp
from jax import lax
from jax.experimental import pallas as pl
from jax.experimental.pallas import tpu as pltpu
from jax.sharding import PartitionSpec as P

NB = 16
REQ = 8
DS = 16
DT_RANK = 256
HD = 128
PAGE = 16
MAXP = 512
CH = 1024
LT = CH // 128
GROUP = 4
PAGES = 256
BLK = 16
NBLK = PAGES // BLK + REQ
UNROLL = 8
BEAM_ORDER = (
    (2, 2), (2, 1), (1, 2), (2, -1), (-1, 2), (2, 0), (0, 2), (1, 1), (-1, -1), (1, -1), (-1, 1), (0, 1), (1, 0),
    (0, -1), (-1, 0),
)
POOL = 4096
PROJ = DT_RANK + 2 * DS
PROJ_PAD = 384
LOG2E = 1.4426950408889634
NEG = -1e30

f32 = jnp.float32
bf16 = jnp.bfloat16
i32 = jnp.int32
MESH = pl.DeviceIdType.MESH


def iota(shape, dim):
    return lax.broadcasted_iota(i32, shape, dim)


def dot(a, b):
    return lax.dot_general(a, b, (((1,), (0,)), ((), ())), preferred_element_type=f32)


def dot_nt(a, b):
    return lax.dot_general(a, b, (((1,), (1,)), ((), ())), preferred_element_type=f32)


def one(mask):
    return jnp.where(mask, 1.0, 0.0).astype(bf16)


def onef(mask):
    return jnp.where(mask, 1.0, 0.0).astype(f32)


def to_rows(x):
    return jnp.concatenate([x[:, i * 128 : (i + 1) * 128] for i in range(LT)], axis=0)


def from_rows(x):
    return jnp.concatenate([x[i * REQ : (i + 1) * REQ] for i in range(LT)], axis=1)


def silu(v):
    return v / (1.0 + jnp.exp(-v))


def softplus(v):
    return jnp.maximum(v, 0.0) + jnp.log(1.0 + jnp.exp(-jnp.abs(v)))


def slot_key(par, me):
    chosen = par == me
    upper = one(iota((REQ, REQ), 0) < iota((REQ, REQ), 1))
    rank = dot(one(chosen), upper)
    return jnp.where(chosen, rank, -1.0)


def pack_matrix(key):
    rows, cols = NB * LT * 2, LT * REQ
    rb = one((iota((rows, NB), 0) >> 4) == iota((rows, NB), 1))
    cr = one((iota((REQ, cols), 1) & 7) == iota((REQ, cols), 0))
    spread = dot(dot(rb, key.astype(bf16)).astype(bf16), cr)
    row, col = iota((rows, cols), 0), iota((rows, cols), 1)
    return one((spread == (row & 1).astype(f32)) & (((row >> 1) & 7) == (col >> 3)))


def own_column(par, me):
    row = jnp.sum(jnp.where(iota((NB, REQ), 0) == me, par.astype(f32), 0.0), axis=0, keepdims=True)
    eye = iota((REQ, REQ), 0) == iota((REQ, REQ), 1)
    col = jnp.sum(jnp.where(eye, row, 0.0), axis=1, keepdims=True)
    return row, col


def unpack_matrix(par, me):
    row, col = own_column(par, me)
    alike = (row == col) & (iota((REQ, REQ), 1) < iota((REQ, REQ), 0))
    order = jnp.sum(onef(alike), axis=1, keepdims=True)
    code = jnp.concatenate([col * 2.0 + order] * LT, axis=0)
    rows, cols = LT * REQ, NB * LT * 2
    r, c = iota((rows, cols), 0), iota((rows, cols), 1)
    code_of = ((c >> 4) * 2 + (c & 1)).astype(f32)
    return one((code == code_of) & ((r >> 3) == ((c >> 1) & 7)))


def column128(m):
    spread = dot(one((iota((128, NB), 0) >> 3) == iota((128, NB), 1)), m.astype(bf16))
    pick = iota((128, REQ), 1) == (iota((128, REQ), 0) & 7)
    return jnp.sum(jnp.where(pick, spread, 0.0), axis=1, keepdims=True)


def kernel(
    par_h, po_h, ctx_h, cs_h, cw_h, cb_h, x_h, gate_h, q_h, nkv_h, suf_h, gain_h, dtb_h, rates_h, skip_h,
    s_h, xw_h, dtw_h, kv_h,
    mo_h, ao_h,
    par_ref, po_ref, ctx_ref, cs_ref, cw_ref, cb_ref, x_ref, gate_ref, q_ref, nkv_ref, suf_ref, gain_ref, dtb_ref,
    rates_ref, skip_ref, s_v, xw_v, dtw_v, kv_v,
    mo_ref, ao_ref,
    h1s, h1r, hcs, hcr, qa, zb, prb, zzs, zzr, os_, or_, lse,
    tab, tabs, bias, qr, orun, mrun, osf, s0, s1, rt, d1, d0g, c1, okm,
    lsem, tsem, ssem, rsem,
):
    me = lax.axis_index("beam")
    mt = lax.axis_index("tensor")
    nt = zb.shape[0]
    H1, QA, ZB, PR, OO, LS, ZZ, HC = range(8)

    def remote(src, dst, k, device):
        return pltpu.make_async_remote_copy(
            src_ref=src, dst_ref=dst, send_sem=ssem.at[k], recv_sem=rsem.at[k], device_id=device,
            device_id_type=MESH,
        )

    core, mz, nz = mt & 1, mt >> 1, nt // 2
    mx, my = me >> 2, me & 3

    def beam_at(dx, dy):
        return ((mx + dx + core * (-dy - dx)) & 3) * 4 + ((my + dy + core * (-dx - dy)) & 3)

    def tensor_at(dz, other):
        return ((mz + dz * (1 - 2 * core)) & (nz - 1)) * 2 + ((core + other) & 1)

    beam_peers = [(beam_at(dx, dy), mt) for dx, dy in BEAM_ORDER]
    z_order = [k for far in range(nz // 2, 0, -1) for k in sorted({far % nz, -far % nz})]
    tensor_peers = [(me, tensor_at(dz, other)) for dz in z_order for other in (0, 1)] + [(me, tensor_at(0, 1))]

    def exchange(src, dst, k):
        for peer in beam_peers:
            remote(src.at[peer[0]], dst.at[me], k, peer).start()

    def gather(buf, k, at, peers):
        for peer in peers:
            remote(buf.at[at], buf.at[at], k, peer).start()

    def all_of(buf, k):
        part = buf.at[pl.ds(0, buf.shape[0] - 1)]
        return remote(part, part, k, (me, mt))

    def landed(buf, k):
        all_of(buf, k).wait_recv()

    def sent(buf, k):
        all_of(buf, k).wait_send()

    pairs = [
        (par_h, par_ref), (cs_h, cs_ref), (cw_h, cw_ref), (x_h, x_ref), (q_h, q_ref), (s_h, s_v),
        (rates_h, rates_ref), (cb_h, cb_ref), (po_h, po_ref), (ctx_h, ctx_ref), (xw_h, xw_v), (kv_h, kv_v),
        (suf_h, suf_ref), (nkv_h, nkv_ref), (dtw_h, dtw_v), (dtb_h, dtb_ref), (gain_h, gain_ref),
        (skip_h, skip_ref), (gate_h, gate_ref),
    ]
    copies = [pltpu.make_async_copy(a, b, lsem.at[i]) for i, (a, b) in enumerate(pairs)]
    (c_par, c_cs, c_cw, c_x, c_q, c_s, c_rates, c_cb, c_po, c_ctx, c_xw, c_kv, c_suf, c_nkv, c_dtw, c_dtb, c_gain,
     c_skip, c_gate) = copies
    for c in copies[0:5]:
        c.start()
    barrier = pltpu.get_barrier_semaphore()
    greeted = beam_peers + tensor_peers
    for peer in greeted:
        pl.semaphore_signal(barrier, inc=1, device_id=peer, device_id_type=MESH)
    for c in copies[5:]:
        c.start()

    c_par.wait()
    par_t = par_ref[...].astype(f32).astype(bf16)
    eye16 = one(iota((NB, NB), 0) == iota((NB, NB), 1))
    p0 = dot_nt(eye16, par_t[0:REQ]).astype(i32)
    p1 = dot_nt(eye16, par_t[REQ : 2 * REQ]).astype(i32)
    key0 = slot_key(p0, me)
    c_cs.wait()
    c_cw.wait()
    cw = cw_ref[...].astype(f32)
    cw_row = [cw[k : k + 1] for k in range(4)]
    win = [cs_ref[k].astype(f32) for k in range(3)]
    a0 = win[0] * cw_row[0] + win[1] * cw_row[1] + win[2] * cw_row[2]
    a1 = win[1] * cw_row[0] + win[2] * cw_row[1]
    h1s[:, 0:64, :] = jnp.broadcast_to(to_rows(a1).astype(bf16)[None], (NB, 64, 128))
    h1s[:, 64:80, :] = dot(pack_matrix(key0), to_rows(a0).astype(bf16)).astype(bf16).reshape(NB, 16, 128)
    key1 = slot_key(p1, me)
    pb1 = pack_matrix(key1)
    c_x.wait()
    x0 = x_ref[0].astype(f32)
    x1 = x_ref[1].astype(f32)
    h1s[:, 80:96, :] = dot(pb1, to_rows(x0).astype(bf16)).astype(bf16).reshape(NB, 16, 128)
    h1r[pl.ds(me, 1)] = h1s[pl.ds(me, 1)]

    c_q.wait()
    qrows = jnp.concatenate(
        [q_ref[s][:, h * 128 : (h + 1) * 128].astype(f32) for s in range(2) for h in range(GROUP)], axis=0
    ).astype(bf16)
    ri, ci = iota((64, 64), 0), iota((64, 64), 1)
    swap = one(((ri >> 3) == (ci & 7)) & ((ri & 7) == (ci >> 3)))
    qa[pl.ds(me, 1)] = dot(swap, qrows).astype(bf16)[None]

    pl.semaphore_wait(barrier, len(greeted))

    exchange(h1s, h1r, H1)

    ub0 = unpack_matrix(p0, me)
    ub1 = unpack_matrix(p1, me)
    g = jnp.zeros((NB, REQ), i32)
    for p in range(NB):
        g = g + jnp.where(p1 == p, p0[p : p + 1, :], 0)
    _, g_own = own_column(g, me)
    g64 = jnp.concatenate([g_own] * LT, axis=0)
    ai, aj = iota((64, NB * 64), 0), iota((64, NB * 64), 1)
    ug = one((g64 == (aj >> 6).astype(f32)) & (ai == (aj & 63)))
    c_cb.wait()
    cb8 = cb_ref[...].astype(f32)
    cb = jnp.concatenate([cb8[i : i + 1] for i in range(LT)], axis=1)

    c_po.wait()
    c_ctx.wait()
    ctx_col = jnp.zeros((REQ, MAXP), i32)
    for r in range(REQ):
        ctx_col = jnp.where(iota((REQ, MAXP), 0) == r, ctx_ref[r], ctx_col)
    nvis = jnp.clip(ctx_col - iota((REQ, MAXP), 1) * PAGE, 0, PAGE)
    po = jnp.concatenate([po_ref[pl.ds(j, REQ, stride=4), :] for j in range(4)], axis=1)
    loc = po - me * PAGES
    flag = (loc >= 0) & (loc < PAGES) & (nvis > 0)
    tri = one(iota((MAXP, MAXP), 0) < iota((MAXP, MAXP), 1))
    rank = dot(one(flag), tri).astype(i32)
    count = jnp.sum(onef(flag), axis=1, keepdims=True).astype(i32)
    nblk = ((count + (BLK - 1)) >> 4).astype(f32)
    eye8 = iota((REQ, REQ), 0) == iota((REQ, REQ), 1)
    nblk_row = jnp.sum(jnp.where(eye8, nblk, 0.0), axis=0, keepdims=True)
    sblk = jnp.sum(
        jnp.where(iota((REQ, REQ), 1) < iota((REQ, REQ), 0), nblk_row, 0.0), axis=1, keepdims=True
    )
    dest = jnp.where(flag, sblk.astype(i32) * BLK + rank, -1)
    hi = dest >> 4
    lo = jnp.where(flag, dest & 15, -1)
    table = jnp.zeros((NBLK, 32), f32)
    for r in range(REQ):
        hot = one(hi[r : r + 1] == iota((NBLK, MAXP), 0))
        low = lo[r : r + 1] == iota((16, MAXP), 0)
        vals = jnp.concatenate(
            [
                jnp.where(low, loc[r : r + 1].astype(f32), 0.0),
                jnp.where(low, nvis[r : r + 1].astype(f32), 0.0),
            ],
            axis=0,
        ).astype(bf16)
        table = table + dot_nt(hot, vals)
    tab[...] = jnp.zeros_like(tab)
    tab[0:NBLK, 0:32] = table.astype(i32)
    lane = iota((REQ, 128), 1)
    subl = iota((REQ, 128), 0)
    sb_i, nb_i = sblk.astype(i32), nblk.astype(i32)
    inside = (sb_i <= lane) & (lane < sb_i + nb_i)
    tab[NBLK : NBLK + 1, :] = jnp.sum(jnp.where(inside, subl, 0).astype(f32), axis=0, keepdims=True).astype(i32)
    tab[NBLK + 1 : NBLK + 2, :] = jnp.sum(
        onef((lane == sb_i) & (nb_i > 0)), axis=0, keepdims=True
    ).astype(i32)
    tab[NBLK + 2 : NBLK + 3, :] = jnp.sum(
        jnp.where((lane == subl) & (nb_i > 0), sb_i + nb_i, 0).astype(f32), axis=0, keepdims=True
    ).astype(i32)
    cp_tab = pltpu.make_async_copy(tab, tabs, tsem)
    cp_tab.start()
    spread = one((iota((16, BLK * PAGE), 1) >> 4) == iota((16, BLK * PAGE), 0))
    seen = dot(table[:, 16:32].astype(bf16), spread)
    bias[...] = jnp.where((iota((NBLK, BLK * PAGE), 1) & 15).astype(f32) < seen, 0.0, NEG)
    orun[0] = jnp.zeros((128, 2 * HD), f32)
    mrun[0] = jnp.full((128, HD), NEG, f32)
    cp_tab.wait()

    gather(qa, QA, me, beam_peers)

    wide = one((iota((REQ, REQ * 128), 1) >> 7) == iota((REQ, REQ * 128), 0))
    x_s0 = dot(one(p0 == me), wide)
    x_sg = dot(one(g == me), wide)
    x_s1 = dot(one(p1 == me), wide)
    tok = iota((NB, REQ * 128), 1) & 127
    mine = onef(iota((NB, REQ * 128), 0) == me)
    ok0 = jnp.where(tok < 16, x_s0, jnp.where(tok == 16, mine, 0.0))
    ok1 = jnp.where(tok < 16, x_sg, jnp.where(tok == 16, x_s1, jnp.where(tok == 17, mine, 0.0)))
    qi, qj = iota((128, 2 * NB), 0), iota((128, 2 * NB), 1)
    pick = one((((qi >> 2) & 1) == (qj >> 4)) & ((qi >> 3) == (qj & 15)))
    okm[...] = dot(pick, jnp.concatenate([ok0, ok1], axis=0).astype(bf16))

    c_rates.wait()
    for n in range(DS):
        rt[n] = jnp.broadcast_to(rates_ref[n : n + 1, :] * (-LOG2E), (REQ, CH))
    c_s.wait()
    row, col = iota((DS * NB * 2, 128), 0), iota((DS * NB * 2, 128), 1)
    rs_ = one(((iota((DS * NB * 2, NB), 0) >> 1) & 15) == iota((DS * NB * 2, NB), 1))
    crn = one((iota((REQ, 128), 1) >> 4) == iota((REQ, 128), 0))
    keys = dot(rs_, dot(key0.astype(bf16), crn).astype(bf16))
    sel0 = one((keys == (row & 1).astype(f32)) & ((row >> 5) == (col & 15)))
    pi, pj = iota((128, 128), 0), iota((128, 128), 1)
    perm1 = one(((pi & 7) == (pj >> 4)) & ((pi >> 3) == (pj & 15)))
    for j in range(4):
        sl = slice(j * 256, (j + 1) * 256)
        sj = s_v[:, sl].astype(bf16)
        s0[:, :, sl] = dot(sel0, sj).reshape(DS, NB * 2, 256)
        s1[:, :, sl] = dot(perm1, sj).reshape(DS, REQ, 256)
    held_here = column128(onef(g == me))
    g1 = one((column128(p1) == (pj >> 3).astype(f32)) & ((pi & 7) == (pj & 7)))
    r32 = one((iota((32, NB), 0) >> 1) == iota((32, NB), 1))
    c32 = one((iota((REQ, 128), 1) & 7) == iota((REQ, 128), 0))
    key32 = dot(dot(r32, key0.astype(bf16)).astype(bf16), c32)
    si, sj_ = iota((32, 128), 0), iota((32, 128), 1)
    psl = one((key32 == (si & 1).astype(f32)) & ((si >> 1) == (sj_ >> 3)))
    ui, uj = iota((256, 256), 0), iota((256, 256), 1)
    relay = one(((ui >> 4) == ((uj >> 1) & 15)) & (((ui >> 1) & 7) == (uj >> 5)) & ((ui & 1) == (uj & 1)))
    _, own1 = own_column(p1, me)
    gi, gj = iota((REQ, 128), 0), iota((REQ, 128), 1)
    og = one((own1 == (gj >> 3).astype(f32)) & (gi == (gj & 7)))

    c_xw.wait()
    landed(h1r, H1)
    conv0 = silu(from_rows(dot(ub0, h1r[:, 64:80, :].reshape(NB * 16, 128))) + cw_row[3] * x0 + cb)
    older = from_rows(dot(ug, h1r[:, 0:64, :].reshape(NB * 64, 128)))
    newer = from_rows(dot(ub1, h1r[:, 80:96, :].reshape(NB * 16, 128)))
    conv1 = silu(older + cw_row[2] * newer + cw_row[3] * x1 + cb)
    part = dot_nt(jnp.concatenate([conv0, conv1], axis=0).astype(bf16), xw_v[...])
    zb[pl.ds(mt, 1)] = jnp.zeros((1, 16, PROJ_PAD), bf16)
    zb[pl.ds(mt, 1), :, 0:PROJ] = part.astype(bf16)[None]
    gather(zb, ZB, mt, tensor_peers)
    hcs[...] = dot(pb1, to_rows(conv0).astype(bf16)).astype(bf16).reshape(NB, 16, 128)
    hcr[pl.ds(me, 1)] = hcs[pl.ds(me, 1)]
    exchange(hcs, hcr, HC)


    landed(qa, QA)
    qf = qa[...].astype(f32)
    for r in range(REQ):
        qr[r] = jnp.concatenate([qf[b, r * 8 : (r + 1) * 8] for b in range(NB)], axis=0).astype(bf16)
    c_kv.wait()
    scale = HD**-0.5 * LOG2E
    ones_blk = jnp.ones((BLK * PAGE, HD), bf16)

    def blocks(step, c):
        first = step * UNROLL
        m_old, o_old = mrun[first], orun[first]
        for u in range(UNROLL):
            i = first + u
            kv = jnp.concatenate([kv_v[tabs[i, k] & (PAGES - 1)] for k in range(BLK)], axis=0)
            s = dot_nt(qr[tabs[NBLK, i] & (REQ - 1)], kv[:, 0:HD]) * scale + bias[pl.ds(i, 1), :]
            m_old = jnp.where(tabs[NBLK + 1, i] > 0, NEG, m_old)
            m_new = jnp.maximum(m_old, jnp.max(s, axis=1, keepdims=True))
            e = jnp.exp2(s - jnp.concatenate([m_new, m_new], axis=1)).astype(bf16)
            v = jnp.concatenate([kv[:, HD : 2 * HD], ones_blk], axis=1)
            fade = jnp.exp2(m_old - m_new)
            o_old = o_old * jnp.concatenate([fade, fade], axis=1) + dot(e, v)
            m_old = m_new
            orun[i + 1] = o_old
            mrun[i + 1] = m_old
        return c

    steps = NBLK // UNROLL
    lax.fori_loop(0, 2, blocks, 0)

    landed(zb, ZB)
    proj = jnp.zeros((16, PROJ_PAD), f32)
    for t in range(nt):
        proj = proj + zb[t].astype(f32)
    prb[pl.ds(me, 1)] = proj.astype(bf16)[None]
    gather(prb, PR, me, beam_peers)

    lax.fori_loop(2, steps, blocks, 0)
    c_suf.wait()
    c_nkv.wait()
    nk0 = nkv_ref[0].astype(f32)
    nk1 = nkv_ref[1].astype(f32)
    diag = iota((128, 128), 0) == iota((128, 128), 1)
    ti = iota((16, 256), 0)
    for r in range(REQ):
        tail = jnp.where(ti == 0, nk0[r : r + 1], jnp.where(ti == 1, nk1[r : r + 1], 0.0)).astype(bf16)
        kv = jnp.concatenate([suf_ref[r], tail], axis=0)
        s = jnp.where(
            okm[:, r * 128 : r * 128 + 32] > 0.5, dot_nt(qr[r], kv[:, 0:HD]) * scale, NEG
        )
        last = jnp.clip(tabs[NBLK + 2, r], 0, NBLK)
        m_old = mrun[last]
        m_new = jnp.maximum(m_old, jnp.max(s, axis=1, keepdims=True))
        e = jnp.exp2(s - m_new[:, 0:32]).astype(bf16)
        v = jnp.concatenate([kv[:, HD : 2 * HD], jnp.ones((32, HD), bf16)], axis=1)
        fade = jnp.exp2(m_old - m_new)
        o = orun[last] * jnp.concatenate([fade, fade], axis=1) + dot(e, v)
        total = o[:, HD : 2 * HD]
        val = o[:, 0:HD] / total
        for b in range(NB):
            osf[b, r * 8 : (r + 1) * 8, :] = val[b * 8 : (b + 1) * 8]
        lg = m_new + jnp.log2(total)
        lse[pl.ds(me, 1), r : r + 1, :] = jnp.sum(jnp.where(diag, lg, 0.0), axis=0, keepdims=True)[None]
    os_[...] = osf[...].astype(bf16)
    or_[pl.ds(me, 1)] = os_[pl.ds(me, 1)]
    exchange(os_, or_, OO)
    gather(lse, LS, me, beam_peers)

    for c in (c_dtw, c_dtb, c_gain, c_skip, c_gate):
        c.wait()
    gain = gain_ref[...]

    def normed(rank_rows):
        mean = jnp.sum(rank_rows * rank_rows, axis=1, keepdims=True) * (1.0 / DT_RANK)
        return (rank_rows * lax.rsqrt(mean + 1e-6) * gain).astype(bf16)

    dtb = dtb_ref[...]
    landed(prb, PR)
    prf = prb[...].astype(f32)
    pr0 = prf[:, 0:REQ, :].reshape(128, PROJ_PAD)
    pr1 = prf[:, REQ : 2 * REQ, :].reshape(128, PROJ_PAD)
    rn0 = normed(pr0[:, 0:DT_RANK])
    rn1 = normed(pr1[:, 0:DT_RANK])
    bc0 = pr0[:, DT_RANK:PROJ].astype(bf16)
    c1[...] = (pr1[:, DT_RANK:PROJ_PAD] * held_here).reshape(NB, REQ, 128)
    rn0g = dot(g1, rn0).astype(bf16)

    rn0s = dot(psl, rn0).astype(bf16)
    c0s = dot(psl, bc0)
    c0b = [jnp.broadcast_to(c0s[:, DS + n : DS + n + 1], (NB * 2, 128)) for n in range(DS)]
    z0 = []
    for j in range(4):
        sl = slice(j * 256, (j + 1) * 256)
        w = dtw_v[:, sl]
        part1 = softplus(dot(rn1, w) + dtb[:, sl])
        part0 = softplus(dot(rn0g, w) + dtb[:, sl])
        d0g[:, :, sl] = part0.reshape(NB, REQ, 256)
        d1[:, :, sl] = (part0 + part1).reshape(NB, REQ, 256)
        dj = softplus(dot(rn0s, w) + dtb[:, sl])
        acc = jnp.zeros((32, 256), f32)
        for n in range(DS):
            cn = jnp.concatenate([c0b[n], c0b[n]], axis=1)
            acc = acc + cn * (jnp.exp2(dj * (rates_ref[n : n + 1, sl] * (-LOG2E))) * s0[n, :, sl])
        z0 += [acc[:, 0:128], acc[:, 128:256]]
    z0 = jnp.concatenate(z0, axis=0).astype(bf16)
    zzs[:, 64:80, :] = dot(relay, z0).astype(bf16).reshape(NB, 16, 128)

    def children(i, c):
        two = [(turn >> 2, turn & 3) for turn in (NB - 1 - 2 * i, NB - 2 - 2 * i)]
        two = [beam_at(dx, dy) for dx, dy in two]
        outs = [c1[b] for b in two]
        deltas = [d1[b] for b in two]
        accs = [jnp.zeros((REQ, CH), f32) for _ in two]
        for n in range(DS):
            rn, sn = rt[n], s1[n]
            for k in range(2):
                accs[k] = accs[k] + outs[k][:, DS + n : DS + n + 1] * (jnp.exp2(deltas[k] * rn) * sn)
        for k in range(2):
            zzs[two[k], 0:64, :] = to_rows(accs[k]).astype(bf16)
        remote(zzs.at[two[0]], zzr.at[me], ZZ, (two[0], mt)).start()

        @pl.when(i < NB // 2 - 1)
        def _():
            remote(zzs.at[two[1]], zzr.at[me], ZZ, (two[1], mt)).start()

        return c

    lax.fori_loop(0, NB // 2, children, 0)
    zzr[pl.ds(me, 1)] = zzs[pl.ds(me, 1)]

    own = proj.astype(bf16).astype(f32)
    d_own = softplus(dot(normed(own[:, 0:DT_RANK]), dtw_v[...]) + dtb)
    d_own0, d_own1 = d_own[0:REQ], d_own[REQ : 2 * REQ]
    own_in = own[:, DT_RANK : DT_RANK + DS]
    own_out = own[:, DT_RANK + DS : DT_RANK + 2 * DS]
    cb_own = jnp.sum(own_in * own_out, axis=1, keepdims=True)
    skip = skip_ref[...]
    base0 = d_own0 * conv0 * cb_own[0:REQ] + skip * conv0
    base1 = d_own1 * conv1 * cb_own[REQ : 2 * REQ] + skip * conv1
    gate0 = silu(gate_ref[0].astype(f32))
    gate1 = silu(gate_ref[1].astype(f32))

    landed(hcr, HC)
    conv0p = from_rows(dot(ub1, hcr[...].reshape(NB * 16, 128)))
    in0p = dot(og, bc0)[:, 0:DS]
    cross = in0p * own_out[REQ : 2 * REQ]
    mixed = jnp.zeros((REQ, CH), f32)
    for n in range(DS):
        mixed = mixed + cross[:, n : n + 1] * jnp.exp2(d_own1 * rt[n])
    base1 = base1 + mixed * (d0g[pl.ds(me, 1)][0] * conv0p)

    landed(or_, OO)
    landed(lse, LS)
    lanes = iota((8, 128), 1)
    want = lanes == me * 8 + iota((8, 128), 0)
    parts = []
    for p in range(NB):
        lp = lse[p]
        parts.append(
            jnp.concatenate(
                [
                    jnp.sum(jnp.where(want, lp[r : r + 1], 0.0), axis=1, keepdims=True)
                    for r in range(REQ)
                ],
                axis=0,
            )
        )
    top = parts[0]
    for p in range(1, NB):
        top = jnp.maximum(top, parts[p])
    den = jnp.zeros((64, 1), f32)
    num = jnp.zeros((64, HD), f32)
    for p in range(NB):
        w = jnp.exp2(parts[p] - top)
        den = den + w
        num = num + w * or_[p].astype(f32)
    att = dot(swap, (num / den).astype(bf16))
    for s in range(2):
        ao_ref[s, 0] = jnp.concatenate(
            [att[(s * GROUP + h) * 8 : (s * GROUP + h + 1) * 8] for h in range(GROUP)], axis=1
        ).astype(bf16)
    out_a = pltpu.make_async_copy(ao_ref, ao_h, tsem)
    out_a.start()

    landed(zzr, ZZ)
    z1 = jnp.zeros((64, 128), f32)
    for p in range(NB):
        z1 = z1 + zzr[p, 0:64, :].astype(f32)
    z0 = dot(ub0, zzr[:, 64:80, :].reshape(256, 128))
    mo_ref[0, 0] = ((from_rows(z0) + base0) * gate0).astype(bf16)
    mo_ref[1, 0] = ((from_rows(z1) + base1) * gate1).astype(bf16)
    out_m = pltpu.make_async_copy(mo_ref, mo_h, lsem.at[0])
    out_m.start()

    sent(h1s, H1)
    sent(hcs, HC)
    sent(qa, QA)
    sent(zb, ZB)
    sent(prb, PR)
    sent(os_, OO)
    sent(lse, LS)
    sent(zzs, ZZ)
    out_a.wait()
    out_m.wait()


def publish(m_ref, a_ref, mo_ref, ao_ref, m_v, a_v, sem):
    first = pltpu.make_async_copy(m_ref, m_v, sem.at[0])
    second = pltpu.make_async_copy(a_ref, a_v, sem.at[1])
    first.start()
    second.start()
    first.wait()
    first = pltpu.make_async_copy(m_v, mo_ref, sem.at[0])
    first.start()
    second.wait()
    second = pltpu.make_async_copy(a_v, ao_ref, sem.at[1])
    second.start()
    first.wait()
    second.wait()


def local(
    ssm_state,
    conv_state,
    suffix_kv,
    mamba_x,
    mamba_gate,
    conv_weight,
    conv_bias,
    xproj_weight,
    dt_gain,
    dtproj_weight,
    dt_bias,
    state_rates,
    skip_gain,
    queries,
    new_kv,
    kv_pool,
    page_order,
    ctx_len,
    parents,
):
    nt = lax.axis_size("tensor")
    hb = pl.BlockSpec(memory_space=pltpu.HBM)
    dma = pltpu.SemaphoreType.DMA
    V = pltpu.VMEM
    operands = [
        parents.transpose(0, 2, 1, 3).reshape(2 * REQ, NB),
        page_order.reshape(POOL // 128, 128),
        ctx_len,
        conv_state.transpose(0, 2, 1, 3)[0],
        conv_weight,
        conv_bias.reshape(LT, 128),
        mamba_x[:, 0],
        mamba_gate[:, 0],
        queries[:, 0],
        new_kv[:, 0],
        suffix_kv[0],
        dt_gain.reshape(1, DT_RANK),
        dt_bias.reshape(1, CH),
        state_rates,
        skip_gain.reshape(1, CH),
        ssm_state.reshape(REQ * DS, CH),
        xproj_weight.T,
        dtproj_weight,
        kv_pool,
    ]
    held = [V(a.shape, a.dtype) for a in operands]
    held[2] = pltpu.SMEM((REQ,), i32)
    outs = (
        jax.ShapeDtypeStruct((2, 1, REQ, CH), bf16),
        jax.ShapeDtypeStruct((2, 1, REQ, GROUP * HD), bf16),
    )
    results = pl.pallas_call(
        kernel,
        out_shape=outs,
        in_specs=[hb] * len(operands),
        out_specs=(hb, hb),
        scratch_shapes=held
        + [
            V(outs[0].shape, bf16),
            V(outs[1].shape, bf16),
            V((NB, 96, 128), bf16),
            V((NB, 96, 128), bf16),
            V((NB, 16, 128), bf16),
            V((NB, 16, 128), bf16),
            V((NB, 64, HD), bf16),
            V((nt, 16, PROJ_PAD), bf16),
            V((NB, 16, PROJ_PAD), bf16),
            V((NB, 80, 128), bf16),
            V((NB, 80, 128), bf16),
            V((NB, 64, HD), bf16),
            V((NB, 64, HD), bf16),
            V((NB, REQ, 128), f32),
            V((32, 128), i32),
            pltpu.SMEM((32, 128), i32),
            V((NBLK, BLK * PAGE), f32),
            V((REQ, 128, HD), bf16),
            V((NBLK + 1, 128, 2 * HD), f32),
            V((NBLK + 1, 128, HD), f32),
            V((NB, 64, HD), f32),
            V((DS, NB * 2, CH), f32),
            V((DS, REQ, CH), f32),
            V((DS, REQ, CH), f32),
            V((NB, REQ, CH), f32),
            V((NB, REQ, CH), f32),
            V((NB, REQ, 128), f32),
            V((128, REQ * 128), f32),
            dma((len(operands),)),
            dma,
            dma((8,)),
            dma((8,)),
        ],
        compiler_params=pltpu.CompilerParams(
            collective_id=0, has_side_effects=True, vmem_limit_bytes=63 * 2**20
        ),
        name="decode",
    )(*operands)
    return pl.pallas_call(
        publish,
        out_shape=outs,
        in_specs=[hb, hb],
        out_specs=(hb, hb),
        scratch_shapes=[V(outs[0].shape, bf16), V(outs[1].shape, bf16), dma((2,))],
        compiler_params=pltpu.CompilerParams(vmem_limit_bytes=63 * 2**20),
        name="publish",
    )(*results)


def solution(mesh):
    in_specs = (
        P("beam", None, None, "tensor"),
        P("beam", None, None, "tensor"),
        P("beam", None, None, "tensor"),
        P(None, "beam", None, "tensor"),
        P(None, "beam", None, "tensor"),
        P(None, "tensor"),
        P("tensor"),
        P("tensor", None),
        P(),
        P(None, "tensor"),
        P("tensor"),
        P(None, "tensor"),
        P("tensor"),
        P(None, "beam", None, "tensor"),
        P(None, "beam", None, "tensor"),
        P("beam", None, "tensor"),
        P(),
        P(),
        P(),
    )
    out_specs = (P(None, "beam", None, "tensor"), P(None, "beam", None, "tensor"))
    return jax.shard_map(local, mesh=mesh, in_specs=in_specs, out_specs=out_specs, check_vma=False)
```
